32 devices in a mesh: frames: 8 (over y, x, core), rows: 4 (over z).
Axes of the slice: x: 2, y: 2, z: 4, core: 2. Of those that a mesh axis runs over, the one named last changes fastest.
Arguments:
- block_in: bfloat16 [8, 2, 32, 32, 1024], P('frames', None, 'rows'), may hold values from -6 to 6
- block_map: int32 [8], replicated, may hold values from 0 to 7, each once
- noise_level: int32 [8, 2], P('frames'), may hold values from 0 to 999
- w_query: bfloat16 [1024, 1024], replicated, may hold values from -0.1875 to 0.1875
- w_key: bfloat16 [1024, 1024], replicated, may hold values from -0.1875 to 0.1875
- w_value: bfloat16 [1024, 1024], replicated, may hold values from -0.1875 to 0.1875
- w_proj: bfloat16 [1024, 1024], replicated, may hold values from -3 to 3
- w_up: bfloat16 [1024, 4096], replicated, may hold values from -0.1875 to 0.1875
- w_down: bfloat16 [4096, 1024], replicated, may hold values from -0.09375 to 0.09375
- w_mod: bfloat16 [1024, 6144], replicated, may hold values from -0.1875 to 0.1875
- cotangent: bfloat16 [8, 2, 32, 32, 1024], P('frames', None, 'rows'), may hold values from -6 to 6
Outputs:
- block_out: bfloat16 [8, 2, 32, 32, 1024], P('frames', None, 'rows')
- grad_input: float32 [8, 2, 32, 32, 1024], P('frames', None, 'rows')
- grad_query: float32 [1024, 1024], P(('frames', 'rows'))
- grad_key: float32 [1024, 1024], P(('frames', 'rows'))
- grad_value: float32 [1024, 1024], P(('frames', 'rows'))
- grad_proj: float32 [1024, 1024], P(('frames', 'rows'))
- grad_up: float32 [1024, 4096], P(('frames', 'rows'))
- grad_down: float32 [4096, 1024], P(('frames', 'rows'))
- grad_mod: float32 [1024, 6144], P(('frames', 'rows'))
The draws below stay inside these ranges and needn't reach their ends.
Inputs may be any that keep to these rules, and one draw needn't show every extreme that they name: `block_map`: a permutation: no two slots hold the same frame.
All inputs are finite; a program needn't handle non-finite values.
Results may differ from the reference program's by a relative error of at most 0.014.
Values may be sent and summed in bfloat16 or wider, within the bound.
No kernel may reach another device: no remote copies, remote signals or barrier semaphores. Data moves between devices by JAX's collectives and lax.ppermute only.
A program may use at most 320 MiB of HBM per device.

```python
import math
import jax
import jax.numpy as jnp
from jax import lax

D = 1024
H = 16
HD = 64
FF = 4096
PR = 32
PC = 32
CLIPS = 2
FRAMES = 8


def set_ends(entries, stream_key, low, largest):
    place = [jax.random.randint(jax.random.fold_in(stream_key, axis), (), 0, length) for axis, length in enumerate(entries.shape)]
    widest = entries.shape.index(max(entries.shape))
    next_to = place[:widest] + [(place[widest] + 1) % entries.shape[widest]] + place[widest + 1:]
    return entries.at[tuple(place)].set(low).at[tuple(next_to)].set(largest)


def block_scale(stream_key, dims, cuts, low, largest):
    loudness = 1.0
    for dim, blocks in cuts:
        draws = jax.random.uniform(jax.random.fold_in(jax.random.fold_in(stream_key, 6), dim), (blocks,), jnp.float32, low / len(cuts), largest / len(cuts))
        loudness = loudness * jnp.repeat(jnp.exp(draws), dims[dim] // blocks).reshape((-1,) + (1,) * (len(dims) - 1 - dim))
    return loudness


def gaussian(own_key, dims, width, limit, cuts=(), kind=jnp.bfloat16):
    drawn = jax.random.normal(own_key, dims, jnp.float32) * width
    if len(cuts) > 0:
        drawn = block_scale(own_key, dims, cuts, -0.22, 0.18) * drawn
    return jnp.clip(drawn, min=-limit, max=limit).astype(kind)


def setup_inputs(seed: int = 0) -> dict:
    seeds = jax.random.split(jax.random.key(seed), 12)
    block_in = gaussian(seeds[0], (FRAMES, CLIPS, PR, PC, D), 1.0, 6.0, ((0, 8), (2, 4)))
    block_map = jax.random.permutation(seeds[1], FRAMES).astype(jnp.int32)
    noise_level = set_ends(jax.random.randint(seeds[2], (FRAMES, CLIPS), 0, 1000), jax.random.fold_in(seeds[2], 1), 0, 999).astype(jnp.int32)
    w_query = gaussian(seeds[3], (D, D), D ** -0.5, 0.1875)
    w_key = gaussian(seeds[4], (D, D), D ** -0.5, 0.1875)
    w_value = gaussian(seeds[5], (D, D), D ** -0.5, 0.1875)
    w_proj = gaussian(seeds[6], (D, D), 4 ** -0.5, 3.0)
    w_up = gaussian(seeds[7], (D, FF), D ** -0.5, 0.1875)
    w_down = gaussian(seeds[8], (FF, D), FF ** -0.5, 0.09375)
    w_mod = gaussian(seeds[9], (D, 6 * D), D ** -0.5, 0.1875)
    cotangent = gaussian(seeds[10], (FRAMES, CLIPS, PR, PC, D), 1.0, 6.0, ((0, 8), (2, 4)))
    return {"block_in": block_in, "block_map": block_map, "noise_level": noise_level, "w_query": w_query, "w_key": w_key, "w_value": w_value, "w_proj": w_proj, "w_up": w_up, "w_down": w_down, "w_mod": w_mod, "cotangent": cotangent}


@jax.custom_vjp
def low(v):
    return lax.optimization_barrier(v.astype(jnp.bfloat16)).astype(jnp.float32)

@jax.custom_vjp
def low_back(v):
    return v

def low_keep(v):
    return (low(v), None)

def low_pass(kept, grad):
    return (grad,)

def back_keep(v):
    return (v, None)

def back_low(kept, grad):
    return (low(grad),)
low.defvjp(low_keep, low_pass)
low_back.defvjp(back_keep, back_low)
norm_eps = 1e-06

def sinusoid(levels):
    half_size = D // 2
    freq_table = 10000.0 ** (-jnp.arange(half_size, dtype=jnp.float32) / half_size)
    angle_table = levels.astype(jnp.float32)[..., None] * freq_table
    return jnp.concatenate([jnp.cos(angle_table), jnp.sin(angle_table)], axis=-1)

def rotate(vector, time_pos, row_pos, col_pos, flip_sign):
    width_all = vector.shape[-1]
    quarter = width_all // 4
    rest_size = 3 * width_all // 8
    pieces = []
    offset = 0
    for position, part_size in ((time_pos, quarter), (row_pos, rest_size), (col_pos, rest_size)):
        half_size = part_size // 2
        first_half = vector[..., offset:offset + half_size]
        second_half = vector[..., offset + half_size:offset + part_size]
        freq_table = 10000.0 ** (-jnp.arange(half_size, dtype=jnp.float32) / half_size)
        angle_table = position[..., None] * freq_table
        cosine = jnp.cos(angle_table)
        sine_part = flip_sign * jnp.sin(angle_table)
        pieces.append(first_half * cosine - second_half * sine_part)
        pieces.append(second_half * cosine + first_half * sine_part)
        offset += part_size
    return jnp.concatenate(pieces, axis=-1)

def normalize(values):
    centered = values - lax.optimization_barrier(jnp.mean(values, axis=-1, keepdims=True))
    inverse = lax.rsqrt(lax.optimization_barrier(jnp.mean(centered * centered, axis=-1, keepdims=True)) + norm_eps)
    return centered * inverse

def reference(block_in, block_map, noise_level, w_query, w_key, w_value, w_proj, w_up, w_down, w_mod, cotangent):
    highest = lax.Precision.HIGHEST
    frame_total = block_map.shape[0]
    clip_total = block_in.shape[1]
    token_total = frame_total * PR * PC
    times = block_map.astype(jnp.float32)
    time_pos = times[:, None, None, None, None]
    row_pos = jnp.arange(PR, dtype=jnp.float32)[None, None, :, None, None]
    col_pos = jnp.arange(PC, dtype=jnp.float32)[None, None, None, :, None]
    token_time = jnp.repeat(block_map, PR * PC)
    allowed = token_time[None, :] <= token_time[:, None]
    scale_factor = 1.0 / math.sqrt(HD)

    def attend(triple):
        query, keys, values = triple
        scores = low_back(jnp.einsum('qd,kd->qk', query, keys, precision=highest) * scale_factor)
        scores = jnp.where(allowed, scores, -1e+30)
        probs = low(jax.nn.softmax(scores, axis=-1))
        return jnp.dot(probs, values, precision=highest)

    def project(values, matrix):
        return jnp.einsum('fcrpd,de->fcrpe', values, matrix, precision=highest)

    def forward(source, m_query, m_key, m_value, m_proj, m_up, m_down, m_mod):
        embed = low(jax.nn.silu(sinusoid(noise_level)))
        modulation = jnp.einsum('fcd,de->fce', embed, m_mod, precision=highest)[:, :, None, None, :]
        shift_one, scale_one, gate_one, shift_two, scale_two, gate_two = jnp.split(modulation, 6, axis=-1)
        hidden_one = low(normalize(source) * (1.0 + scale_one) + shift_one)
        head_shape = source.shape[:4] + (H, HD)
        query_pre = low_back(project(hidden_one, m_query))
        key_pre = low_back(project(hidden_one, m_key))
        value_all = low(low_back(project(hidden_one, m_value))).reshape(head_shape)
        query_all = low(rotate(query_pre.reshape(head_shape), time_pos, row_pos, col_pos, 1.0))
        key_all = low(rotate(key_pre.reshape(head_shape), time_pos, row_pos, col_pos, 1.0))

        def to_heads(array):
            return jnp.transpose(array, (1, 4, 0, 2, 3, 5)).reshape(clip_total * H, token_total, HD)
        attended = lax.map(jax.checkpoint(attend), (to_heads(query_all), to_heads(key_all), to_heads(value_all)))
        attended = attended.reshape(clip_total, H, frame_total, PR, PC, HD)
        attended = jnp.transpose(attended, (2, 0, 3, 4, 1, 5)).reshape(source.shape)
        attended = low(low_back(attended))
        branch_one = low_back(project(attended, m_proj))
        middle = source + gate_one * branch_one
        hidden_two = low(normalize(middle) * (1.0 + scale_two) + shift_two)
        upward = low_back(project(hidden_two, m_up))
        active = low(jax.nn.gelu(upward, approximate=True))
        branch_two = low_back(project(active, m_down))
        return middle + gate_two * branch_two
    result, pullback = jax.vjp(forward, block_in.astype(jnp.float32), w_query.astype(jnp.float32), w_key.astype(jnp.float32), w_value.astype(jnp.float32), w_proj.astype(jnp.float32), w_up.astype(jnp.float32), w_down.astype(jnp.float32), w_mod.astype(jnp.float32))
    grads = pullback(cotangent.astype(jnp.float32))
    return (result.astype(jnp.bfloat16), grads[0], grads[1], grads[2], grads[3], grads[4], grads[5], grads[6], grads[7])
```

```python
import functools
import math

import jax
import jax.numpy as jnp
from jax import lax
from jax.experimental import pallas as pl
from jax.experimental.pallas import tpu as pltpu
from jax.sharding import Mesh, PartitionSpec as P

D = 1024
H = 16
HD = 64
FF = 4096
PR = 32
PC = 32

norm_eps = 1e-06
LOW = jnp.bfloat16
WIDE = jnp.float32
MIB = 2**20
SCALE2 = math.log2(math.e) / math.sqrt(HD)
SAFE_LOG2 = 100.0
ROWS_ROWS = (((1,), (1,)), ((), ()))
ROWS_COLS = (((1,), (0,)), ((), ()))
SHIFT_ONE, SCALE_ONE, GATE_ONE, SHIFT_TWO, SCALE_TWO, GATE_TWO = range(6)


def dot(left, right, dims=ROWS_COLS):
    return lax.dot_general(left, right, dims, preferred_element_type=WIDE)


def exact_dot(left, right, dims=ROWS_COLS):
    return lax.dot_general(
        left, right, dims, preferred_element_type=WIDE, precision=lax.Precision.HIGHEST
    )


def vmem():
    return pl.BlockSpec(memory_space=pltpu.VMEM)


def smem():
    return pl.BlockSpec(memory_space=pltpu.SMEM)


def whole(shape):
    return pl.BlockSpec(shape, lambda *unused: (0,) * len(shape))


def column_sum(values):
    return jnp.sum(values, axis=0, keepdims=True)


def head_masks(rows, lanes, heads):
    lane = lax.broadcasted_iota(jnp.int32, (rows, lanes), 1)
    return [lane // HD == h for h in range(heads)]


def square_norm(values, masks):
    squared = values.astype(WIDE)
    squared = squared * squared
    return [
        jnp.max(jnp.sum(jnp.where(mask, squared, 0.0), axis=1, keepdims=True)) for mask in masks
    ]


def forward_kernel(order, flag_in, query, pair, *refs, first, last, heads):
    frames, tokens, lanes = query.shape
    if not first:
        num_in, sum_in, top_in = refs[:3]
        refs = refs[3:]
    if last:
        attn_out, log_out, keys, values = refs
    else:
        flag_out, num_out, sum_out, top_out, keys, values = refs
    masks = head_masks(tokens, lanes, heads)
    one = jnp.ones((tokens, lanes), LOW)
    zero = jnp.zeros((tokens, lanes), LOW)
    width = 2 * HD
    bound = jnp.float32(0.0)
    q_top = [jnp.float32(0.0)] * heads
    k_top = [jnp.float32(0.0)] * heads
    for f in range(frames):
        k = pair[f, 0]
        v = pair[f, 1]
        q_top = [jnp.maximum(a, b) for a, b in zip(q_top, square_norm(query[f], masks))]
        k_top = [jnp.maximum(a, b) for a, b in zip(k_top, square_norm(k, masks))]
        for h in range(heads):
            keys[h, f] = jnp.where(masks[h], k, zero)
            if heads == 2:
                values[h, f] = jnp.where(masks[h], v, one)
            else:
                values[h, f] = jnp.concatenate([v, one], axis=1)
    for a, b in zip(q_top, k_top):
        bound = jnp.maximum(bound, a * b)
    fast = bound * (SCALE2 * SCALE2) <= SAFE_LOG2 * SAFE_LOG2
    if not first:
        fast = jnp.logical_and(fast, flag_in[0] == 1)
    if not last:
        flag_out[0] = jnp.where(fast, 1, 0).astype(jnp.int32)
    low_lane = lax.broadcasted_iota(jnp.int32, (tokens, lanes), 1) < HD
    pick = lax.broadcasted_iota(jnp.int32, (8, lanes), 1) == HD * lax.broadcasted_iota(
        jnp.int32, (8, lanes), 0
    )
    pick = jnp.where(pick, 1.0, 0.0).astype(WIDE)

    def split(num, total):
        if heads == 2:
            turned = pltpu.roll(total, HD, 1)
            return [jnp.where(low_lane, num, turned), jnp.where(low_lane, turned, num)]
        return [jnp.concatenate([num, total], axis=1)]

    def join(accs):
        if heads == 2:
            num = jnp.where(low_lane, accs[0], accs[1])
            total = jnp.where(low_lane, accs[1], accs[0])
            return num, pltpu.roll(total, HD, 1)
        return accs[0][:, :HD], accs[0][:, HD:]

    def start(slot):
        if first:
            return [jnp.zeros((tokens, width), WIDE) for _ in range(heads)]
        return split(num_in[slot], sum_in[slot])

    def store(slot, accs, top):
        num, total = join(accs)
        if last:
            attn_out[slot] = (num / total).astype(LOW)
            logs = jnp.log2(total)
            if top is not None:
                logs = logs + top
            log_out[slot] = exact_dot(pick, logs, ROWS_ROWS)
        else:
            num_out[slot] = num
            sum_out[slot] = total
            top_out[slot] = jnp.zeros((tokens, lanes), WIDE) if top is None else top

    @pl.when(fast)
    def _():
        def outer(t, unused):
            slot = order[t]
            q = query[slot]

            def inner(j, accs):
                other = order[j]
                new = []
                for h in range(heads):
                    s = dot(q, keys[h, other], ROWS_ROWS)
                    p = jnp.exp2(s * SCALE2).astype(LOW)
                    new.append(accs[h] + dot(p, values[h, other]))
                return new

            store(slot, lax.fori_loop(0, t + 1, inner, start(slot)), None)
            return unused

        lax.fori_loop(0, frames, outer, 0)

    @pl.when(jnp.logical_not(fast))
    def _():
        def outer(t, unused):
            slot = order[t]
            q = query[slot]

            def inner(j, state):
                other = order[j]
                accs, tops = state
                new_accs, new_tops = [], []
                for h in range(heads):
                    s = dot(q, keys[h, other], ROWS_ROWS) * SCALE2
                    top = jnp.maximum(tops[h], jnp.max(s, axis=1, keepdims=True))
                    p = jnp.exp2(s - top).astype(LOW)
                    keep = jnp.exp2(tops[h] - top)
                    new_accs.append(accs[h] * keep + dot(p, values[h, other]))
                    new_tops.append(top)
                return new_accs, new_tops

            if first:
                tops = [jnp.full((tokens, 1), -1e30, WIDE)] * heads
            else:
                tops = [top_in[slot][:, h * HD : h * HD + 1] for h in range(heads)]
            accs, tops = lax.fori_loop(0, t + 1, inner, (start(slot), tops))
            top = jnp.broadcast_to(tops[0], (tokens, lanes))
            if heads == 2:
                top = jnp.where(low_lane, top, jnp.broadcast_to(tops[1], (tokens, lanes)))
            store(slot, accs, top)
            return unused

        lax.fori_loop(0, frames, outer, 0)


def attention_forward(order, state, query, pair, last):
    frames, tokens, lanes = query.shape
    heads = lanes // HD
    first = state is None
    wide = jax.ShapeDtypeStruct(query.shape, WIDE)
    if last:
        out_shape = [
            jax.ShapeDtypeStruct(query.shape, LOW),
            jax.ShapeDtypeStruct((frames, 8, tokens), WIDE),
        ]
        out_specs = [vmem()] * 2
    else:
        out_shape = [jax.ShapeDtypeStruct((1,), jnp.int32), wide, wide, wide]
        out_specs = [smem()] + [vmem()] * 3
    flag = jnp.zeros((1,), jnp.int32) if first else state[0]
    rest = () if first else tuple(state[1:])
    pairs = heads * frames * (frames + 1) // 2 * tokens * tokens
    return pl.pallas_call(
        functools.partial(forward_kernel, first=first, last=last, heads=heads),
        out_shape=out_shape,
        in_specs=[smem(), smem()] + [vmem()] * (2 + len(rest)),
        out_specs=out_specs,
        scratch_shapes=[
            pltpu.VMEM((heads, frames, tokens, lanes), LOW),
            pltpu.VMEM((heads, frames, tokens, max(lanes, 2 * HD)), LOW),
        ],
        compiler_params=pltpu.CompilerParams(vmem_limit_bytes=56 * MIB),
        cost_estimate=pl.CostEstimate(
            flops=pairs * 4 * HD * 8, bytes_accessed=16 * MIB, transcendentals=pairs
        ),
        name="attention_forward",
    )(order, flag, query, pair, *rest)


def backward_kernel(
    order, query, pair, grad, out, lse, *refs, first, last, begin, end, came, heads
):
    frames, tokens, lanes = query.shape
    if not first:
        dq_in = refs[0]
        refs = refs[1:]
    if begin > 0:
        pair_in = refs[0]
        refs = refs[1:]
    if came:
        pair_came = refs[0]
        refs = refs[1:]
    if last:
        final, queries, grads, delta, key_turned, dq_sum = refs
        places = (1, 2)
    else:
        dq_sum, final, queries, grads, delta, key_turned = refs
        places = (0, 1)
    masks = head_masks(tokens, lanes, heads)
    zero = jnp.zeros((tokens, lanes), LOW)
    lane8 = lax.broadcasted_iota(jnp.int32, (8, lanes), 1) // HD
    pick = jnp.where(lane8 == lax.broadcasted_iota(jnp.int32, (8, lanes), 0), 1.0, 0.0)
    for f in range(frames):
        q = query[f]
        g = grad[f]
        for h in range(heads):
            queries[h, f] = jnp.where(masks[h], q, zero)
            grads[h, f] = jnp.where(masks[h], g, zero)
        key_turned[f] = pair[f, 0].T
        delta[f] = exact_dot(
            pick.astype(WIDE), g.astype(WIDE) * out[f].astype(WIDE), ROWS_ROWS
        )
        dq_sum[f] = jnp.zeros((lanes, tokens), WIDE) if first else dq_in[f]
        if begin > 0:
            for i in range(2):
                old = pair_in[f, i]
                if came:
                    old = (old.astype(WIDE) + pair_came[f, i].astype(WIDE)).astype(LOW)
                final[f, places[i]] = old

    def outer(t, unused):
        slot = order[t]
        k = pair[slot, 0]
        v = pair[slot, 1]
        ks = [jnp.where(mask, k, zero) for mask in masks]
        vs = [jnp.where(mask, v, zero) for mask in masks]

        def inner(j, carry):
            other = order[j]
            dk, dv = carry
            for h in range(heads):
                q = queries[h, other]
                g = grads[h, other]
                s = dot(ks[h], q, ROWS_ROWS)
                p = jnp.exp2(s * SCALE2 - lse[other, h : h + 1, :])
                dp = dot(vs[h], g, ROWS_ROWS)
                ds = (p * (dp - delta[other, h : h + 1, :])).astype(LOW)
                dv = dv + dot(p.astype(LOW), g)
                dk = dk + dot(ds, q)
                span = slice(h * HD, (h + 1) * HD)
                dq_sum[other, span, :] += dot(key_turned[slot, span, :], ds)
            return dk, dv

        start = jnp.zeros((tokens, lanes), WIDE)
        dk, dv = lax.fori_loop(t, frames, inner, (start, start))
        dk = dk * (1.0 / math.sqrt(HD))
        if came:
            dk = dk + pair_came[slot, 0].astype(WIDE)
            dv = dv + pair_came[slot, 1].astype(WIDE)
        final[slot, places[0]] = dk.astype(LOW)
        final[slot, places[1]] = dv.astype(LOW)
        return unused

    lax.fori_loop(begin, end, outer, 0)
    if last:
        for f in range(frames):
            final[f, 0] = (dq_sum[f].T * (1.0 / math.sqrt(HD))).astype(LOW)


def attention_backward(order, dq, partial, came, query, pair, grad, out, lse, begin, end, last):
    frames, tokens, lanes = query.shape
    heads = lanes // HD
    first = dq is None
    sums = (frames, lanes, tokens)
    extra = tuple(
        array for array in (dq, partial if begin > 0 else None, came) if array is not None
    )
    steps = sum(frames - t for t in range(begin, end))
    work = heads * steps * tokens * tokens
    scratch = [
        pltpu.VMEM((heads, frames, tokens, lanes), LOW),
        pltpu.VMEM((heads, frames, tokens, lanes), LOW),
        pltpu.VMEM((frames, 8, tokens), WIDE),
        pltpu.VMEM((frames, lanes, tokens), LOW),
    ]
    if last:
        out_shape = [jax.ShapeDtypeStruct((frames, 3, tokens, lanes), LOW)]
        scratch.append(pltpu.VMEM(sums, WIDE))
    else:
        out_shape = [
            jax.ShapeDtypeStruct(sums, WIDE), jax.ShapeDtypeStruct((frames, 2, tokens, lanes), LOW)
        ]
    return pl.pallas_call(
        functools.partial(
            backward_kernel, first=first, last=last, begin=begin, end=end,
            came=came is not None, heads=heads,
        ),
        out_shape=out_shape,
        in_specs=[smem()] + [vmem()] * (5 + len(extra)),
        out_specs=[vmem()] * len(out_shape),
        scratch_shapes=scratch,
        compiler_params=pltpu.CompilerParams(vmem_limit_bytes=56 * MIB),
        cost_estimate=pl.CostEstimate(
            flops=work * 10 * HD * 5, bytes_accessed=16 * MIB, transcendentals=work
        ),
        name="attention_backward",
    )(order, query, pair, grad, out, lse, *extra)


def normalize(values):
    centered = values - jnp.mean(values, axis=-1, keepdims=True)
    inverse = lax.rsqrt(jnp.mean(centered * centered, axis=-1, keepdims=True) + norm_eps)
    return (centered * inverse, inverse)


def norm_backward(grad_normed, normed, inverse):
    mean_grad = jnp.mean(grad_normed, axis=-1, keepdims=True)
    mean_prod = jnp.mean(grad_normed * normed, axis=-1, keepdims=True)
    return inverse * (grad_normed - mean_grad - normed * mean_prod)


def part(mod, index):
    return mod[0:1, index * D : (index + 1) * D]


def swap_halves(values):
    lanes = values.shape[1]
    lane = lax.broadcasted_iota(jnp.int32, values.shape, 1) % HD
    eight, twelve = HD // 8, 3 * HD // 16
    quarter, last = HD // 4, HD // 4 + 2 * twelve

    def ahead(step):
        return pltpu.roll(values, lanes - step, 1)

    def behind(step):
        return pltpu.roll(values, step, 1)

    first_half = ((lane >= quarter) & (lane < quarter + twelve)) | (
        (lane >= last) & (lane < last + twelve)
    )
    short = jnp.where(lane < eight, ahead(eight), behind(eight))
    long = jnp.where(first_half, ahead(twelve), behind(twelve))
    return jnp.where(lane < quarter, short, long)


def turned(values, cosine, sine):
    wide = cosine.shape[1]
    pieces = []
    for at in range(0, values.shape[1], wide):
        block = values[:, at : at + wide]
        pieces.append(block * cosine + swap_halves(block) * sine)
    return pieces[0] if len(pieces) == 1 else jnp.concatenate(pieces, axis=1)


def input_kernel(tokens, mod, w_query, w_key, w_value, cosine, sine, hidden, query, pair):
    @pl.when(pl.program_id(0) == 0)
    def _():
        normed, unused = normalize(tokens[...].astype(WIDE))
        hidden[...] = (normed * (1.0 + part(mod, SCALE_ONE)) + part(mod, SHIFT_ONE)).astype(LOW)

    groups, unused, lanes = query.shape
    h = hidden[...]
    cos, sin = cosine[...], sine[...]
    k = turned(dot(h, w_key[...]), cos, sin).astype(LOW)
    v = dot(h, w_value[...]).astype(LOW)
    q = turned(dot(h, w_query[...]), cos, sin).astype(LOW)
    for g in range(groups):
        span = slice(g * lanes, (g + 1) * lanes)
        pair[g, 0] = k[:, span]
        pair[g, 1] = v[:, span]
        query[g] = q[:, span]


def input_projections(tokens, mod, w_query, w_key, w_value, cosine, sine, frames):
    count = tokens.shape[0]
    lanes = D // frames
    wide = 256
    groups = wide // lanes
    weight = pl.BlockSpec((D, wide), lambda c: (0, c))
    heads = pl.BlockSpec((groups, count, lanes), lambda c: (c, 0, 0))
    pairs = pl.BlockSpec((groups, 2, count, lanes), lambda c: (c, 0, 0, 0))
    return pl.pallas_call(
        input_kernel,
        grid=(D // wide,),
        out_shape=[
            jax.ShapeDtypeStruct((count, D), LOW),
            jax.ShapeDtypeStruct((frames, count, lanes), LOW),
            jax.ShapeDtypeStruct((frames, 2, count, lanes), LOW),
        ],
        in_specs=[whole((count, D)), whole((1, 6 * D)), weight, weight, weight]
        + [whole(cosine.shape)] * 2,
        out_specs=[whole((count, D)), heads, pairs],
        compiler_params=pltpu.CompilerParams(vmem_limit_bytes=48 * MIB),
        cost_estimate=pl.CostEstimate(
            flops=6 * count * D * D, bytes_accessed=12 * MIB, transcendentals=0
        ),
        name="input_projections",
    )(tokens, mod, w_query, w_key, w_value, cosine, sine)


def pull_kernel(cotangent, mod, w_down, pulled, scaled_turned, scaled):
    @pl.when(pl.program_id(0) == 0)
    def _():
        scaled[...] = (part(mod, GATE_TWO) * cotangent[...].astype(WIDE)).astype(LOW)
        scaled_turned[...] = scaled[...].T

    pulled[...] = dot(scaled[...], w_down[...], ROWS_ROWS).astype(LOW)


def pull_down(cotangent, mod, w_down):
    count = cotangent.shape[0]
    wide = 512
    return pl.pallas_call(
        pull_kernel,
        grid=(FF // wide,),
        out_shape=[
            jax.ShapeDtypeStruct((count, FF), LOW), jax.ShapeDtypeStruct((D, count), LOW)
        ],
        in_specs=[
            whole((count, D)), whole((1, 6 * D)), pl.BlockSpec((wide, D), lambda c: (c, 0))
        ],
        out_specs=[pl.BlockSpec((count, wide), lambda c: (0, c)), whole((D, count))],
        scratch_shapes=[pltpu.VMEM((count, D), LOW)],
        compiler_params=pltpu.CompilerParams(vmem_limit_bytes=32 * MIB),
        cost_estimate=pl.CostEstimate(
            flops=2 * count * D * FF, bytes_accessed=14 * MIB, transcendentals=0
        ),
        name="pull_down",
    )(cotangent, mod, w_down)


def middle_kernel(
    attn, tokens, cotangent, mod, w_proj, w_up, pulled,
    middle, hidden, active, grad_up_in, grad_middle, grad_branch, grad_attn,
    grad_gate, grad_shift, grad_scale, branch, normed, inverse, total
):
    step = pl.program_id(0)
    frames, count, lanes = attn.shape

    @pl.when(step == 0)
    def _():
        for f in range(frames):
            hidden[:, f * lanes : (f + 1) * lanes] = attn[f]
        product = dot(hidden[...], w_proj[...])
        branch[...] = product
        mid = tokens[...].astype(WIDE) + part(mod, GATE_ONE) * product
        middle[...] = mid
        n, inv = normalize(mid)
        normed[...] = n
        inverse[...] = inv
        hidden[...] = (n * (1.0 + part(mod, SCALE_TWO)) + part(mod, SHIFT_TWO)).astype(LOW)
        total[...] = jnp.zeros(total.shape, WIDE)

    weight = w_up[...]
    u = dot(hidden[...], weight)
    rate = math.sqrt(2.0 / math.pi)
    square = u * u
    bend = jnp.tanh(rate * (u + 0.044715 * (u * square)))
    half = 0.5 * (1.0 + bend)
    active[...] = (u * half).astype(LOW)
    slope = half + (0.5 * rate) * u * (1.0 - bend * bend) * (1.0 + (3 * 0.044715) * square)
    du = (pulled[...].astype(WIDE) * slope).astype(LOW)
    grad_up_in[...] = du
    total[...] += dot(du, weight, ROWS_ROWS)

    @pl.when(step == pl.num_programs(0) - 1)
    def _():
        dh = total[...]
        n = normed[...]
        grad_scale[...] = column_sum(dh * n)
        grad_shift[...] = column_sum(dh)
        dx = cotangent[...].astype(WIDE) + norm_backward(
            dh * (1.0 + part(mod, SCALE_TWO)), n, inverse[...]
        )
        grad_middle[...] = dx
        grad_gate[...] = column_sum(dx * branch[...])
        dy = (part(mod, GATE_ONE) * dx).astype(LOW)
        grad_branch[...] = dy
        back = dot(dy, w_proj[...], ROWS_ROWS).astype(LOW)
        for f in range(frames):
            grad_attn[f] = back[:, f * lanes : (f + 1) * lanes]


def middle_block(attn, tokens, cotangent, mod, w_proj, w_up, pulled):
    frames, count, lanes = attn.shape
    wide = 512
    flat = whole((count, D))
    row = whole((1, D))
    columns = pl.BlockSpec((count, wide), lambda c: (0, c))
    heads = whole(attn.shape)

    def of(shape, kind):
        return jax.ShapeDtypeStruct(shape, kind)

    return pl.pallas_call(
        middle_kernel,
        grid=(FF // wide,),
        out_shape=[
            of((count, D), WIDE), of((count, D), LOW), of((count, FF), LOW), of((count, FF), LOW),
            of((count, D), WIDE), of((count, D), LOW), of(attn.shape, LOW),
            of((1, D), WIDE), of((1, D), WIDE), of((1, D), WIDE),
        ],
        in_specs=[
            heads, flat, flat, whole((1, 6 * D)), whole((D, D)),
            pl.BlockSpec((D, wide), lambda c: (0, c)), columns,
        ],
        out_specs=[flat, flat, columns, columns, flat, flat, heads, row, row, row],
        scratch_shapes=[
            pltpu.VMEM((count, D), WIDE), pltpu.VMEM((count, D), WIDE),
            pltpu.VMEM((count, 1), WIDE), pltpu.VMEM((count, D), WIDE),
        ],
        compiler_params=pltpu.CompilerParams(vmem_limit_bytes=56 * MIB),
        cost_estimate=pl.CostEstimate(
            flops=2 * count * D * (2 * FF + 2 * D), bytes_accessed=30 * MIB,
            transcendentals=count * FF,
        ),
        name="middle_block",
    )(attn, tokens, cotangent, mod, w_proj, w_up, pulled)


def weights_kernel(
    slot, active, grad_up_in, hidden, scaled_turned, attn, grad_branch, *refs, keep
):
    step = pl.program_id(0)
    frames, count, lanes = attn.shape
    half = frames // 2
    wide = D // frames
    if keep:
        activity, middle, cotangent, mod, w_down = refs[:5]
        out, grad_gate, down_out, up_out, hidden_turned, attn_turned, flat, total = refs[5:]
    else:
        down_out, up_out, hidden_turned, attn_turned, flat = refs
    chunks, narrow = down_out.shape[1], down_out.shape[3]

    @pl.when(step == 0)
    def _():
        for f in range(frames):
            flat[:, f * lanes : (f + 1) * lanes] = attn[f]
        for f in range(frames):
            place = lax.bitwise_xor(f, slot[0])

            @pl.when(place % 2 == (0 if keep else 1))
            def _():
                span = slice(f * wide, (f + 1) * wide)
                hidden_turned[place // 2] = hidden[:, span].T
                attn_turned[place // 2] = flat[:, span].T

        if keep:
            total[...] = jnp.zeros(total.shape, WIDE)

    @pl.when(step < half)
    def _():
        if keep:
            total[...] += dot(activity[...], w_down[...])
        down = dot(scaled_turned[...], active[...]).astype(LOW)
        for r in range(chunks):
            down_out[0, r] = down[:, r * narrow : (r + 1) * narrow]
        up = dot(hidden_turned[...].reshape(D // 2, count), grad_up_in[...]).astype(LOW)
        up_out[...] = up.reshape(half, wide, up.shape[1])

    @pl.when(step >= half)
    def _():
        proj = dot(attn_turned[...].reshape(D // 2, count), grad_branch[...]).astype(LOW)
        up_out[...] = proj.reshape(half, wide, proj.shape[1])

    if keep:
        @pl.when(step == half - 1)
        def _():
            z = total[...]
            out[...] = (middle[...] + part(mod, GATE_TWO) * z).astype(LOW)
            grad_gate[...] = column_sum(cotangent[...].astype(WIDE) * z)


def weight_gradients(
    slot, active, grad_up_in, hidden, scaled_turned, attn, grad_branch, rows, finish
):
    frames, count, lanes = attn.shape
    keep = finish is not None
    half = frames // 2
    narrow = FF // frames
    wide = FF // half
    extra = D // wide

    def down_block(i, slot):
        place = 2 * jnp.minimum(i, half - 1) + (0 if keep else 1)
        return lax.bitwise_xor(place, slot[0])

    def up_block(i, slot):
        return jnp.minimum(i, half - 1)

    flat = whole((count, D))
    down = (1, rows, D, narrow // rows)
    in_specs = [
        pl.BlockSpec((count, narrow), lambda i, slot: (0, down_block(i, slot))),
        pl.BlockSpec((count, wide), lambda i, slot: (0, up_block(i, slot))),
        flat, whole((D, count)), whole(attn.shape),
        pl.BlockSpec((count, wide), lambda i, slot: (0, jnp.maximum(i - half, 0))),
    ]
    out_specs = [
        pl.BlockSpec(down, lambda i, slot: (jnp.minimum(i, half - 1), 0, 0, 0)),
        pl.BlockSpec((half, D // frames, wide), lambda i, slot: (0, 0, i)),
    ]
    out_shape = [
        jax.ShapeDtypeStruct((half, rows, D, narrow // rows), LOW),
        jax.ShapeDtypeStruct((half, D // frames, FF + D), LOW),
    ]
    scratch = [
        pltpu.VMEM((half, D // frames, count), LOW), pltpu.VMEM((half, D // frames, count), LOW),
        pltpu.VMEM((count, D), LOW),
    ]
    args = (slot, active, grad_up_in, hidden, scaled_turned, attn, grad_branch)
    if keep:
        args += (active,) + tuple(finish)
        in_specs += [
            pl.BlockSpec((count, wide), lambda i, slot: (0, up_block(i, slot))),
            flat, flat, whole((1, 6 * D)),
            pl.BlockSpec((wide, D), lambda i, slot: (up_block(i, slot), 0)),
        ]
        out_specs = [flat, whole((1, D))] + out_specs
        out_shape = [
            jax.ShapeDtypeStruct((count, D), LOW), jax.ShapeDtypeStruct((1, D), WIDE)
        ] + out_shape
        scratch.append(pltpu.VMEM((count, D), WIDE))
    return pl.pallas_call(
        functools.partial(weights_kernel, keep=keep),
        grid_spec=pltpu.PrefetchScalarGridSpec(
            num_scalar_prefetch=1, grid=(half + extra,),
            in_specs=in_specs, out_specs=out_specs, scratch_shapes=scratch,
        ),
        out_shape=out_shape,
        compiler_params=pltpu.CompilerParams(vmem_limit_bytes=56 * MIB),
        cost_estimate=pl.CostEstimate(
            flops=count * D * (2 * FF + D + (2 * FF if keep else 0)), bytes_accessed=24 * MIB,
            transcendentals=0,
        ),
        name="weight_gradients",
    )(*args)


def turn_kernel(hidden, target):
    target[...] = hidden[...].T


def turn_hidden(hidden):
    return pl.pallas_call(
        turn_kernel,
        out_shape=jax.ShapeDtypeStruct(hidden.shape[::-1], LOW),
        in_specs=[vmem()],
        out_specs=vmem(),
        compiler_params=pltpu.CompilerParams(vmem_limit_bytes=32 * MIB),
        cost_estimate=pl.CostEstimate(flops=0, bytes_accessed=2 * MIB, transcendentals=0),
        name="turn_hidden",
    )(hidden)


def head_kernel(grads, hidden, cosine, sine, time_cosine, time_sine, product, total):
    step = pl.program_id(0)

    @pl.when(step == 0)
    def _():
        total[...] = jnp.zeros(total.shape, WIDE)

    cos = cosine[...] + time_cosine[0]
    sin = -(sine[...] + time_sine[0])
    block = jnp.concatenate(
        [turned(grads[0, i].astype(WIDE), cos, sin).astype(LOW) for i in range(2)] + [grads[0, 2]],
        axis=1,
    )
    total[...] += dot(hidden[0], block)

    @pl.when(step == pl.num_programs(0) - 1)
    def _():
        product[...] = total[...].astype(LOW)


def head_gradients(grads, hidden_all, tables):
    frames, unused, count, lanes = grads.shape
    frame = pl.BlockSpec((1, 1, lanes), lambda f: (f, 0, 0))
    return pl.pallas_call(
        head_kernel,
        grid=(frames,),
        out_shape=jax.ShapeDtypeStruct((D, 3 * lanes), LOW),
        in_specs=[
            pl.BlockSpec((1, 3, count, lanes), lambda f: (f, 0, 0, 0)),
            pl.BlockSpec((1, D, count), lambda f: (f, 0, 0)),
            whole((count, lanes)), whole((count, lanes)), frame, frame,
        ],
        out_specs=whole((D, 3 * lanes)),
        scratch_shapes=[pltpu.VMEM((D, 3 * lanes), WIDE)],
        compiler_params=pltpu.CompilerParams(vmem_limit_bytes=32 * MIB),
        cost_estimate=pl.CostEstimate(
            flops=6 * frames * count * D * lanes, bytes_accessed=12 * MIB, transcendentals=0
        ),
        name="head_gradients",
    )(grads, hidden_all, *tables)


def output_kernel(
    grads, w_query, w_key, w_value, cosine, sine, tokens, mod, grad_middle,
    grad_tokens, grad_shift, grad_scale, total
):
    step = pl.program_id(0)
    groups = grads.shape[0]

    @pl.when(step == 0)
    def _():
        total[...] = jnp.zeros(total.shape, WIDE)

    dh = total[...]
    for i, weight in enumerate((w_query, w_key, w_value)):
        block = jnp.concatenate([grads[g, i] for g in range(groups)], axis=1)
        if i < 2:
            block = turned(block.astype(WIDE), cosine[...], -sine[...]).astype(LOW)
        dh = dh + dot(block, weight[...], ROWS_ROWS)
    total[...] = dh

    @pl.when(step == pl.num_programs(0) - 1)
    def _():
        dh = total[...]
        n, inverse = normalize(tokens[...].astype(WIDE))
        grad_scale[...] = column_sum(dh * n)
        grad_shift[...] = column_sum(dh)
        grad_tokens[...] = (
            grad_middle[...] + norm_backward(dh * (1.0 + part(mod, SCALE_ONE)), n, inverse)
        ).astype(LOW)


def input_gradients(grads, w_query, w_key, w_value, cosine, sine, tokens, mod, grad_middle):
    frames, unused, count, lanes = grads.shape
    wide = 256
    groups = wide // lanes
    flat = whole((count, D))
    row = whole((1, D))
    weight = pl.BlockSpec((D, wide), lambda c: (0, c))
    rows = jax.ShapeDtypeStruct((1, D), WIDE)
    return pl.pallas_call(
        output_kernel,
        grid=(D // wide,),
        out_shape=[jax.ShapeDtypeStruct((count, D), LOW), rows, rows],
        in_specs=[
            pl.BlockSpec((groups, 3, count, lanes), lambda c: (c, 0, 0, 0)),
            weight, weight, weight, whole(cosine.shape), whole(sine.shape),
            flat, whole((1, 6 * D)), flat,
        ],
        out_specs=[flat, row, row],
        scratch_shapes=[pltpu.VMEM((count, D), WIDE)],
        compiler_params=pltpu.CompilerParams(vmem_limit_bytes=48 * MIB),
        cost_estimate=pl.CostEstimate(
            flops=6 * count * D * D, bytes_accessed=14 * MIB, transcendentals=0
        ),
        name="input_gradients",
    )(grads, w_query, w_key, w_value, cosine, sine, tokens, mod, grad_middle)


def sinusoid(levels):
    half_size = D // 2
    freq_table = 10000.0 ** (-jnp.arange(half_size, dtype=WIDE) / half_size)
    angle_table = levels.astype(WIDE)[..., None] * freq_table
    return jnp.concatenate([jnp.cos(angle_table), jnp.sin(angle_table)], axis=-1)


def turn_tables(positions, heads):
    count = next(position.shape[0] for position in positions if position is not None)
    cosines, sines = [], []
    for position, part_size in zip(positions, (HD // 4, 3 * HD // 8, 3 * HD // 8)):
        half_size = part_size // 2
        if position is None:
            cosine = sine = jnp.zeros((count, half_size), WIDE)
        else:
            freq_table = 10000.0 ** (-jnp.arange(half_size, dtype=WIDE) / half_size)
            angle_table = position[:, None] * freq_table
            cosine = jnp.cos(angle_table)
            sine = jnp.sin(angle_table)
        cosines += [cosine, cosine]
        sines += [-sine, sine]
    return (
        jnp.concatenate(cosines * heads, axis=-1),
        jnp.concatenate(sines * heads, axis=-1),
    )


def shards(
    block_in, block_map, noise_level, w_query, w_key, w_value, w_proj, w_up, w_down, w_mod, cotangent
):
    frames = lax.axis_size("frames")
    sides = lax.axis_size("side")
    row_total = lax.axis_size("half") * sides
    frame_slot = lax.axis_index("frames")
    half = lax.axis_index("half")
    side = lax.axis_index("side")
    across = ("half", "side")
    everyone = ("frames",) + across
    devices = frames * row_total
    clips = block_in.shape[1]
    local_rows = block_in.shape[2]
    lanes = D // frames
    heads = max(lanes // HD, 1)
    order = jnp.argsort(block_map).astype(jnp.int32)
    slot = frame_slot.astype(jnp.int32).reshape(1)

    def tie(*arrays):
        return lax.optimization_barrier(arrays)

    def clip_tokens(tokens, clip):
        return lax.dynamic_index_in_dim(tokens[0], clip, 0, keepdims=False).reshape(-1, D)

    def other_half(array):
        return lax.ppermute(array, "half", [(0, 1), (1, 0)])

    def return_clip(own, came, kind):
        first = jnp.where(half == 0, own, came).astype(kind)
        second = jnp.where(half == 0, came, own).astype(kind)
        return jnp.stack([first, second]).reshape(1, clips, local_rows, PC, D)

    def swap_groups(grouped):
        return lax.all_to_all(grouped, "frames", split_axis=0, concat_axis=0, tiled=True)

    def pass_on(array, step):
        return lax.ppermute(array, "side", [(i, (i + step) % sides) for i in range(sides)])

    def flip(array, bit):
        return lax.ppermute(array, "frames", [(i, i ^ (1 << bit)) for i in range(frames)])

    def add(left, right):
        return (left.astype(WIDE) + right.astype(WIDE)).astype(LOW)

    def swap_rows(total):
        return lax.all_to_all(total, across, split_axis=0, concat_axis=0, tiled=True)

    class Reduction:
        def __init__(self, send, bits):
            self.came = flip(send, 0)
            self.bits = list(bits)
            self.left = sorted(bits, reverse=True)
            self.over_rows = False

        def start(self, keep):
            shape = (2,) * len(self.bits) + keep.shape[1:]
            self.keep = keep.reshape(shape)

        def advance(self):
            came = self.came.reshape(self.keep.shape)
            if not self.bits:
                rows = add(self.keep, came)
                self.came = swap_rows(rows.reshape((row_total, -1) + rows.shape[-1:]))
                self.keep = rows
                self.over_rows = True
                return
            bit = self.bits.pop(0)
            axis = self.left.index(bit)
            self.left.remove(bit)

            def cut(array, which):
                return lax.index_in_dim(array, which, axis, keepdims=False)

            going = add(cut(self.keep, 1), cut(came, 1))
            self.keep = add(cut(self.keep, 0), cut(came, 0))
            self.going = going
            self.came = flip(going, bit)

        def finish(self):
            while not self.over_rows:
                self.advance()
            return jnp.sum(self.came.astype(WIDE), axis=0)

    high_bits = list(range(1, frames.bit_length() - 1))

    source_own = clip_tokens(block_in, half)
    source_came = other_half(clip_tokens(block_in, 1 - half))
    grad_going, source_came = tie(clip_tokens(cotangent, 1 - half), source_came)
    grad_came = other_half(grad_going)
    source = jnp.concatenate([source_own, source_came])
    half_count = source_own.shape[0]

    level = jnp.where(half == 0, noise_level[:, 0], noise_level[:, -1])
    embed = jax.nn.silu(sinusoid(level)).astype(LOW)
    mod = jnp.dot(embed, w_mod, preferred_element_type=WIDE)

    blocks = jnp.stack([half, 1 - half])[:, None, None]
    rows = (blocks * sides + side) * local_rows + jnp.arange(local_rows)[None, :, None]
    row_pos = jnp.broadcast_to(rows, (clips, local_rows, PC)).reshape(-1).astype(WIDE)
    col_pos = jnp.broadcast_to(jnp.arange(PC), (clips, local_rows, PC)).reshape(-1).astype(WIDE)
    place_cosine, place_sine = turn_tables((None, row_pos, col_pos), heads)
    time_cosine, time_sine = turn_tables((block_map.astype(WIDE), None, None), heads)
    cosine = place_cosine + time_cosine[frame_slot]
    sine = place_sine + time_sine[frame_slot]
    tables = (place_cosine, place_sine, time_cosine[:, None], time_sine[:, None])

    hidden_one, query, pair = input_projections(
        source, mod, w_query, w_key, w_value, cosine, sine, frames
    )
    pair = swap_groups(pair)
    query = swap_groups(query)
    hidden_all = lax.all_gather(turn_hidden(hidden_one), "frames", axis=0)
    grad_result = jnp.concatenate([clip_tokens(cotangent, half), grad_came])
    pulled, scaled_turned = pull_down(grad_result, mod, w_down)

    pairs = [pair] + [pass_on(pair, step) for step in range(1, sides)]
    state = None
    for step in range(sides):
        state = attention_forward(order, state, query, pairs[step], step == sides - 1)
    attn_heads, log_total = state
    attn = swap_groups(attn_heads)

    (
        middle, hidden_two, active, grad_up_in, grad_middle, grad_branch, grad_attn,
        grad_gate_one, grad_shift_two, grad_scale_two,
    ) = middle_block(attn, source, grad_result, mod, w_proj, w_up, pulled)
    grad_attn = swap_groups(grad_attn)
    inputs = (slot, active, grad_up_in, hidden_two, scaled_turned, attn, grad_branch, row_total)
    down_send, up_send = weight_gradients(*inputs, None)
    down = Reduction(down_send, high_bits)
    up = Reduction(up_send, high_bits[::-1])
    result, grad_gate_two, down_keep, up_keep = weight_gradients(
        *inputs, (middle, grad_result, mod, w_down)
    )
    down.start(down_keep)
    up.start(up_keep)

    def spread(vectors, codes):
        wide = jnp.concatenate(vectors, axis=-1)
        share_of = D // devices
        codes = codes.reshape(devices, share_of)
        packed = jnp.concatenate(
            [jnp.broadcast_to(wide, (devices, wide.shape[-1])), codes], axis=-1
        )
        return lax.all_to_all(packed, everyone, split_axis=0, concat_axis=0, tiled=True)

    def mod_gradient(came):
        share_of = D // devices
        return jnp.einsum(
            "nd,ne->de",
            came[:, -share_of:],
            came[:, :-share_of],
            precision=lax.Precision.HIGHEST,
        )

    codes = embed.astype(WIDE)
    dq = None
    arrived = []
    cut = frames * 3 // 8
    calls = [(step, span) for step in range(sides - 1, -1, -1) for span in (0, 1)]
    for index, (step, span) in enumerate(calls):
        if index == 0:
            down.advance()
            up.advance()
            grad_attn, *ready = tie(grad_attn, down.going, down.keep, up.going, up.keep, result)
            out_came = other_half(result[half_count:])
        elif index == 1:
            dq, partial, down.came = tie(dq, partial, down.came)
            down.advance()
            mod_came = spread([grad_gate_one, grad_shift_two, grad_scale_two, grad_gate_two], codes)
            dq, partial, out_came, *ready = tie(dq, partial, out_came, down.came)
        elif index == 2:
            dq, down.came, up.came, mod_came = tie(dq, down.came, up.came, mod_came)
            down.advance()
            up.advance()
        elif index == 3:
            dq, partial, down.came, up.came = tie(dq, partial, down.came, up.came)
            up.advance()
        begin, end = ((0, cut), (cut, frames))[span]
        last = index == len(calls) - 1
        came = None
        if last and arrived:
            came = arrived[0]
            for more in arrived[1:]:
                came = add(came, more)
        answer = attention_backward(
            order, dq, None if span == 0 else partial, came, query, pairs[step], grad_attn,
            attn_heads, log_total, begin, end, last,
        )
        if last:
            grads = answer[0]
        else:
            dq, partial = answer
            if span == 1:
                arrived.append(pass_on(partial, -step))

    grads_back = swap_groups(grads)
    product = head_gradients(grads, hidden_all, tables)
    product = lax.all_to_all(
        product.reshape(devices, D // devices, 3 * lanes),
        everyone, split_axis=0, concat_axis=0, tiled=True,
    )
    product = jnp.sum(
        product.reshape(frames, row_total, D // devices, 3, lanes).astype(WIDE), axis=1
    )
    product = jnp.transpose(product, (2, 1, 0, 3)).reshape(3, D // devices, D)
    grad_source, grad_shift_one, grad_scale_one = input_gradients(
        grads_back, w_query, w_key, w_value, cosine, sine, source, mod, grad_middle
    )
    in_came = other_half(grad_source[half_count:])
    late_came = spread([grad_shift_one, grad_scale_one], codes)

    grad_down = down.finish().T
    up_proj = up.finish()
    grad_mod = jnp.concatenate([mod_gradient(late_came), mod_gradient(mod_came)], axis=-1)
    return (
        return_clip(result[:half_count], out_came, LOW),
        return_clip(grad_source[:half_count], in_came, WIDE),
        product[0], product[1], product[2],
        up_proj[:, FF:], up_proj[:, :FF], grad_down, grad_mod,
    )


def solution(mesh):
    frames, rows = mesh.shape["frames"], mesh.shape["rows"]
    clips = 2
    split = Mesh(
        mesh.devices.reshape(frames, clips, rows // clips), ("frames", "half", "side")
    )
    tokens = P("frames", None, ("half", "side"), None, None)
    shared = P(("frames", "half", "side"), None)
    return jax.shard_map(
        shards,
        mesh=split,
        in_specs=(tokens, P(), P("frames", None), P(), P(), P(), P(), P(), P(), P(), tokens),
        out_specs=(tokens, tokens) + (shared,) * 7,
        check_vma=False,
    )
```

```python
import functools
import math

import jax
import jax.numpy as jnp
from jax import lax
from jax.experimental import pallas as pl
from jax.experimental.pallas import tpu as pltpu
from jax.sharding import Mesh, PartitionSpec as P

D = 1024
H = 16
HD = 64
FF = 4096
PR = 32
PC = 32

norm_eps = 1e-06
LOW = jnp.bfloat16
WIDE = jnp.float32
MIB = 2**20
SCALE2 = math.log2(math.e) / math.sqrt(HD)
SAFE_LOG2 = 100.0
ROWS_ROWS = (((1,), (1,)), ((), ()))
ROWS_COLS = (((1,), (0,)), ((), ()))
SHIFT_ONE, SCALE_ONE, GATE_ONE, SHIFT_TWO, SCALE_TWO, GATE_TWO = range(6)


def dot(left, right, dims=ROWS_COLS):
    return lax.dot_general(left, right, dims, preferred_element_type=WIDE)


def exact_dot(left, right, dims=ROWS_COLS):
    return lax.dot_general(
        left, right, dims, preferred_element_type=WIDE, precision=lax.Precision.HIGHEST
    )


def vmem():
    return pl.BlockSpec(memory_space=pltpu.VMEM)


def smem():
    return pl.BlockSpec(memory_space=pltpu.SMEM)


def whole(shape):
    return pl.BlockSpec(shape, lambda *unused: (0,) * len(shape))


def behind(kernel, count):
    def ordered(*refs):
        return kernel(*refs[count:])

    return ordered


def anywhere(count):
    return [pl.BlockSpec(memory_space=pl.ANY)] * count


def column_sum(values):
    return jnp.sum(values, axis=0, keepdims=True)


def head_masks(rows, lanes, heads):
    lane = lax.broadcasted_iota(jnp.int32, (rows, lanes), 1)
    return [lane // HD == h for h in range(heads)]


def square_norm(values, masks):
    squared = values.astype(WIDE)
    squared = squared * squared
    return [
        jnp.max(jnp.sum(jnp.where(mask, squared, 0.0), axis=1, keepdims=True)) for mask in masks
    ]


def forward_kernel(order, flag_in, query, pair, *refs, first, last, heads):
    frames, tokens, lanes = query.shape
    if not first:
        num_in, sum_in, top_in = refs[:3]
        refs = refs[3:]
    if last:
        attn_out, log_out, keys, values = refs
    else:
        flag_out, num_out, sum_out, top_out, keys, values = refs
    masks = head_masks(tokens, lanes, heads)
    one = jnp.ones((tokens, lanes), LOW)
    zero = jnp.zeros((tokens, lanes), LOW)
    width = 2 * HD
    bound = jnp.float32(0.0)
    q_top = [jnp.float32(0.0)] * heads
    k_top = [jnp.float32(0.0)] * heads
    for f in range(frames):
        k = pair[f, 0]
        v = pair[f, 1]
        q_top = [jnp.maximum(a, b) for a, b in zip(q_top, square_norm(query[f], masks))]
        k_top = [jnp.maximum(a, b) for a, b in zip(k_top, square_norm(k, masks))]
        for h in range(heads):
            keys[h, f] = jnp.where(masks[h], k, zero)
            if heads == 2:
                values[h, f] = jnp.where(masks[h], v, one)
            else:
                values[h, f] = jnp.concatenate([v, one], axis=1)
    for a, b in zip(q_top, k_top):
        bound = jnp.maximum(bound, a * b)
    fast = bound * (SCALE2 * SCALE2) <= SAFE_LOG2 * SAFE_LOG2
    if not first:
        fast = jnp.logical_and(fast, flag_in[0] == 1)
    if not last:
        flag_out[0] = jnp.where(fast, 1, 0).astype(jnp.int32)
    low_lane = lax.broadcasted_iota(jnp.int32, (tokens, lanes), 1) < HD
    pick = lax.broadcasted_iota(jnp.int32, (8, lanes), 1) == HD * lax.broadcasted_iota(
        jnp.int32, (8, lanes), 0
    )
    pick = jnp.where(pick, 1.0, 0.0).astype(WIDE)

    def split(num, total):
        if heads == 2:
            turned = pltpu.roll(total, HD, 1)
            return [jnp.where(low_lane, num, turned), jnp.where(low_lane, turned, num)]
        return [jnp.concatenate([num, total], axis=1)]

    def join(accs):
        if heads == 2:
            num = jnp.where(low_lane, accs[0], accs[1])
            total = jnp.where(low_lane, accs[1], accs[0])
            return num, pltpu.roll(total, HD, 1)
        return accs[0][:, :HD], accs[0][:, HD:]

    def start(slot):
        if first:
            return [jnp.zeros((tokens, width), WIDE) for _ in range(heads)]
        return split(num_in[slot], sum_in[slot])

    def store(slot, accs, top):
        num, total = join(accs)
        if last:
            attn_out[slot] = (num / total).astype(LOW)
            logs = jnp.log2(total)
            if top is not None:
                logs = logs + top
            log_out[slot] = exact_dot(pick, logs, ROWS_ROWS)
        else:
            num_out[slot] = num
            sum_out[slot] = total
            top_out[slot] = jnp.zeros((tokens, lanes), WIDE) if top is None else top

    @pl.when(fast)
    def _():
        def outer(t, unused):
            slot = order[t]
            q = query[slot]

            def inner(j, accs):
                other = order[j]
                new = []
                for h in range(heads):
                    s = dot(q, keys[h, other], ROWS_ROWS)
                    p = jnp.exp2(s * SCALE2).astype(LOW)
                    new.append(accs[h] + dot(p, values[h, other]))
                return new

            store(slot, lax.fori_loop(0, t + 1, inner, start(slot)), None)
            return unused

        lax.fori_loop(0, frames, outer, 0)

    @pl.when(jnp.logical_not(fast))
    def _():
        def outer(t, unused):
            slot = order[t]
            q = query[slot]

            def inner(j, state):
                other = order[j]
                accs, tops = state
                new_accs, new_tops = [], []
                for h in range(heads):
                    s = dot(q, keys[h, other], ROWS_ROWS) * SCALE2
                    top = jnp.maximum(tops[h], jnp.max(s, axis=1, keepdims=True))
                    p = jnp.exp2(s - top).astype(LOW)
                    keep = jnp.exp2(tops[h] - top)
                    new_accs.append(accs[h] * keep + dot(p, values[h, other]))
                    new_tops.append(top)
                return new_accs, new_tops

            if first:
                tops = [jnp.full((tokens, 1), -1e30, WIDE)] * heads
            else:
                tops = [top_in[slot][:, h * HD : h * HD + 1] for h in range(heads)]
            accs, tops = lax.fori_loop(0, t + 1, inner, (start(slot), tops))
            top = jnp.broadcast_to(tops[0], (tokens, lanes))
            if heads == 2:
                top = jnp.where(low_lane, top, jnp.broadcast_to(tops[1], (tokens, lanes)))
            store(slot, accs, top)
            return unused

        lax.fori_loop(0, frames, outer, 0)


def attention_forward(order, state, query, pair, last):
    frames, tokens, lanes = query.shape
    heads = lanes // HD
    first = state is None
    wide = jax.ShapeDtypeStruct(query.shape, WIDE)
    if last:
        out_shape = [
            jax.ShapeDtypeStruct(query.shape, LOW),
            jax.ShapeDtypeStruct((frames, 8, tokens), WIDE),
        ]
        out_specs = [vmem()] * 2
    else:
        out_shape = [jax.ShapeDtypeStruct((1,), jnp.int32), wide, wide, wide]
        out_specs = [smem()] + [vmem()] * 3
    flag = jnp.zeros((1,), jnp.int32) if first else state[0]
    rest = () if first else tuple(state[1:])
    pairs = heads * frames * (frames + 1) // 2 * tokens * tokens
    return pl.pallas_call(
        functools.partial(forward_kernel, first=first, last=last, heads=heads),
        out_shape=out_shape,
        in_specs=[smem(), smem()] + [vmem()] * (2 + len(rest)),
        out_specs=out_specs,
        scratch_shapes=[
            pltpu.VMEM((heads, frames, tokens, lanes), LOW),
            pltpu.VMEM((heads, frames, tokens, max(lanes, 2 * HD)), LOW),
        ],
        compiler_params=pltpu.CompilerParams(vmem_limit_bytes=56 * MIB),
        cost_estimate=pl.CostEstimate(
            flops=pairs * 4 * HD * 8, bytes_accessed=16 * MIB, transcendentals=pairs
        ),
        name="attention_forward",
    )(order, flag, query, pair, *rest)


def backward_kernel(
    order, query, pair, grad, out, lse, *refs, first, last, begin, end, came, heads
):
    frames, tokens, lanes = query.shape
    if not first:
        dq_in = refs[0]
        refs = refs[1:]
    if begin > 0:
        pair_in = refs[0]
        refs = refs[1:]
    if came:
        pair_came = refs[0]
        refs = refs[1:]
    if last:
        final, queries, grads, delta, key_turned, dq_sum = refs
        places = (1, 2)
    else:
        dq_sum, final, queries, grads, delta, key_turned = refs
        places = (0, 1)
    masks = head_masks(tokens, lanes, heads)
    zero = jnp.zeros((tokens, lanes), LOW)
    lane8 = lax.broadcasted_iota(jnp.int32, (8, lanes), 1) // HD
    pick = jnp.where(lane8 == lax.broadcasted_iota(jnp.int32, (8, lanes), 0), 1.0, 0.0)
    for f in range(frames):
        q = query[f]
        g = grad[f]
        for h in range(heads):
            queries[h, f] = jnp.where(masks[h], q, zero)
            grads[h, f] = jnp.where(masks[h], g, zero)
        key_turned[f] = pair[f, 0].T
        delta[f] = exact_dot(
            pick.astype(WIDE), g.astype(WIDE) * out[f].astype(WIDE), ROWS_ROWS
        )
        dq_sum[f] = jnp.zeros((lanes, tokens), WIDE) if first else dq_in[f]
        if begin > 0:
            for i in range(2):
                old = pair_in[f, i]
                if came:
                    old = (old.astype(WIDE) + pair_came[f, i].astype(WIDE)).astype(LOW)
                final[f, places[i]] = old

    def outer(t, unused):
        slot = order[t]
        k = pair[slot, 0]
        v = pair[slot, 1]
        ks = [jnp.where(mask, k, zero) for mask in masks]
        vs = [jnp.where(mask, v, zero) for mask in masks]

        def inner(j, carry):
            other = order[j]
            dk, dv = carry
            for h in range(heads):
                q = queries[h, other]
                g = grads[h, other]
                s = dot(ks[h], q, ROWS_ROWS)
                p = jnp.exp2(s * SCALE2 - lse[other, h : h + 1, :])
                dp = dot(vs[h], g, ROWS_ROWS)
                ds = (p * (dp - delta[other, h : h + 1, :])).astype(LOW)
                dv = dv + dot(p.astype(LOW), g)
                dk = dk + dot(ds, q)
                span = slice(h * HD, (h + 1) * HD)
                dq_sum[other, span, :] += dot(key_turned[slot, span, :], ds)
            return dk, dv

        start = jnp.zeros((tokens, lanes), WIDE)
        dk, dv = lax.fori_loop(t, frames, inner, (start, start))
        dk = dk * (1.0 / math.sqrt(HD))
        if came:
            dk = dk + pair_came[slot, 0].astype(WIDE)
            dv = dv + pair_came[slot, 1].astype(WIDE)
        final[slot, places[0]] = dk.astype(LOW)
        final[slot, places[1]] = dv.astype(LOW)
        return unused

    lax.fori_loop(begin, end, outer, 0)
    if last:
        for f in range(frames):
            final[f, 0] = (dq_sum[f].T * (1.0 / math.sqrt(HD))).astype(LOW)


def attention_backward(
    order, dq, partial, came, query, pair, grad, out, lse, begin, end, last, after
):
    frames, tokens, lanes = query.shape
    heads = lanes // HD
    first = dq is None
    sums = (frames, lanes, tokens)
    extra = tuple(
        array for array in (dq, partial if begin > 0 else None, came) if array is not None
    )
    steps = sum(frames - t for t in range(begin, end))
    work = heads * steps * tokens * tokens
    scratch = [
        pltpu.VMEM((heads, frames, tokens, lanes), LOW),
        pltpu.VMEM((heads, frames, tokens, lanes), LOW),
        pltpu.VMEM((frames, 8, tokens), WIDE),
        pltpu.VMEM((frames, lanes, tokens), LOW),
    ]
    if last:
        out_shape = [jax.ShapeDtypeStruct((frames, 3, tokens, lanes), LOW)]
        scratch.append(pltpu.VMEM(sums, WIDE))
    else:
        out_shape = [
            jax.ShapeDtypeStruct(sums, WIDE), jax.ShapeDtypeStruct((frames, 2, tokens, lanes), LOW)
        ]
    return pl.pallas_call(
        behind(
            functools.partial(
                backward_kernel, first=first, last=last, begin=begin, end=end,
                came=came is not None, heads=heads,
            ),
            len(after),
        ),
        out_shape=out_shape,
        in_specs=anywhere(len(after)) + [smem()] + [vmem()] * (5 + len(extra)),
        out_specs=[vmem()] * len(out_shape),
        scratch_shapes=scratch,
        compiler_params=pltpu.CompilerParams(vmem_limit_bytes=56 * MIB),
        cost_estimate=pl.CostEstimate(
            flops=work * 10 * HD * 5, bytes_accessed=16 * MIB, transcendentals=work
        ),
        name="attention_backward",
    )(*after, order, query, pair, grad, out, lse, *extra)


def normalize(values):
    centered = values - jnp.mean(values, axis=-1, keepdims=True)
    inverse = lax.rsqrt(jnp.mean(centered * centered, axis=-1, keepdims=True) + norm_eps)
    return (centered * inverse, inverse)


def norm_backward(grad_normed, normed, inverse):
    mean_grad = jnp.mean(grad_normed, axis=-1, keepdims=True)
    mean_prod = jnp.mean(grad_normed * normed, axis=-1, keepdims=True)
    return inverse * (grad_normed - mean_grad - normed * mean_prod)


def part(mod, index):
    return mod[0:1, index * D : (index + 1) * D]


def swap_halves(values):
    lanes = values.shape[1]
    lane = lax.broadcasted_iota(jnp.int32, values.shape, 1) % HD
    eight, twelve = HD // 8, 3 * HD // 16
    quarter, last = HD // 4, HD // 4 + 2 * twelve

    def ahead(step):
        return pltpu.roll(values, lanes - step, 1)

    def behind(step):
        return pltpu.roll(values, step, 1)

    first_half = ((lane >= quarter) & (lane < quarter + twelve)) | (
        (lane >= last) & (lane < last + twelve)
    )
    short = jnp.where(lane < eight, ahead(eight), behind(eight))
    long = jnp.where(first_half, ahead(twelve), behind(twelve))
    return jnp.where(lane < quarter, short, long)


def turned(values, cosine, sine):
    wide = cosine.shape[1]
    pieces = []
    for at in range(0, values.shape[1], wide):
        block = values[:, at : at + wide]
        pieces.append(block * cosine + swap_halves(block) * sine)
    return pieces[0] if len(pieces) == 1 else jnp.concatenate(pieces, axis=1)


def input_kernel(tokens, mod, w_query, w_key, w_value, cosine, sine, hidden, query, pair):
    @pl.when(pl.program_id(0) == 0)
    def _():
        normed, unused = normalize(tokens[...].astype(WIDE))
        hidden[...] = (normed * (1.0 + part(mod, SCALE_ONE)) + part(mod, SHIFT_ONE)).astype(LOW)

    groups, unused, lanes = query.shape
    h = hidden[...]
    cos, sin = cosine[...], sine[...]
    k = turned(dot(h, w_key[...]), cos, sin).astype(LOW)
    v = dot(h, w_value[...]).astype(LOW)
    q = turned(dot(h, w_query[...]), cos, sin).astype(LOW)
    for g in range(groups):
        span = slice(g * lanes, (g + 1) * lanes)
        pair[g, 0] = k[:, span]
        pair[g, 1] = v[:, span]
        query[g] = q[:, span]


def input_projections(tokens, mod, w_query, w_key, w_value, cosine, sine, frames):
    count = tokens.shape[0]
    lanes = D // frames
    wide = 256
    groups = wide // lanes
    weight = pl.BlockSpec((D, wide), lambda c: (0, c))
    heads = pl.BlockSpec((groups, count, lanes), lambda c: (c, 0, 0))
    pairs = pl.BlockSpec((groups, 2, count, lanes), lambda c: (c, 0, 0, 0))
    return pl.pallas_call(
        input_kernel,
        grid=(D // wide,),
        out_shape=[
            jax.ShapeDtypeStruct((count, D), LOW),
            jax.ShapeDtypeStruct((frames, count, lanes), LOW),
            jax.ShapeDtypeStruct((frames, 2, count, lanes), LOW),
        ],
        in_specs=[whole((count, D)), whole((1, 6 * D)), weight, weight, weight]
        + [whole(cosine.shape)] * 2,
        out_specs=[whole((count, D)), heads, pairs],
        compiler_params=pltpu.CompilerParams(vmem_limit_bytes=48 * MIB),
        cost_estimate=pl.CostEstimate(
            flops=6 * count * D * D, bytes_accessed=12 * MIB, transcendentals=0
        ),
        name="input_projections",
    )(tokens, mod, w_query, w_key, w_value, cosine, sine)


def pull_kernel(cotangent, mod, w_down, pulled, scaled_turned, scaled):
    @pl.when(pl.program_id(0) == 0)
    def _():
        scaled[...] = (part(mod, GATE_TWO) * cotangent[...].astype(WIDE)).astype(LOW)
        scaled_turned[...] = scaled[...].T

    pulled[...] = dot(scaled[...], w_down[...], ROWS_ROWS).astype(LOW)


def pull_down(cotangent, mod, w_down):
    count = cotangent.shape[0]
    wide = 512
    return pl.pallas_call(
        pull_kernel,
        grid=(FF // wide,),
        out_shape=[
            jax.ShapeDtypeStruct((count, FF), LOW), jax.ShapeDtypeStruct((D, count), LOW)
        ],
        in_specs=[
            whole((count, D)), whole((1, 6 * D)), pl.BlockSpec((wide, D), lambda c: (c, 0))
        ],
        out_specs=[pl.BlockSpec((count, wide), lambda c: (0, c)), whole((D, count))],
        scratch_shapes=[pltpu.VMEM((count, D), LOW)],
        compiler_params=pltpu.CompilerParams(vmem_limit_bytes=32 * MIB),
        cost_estimate=pl.CostEstimate(
            flops=2 * count * D * FF, bytes_accessed=14 * MIB, transcendentals=0
        ),
        name="pull_down",
    )(cotangent, mod, w_down)


def middle_kernel(
    attn, tokens, cotangent, mod, w_proj, w_up, pulled,
    middle, hidden, active, grad_up_in, grad_middle, grad_branch, grad_attn,
    grad_gate, grad_shift, grad_scale, branch, normed, inverse, total
):
    step = pl.program_id(0)
    frames, count, lanes = attn.shape

    @pl.when(step == 0)
    def _():
        for f in range(frames):
            hidden[:, f * lanes : (f + 1) * lanes] = attn[f]
        product = dot(hidden[...], w_proj[...])
        branch[...] = product
        mid = tokens[...].astype(WIDE) + part(mod, GATE_ONE) * product
        middle[...] = mid
        n, inv = normalize(mid)
        normed[...] = n
        inverse[...] = inv
        hidden[...] = (n * (1.0 + part(mod, SCALE_TWO)) + part(mod, SHIFT_TWO)).astype(LOW)
        total[...] = jnp.zeros(total.shape, WIDE)

    weight = w_up[...]
    u = dot(hidden[...], weight)
    rate = math.sqrt(2.0 / math.pi)
    square = u * u
    bend = jnp.tanh(rate * (u + 0.044715 * (u * square)))
    half = 0.5 * (1.0 + bend)
    active[...] = (u * half).astype(LOW)
    slope = half + (0.5 * rate) * u * (1.0 - bend * bend) * (1.0 + (3 * 0.044715) * square)
    du = (pulled[...].astype(WIDE) * slope).astype(LOW)
    grad_up_in[...] = du
    total[...] += dot(du, weight, ROWS_ROWS)

    @pl.when(step == pl.num_programs(0) - 1)
    def _():
        dh = total[...]
        n = normed[...]
        grad_scale[...] = column_sum(dh * n)
        grad_shift[...] = column_sum(dh)
        dx = cotangent[...].astype(WIDE) + norm_backward(
            dh * (1.0 + part(mod, SCALE_TWO)), n, inverse[...]
        )
        grad_middle[...] = dx
        grad_gate[...] = column_sum(dx * branch[...])
        dy = (part(mod, GATE_ONE) * dx).astype(LOW)
        grad_branch[...] = dy
        back = dot(dy, w_proj[...], ROWS_ROWS).astype(LOW)
        for f in range(frames):
            grad_attn[f] = back[:, f * lanes : (f + 1) * lanes]


def middle_block(attn, tokens, cotangent, mod, w_proj, w_up, pulled):
    frames, count, lanes = attn.shape
    wide = 512
    flat = whole((count, D))
    row = whole((1, D))
    columns = pl.BlockSpec((count, wide), lambda c: (0, c))
    heads = whole(attn.shape)

    def of(shape, kind):
        return jax.ShapeDtypeStruct(shape, kind)

    return pl.pallas_call(
        middle_kernel,
        grid=(FF // wide,),
        out_shape=[
            of((count, D), WIDE), of((count, D), LOW), of((count, FF), LOW), of((count, FF), LOW),
            of((count, D), WIDE), of((count, D), LOW), of(attn.shape, LOW),
            of((1, D), WIDE), of((1, D), WIDE), of((1, D), WIDE),
        ],
        in_specs=[
            heads, flat, flat, whole((1, 6 * D)), whole((D, D)),
            pl.BlockSpec((D, wide), lambda c: (0, c)), columns,
        ],
        out_specs=[flat, flat, columns, columns, flat, flat, heads, row, row, row],
        scratch_shapes=[
            pltpu.VMEM((count, D), WIDE), pltpu.VMEM((count, D), WIDE),
            pltpu.VMEM((count, 1), WIDE), pltpu.VMEM((count, D), WIDE),
        ],
        compiler_params=pltpu.CompilerParams(vmem_limit_bytes=56 * MIB),
        cost_estimate=pl.CostEstimate(
            flops=2 * count * D * (2 * FF + 2 * D), bytes_accessed=30 * MIB,
            transcendentals=count * FF,
        ),
        name="middle_block",
    )(attn, tokens, cotangent, mod, w_proj, w_up, pulled)


def weights_kernel(
    slot, active, grad_up_in, hidden, scaled_turned, attn, grad_branch, *refs, keep
):
    step = pl.program_id(0)
    frames, count, lanes = attn.shape
    half = frames // 2
    wide = D // frames
    if keep:
        activity, middle, cotangent, mod, w_down = refs[:5]
        out, grad_gate, down_out, up_out, hidden_turned, attn_turned, flat, total = refs[5:]
    else:
        down_out, up_out, hidden_turned, attn_turned, flat = refs
    chunks, narrow = down_out.shape[1], down_out.shape[3]

    @pl.when(step == 0)
    def _():
        for f in range(frames):
            flat[:, f * lanes : (f + 1) * lanes] = attn[f]
        for f in range(frames):
            place = lax.bitwise_xor(f, slot[0])

            @pl.when(place % 2 == (0 if keep else 1))
            def _():
                span = slice(f * wide, (f + 1) * wide)
                hidden_turned[place // 2] = hidden[:, span].T
                attn_turned[place // 2] = flat[:, span].T

        if keep:
            total[...] = jnp.zeros(total.shape, WIDE)

    @pl.when(step < half)
    def _():
        if keep:
            total[...] += dot(activity[...], w_down[...])
        down = dot(scaled_turned[...], active[...]).astype(LOW)
        for r in range(chunks):
            down_out[0, r] = down[:, r * narrow : (r + 1) * narrow]
        up = dot(hidden_turned[...].reshape(D // 2, count), grad_up_in[...]).astype(LOW)
        up_out[...] = up.reshape(half, wide, up.shape[1])

    @pl.when(step >= half)
    def _():
        proj = dot(attn_turned[...].reshape(D // 2, count), grad_branch[...]).astype(LOW)
        up_out[...] = proj.reshape(half, wide, proj.shape[1])

    if keep:
        @pl.when(step == half - 1)
        def _():
            z = total[...]
            out[...] = (middle[...] + part(mod, GATE_TWO) * z).astype(LOW)
            grad_gate[...] = column_sum(cotangent[...].astype(WIDE) * z)


def weight_gradients(
    slot, active, grad_up_in, hidden, scaled_turned, attn, grad_branch, rows, finish
):
    frames, count, lanes = attn.shape
    keep = finish is not None
    half = frames // 2
    narrow = FF // frames
    wide = FF // half
    extra = D // wide

    def down_block(i, slot):
        place = 2 * jnp.minimum(i, half - 1) + (0 if keep else 1)
        return lax.bitwise_xor(place, slot[0])

    def up_block(i, slot):
        return jnp.minimum(i, half - 1)

    flat = whole((count, D))
    down = (1, rows, D, narrow // rows)
    in_specs = [
        pl.BlockSpec((count, narrow), lambda i, slot: (0, down_block(i, slot))),
        pl.BlockSpec((count, wide), lambda i, slot: (0, up_block(i, slot))),
        flat, whole((D, count)), whole(attn.shape),
        pl.BlockSpec((count, wide), lambda i, slot: (0, jnp.maximum(i - half, 0))),
    ]
    out_specs = [
        pl.BlockSpec(down, lambda i, slot: (jnp.minimum(i, half - 1), 0, 0, 0)),
        pl.BlockSpec((half, D // frames, wide), lambda i, slot: (0, 0, i)),
    ]
    out_shape = [
        jax.ShapeDtypeStruct((half, rows, D, narrow // rows), LOW),
        jax.ShapeDtypeStruct((half, D // frames, FF + D), LOW),
    ]
    scratch = [
        pltpu.VMEM((half, D // frames, count), LOW), pltpu.VMEM((half, D // frames, count), LOW),
        pltpu.VMEM((count, D), LOW),
    ]
    args = (slot, active, grad_up_in, hidden, scaled_turned, attn, grad_branch)
    if keep:
        args += (active,) + tuple(finish)
        in_specs += [
            pl.BlockSpec((count, wide), lambda i, slot: (0, up_block(i, slot))),
            flat, flat, whole((1, 6 * D)),
            pl.BlockSpec((wide, D), lambda i, slot: (up_block(i, slot), 0)),
        ]
        out_specs = [flat, whole((1, D))] + out_specs
        out_shape = [
            jax.ShapeDtypeStruct((count, D), LOW), jax.ShapeDtypeStruct((1, D), WIDE)
        ] + out_shape
        scratch.append(pltpu.VMEM((count, D), WIDE))
    return pl.pallas_call(
        functools.partial(weights_kernel, keep=keep),
        grid_spec=pltpu.PrefetchScalarGridSpec(
            num_scalar_prefetch=1, grid=(half + extra,),
            in_specs=in_specs, out_specs=out_specs, scratch_shapes=scratch,
        ),
        out_shape=out_shape,
        compiler_params=pltpu.CompilerParams(vmem_limit_bytes=56 * MIB),
        cost_estimate=pl.CostEstimate(
            flops=count * D * (2 * FF + D + (2 * FF if keep else 0)), bytes_accessed=24 * MIB,
            transcendentals=0,
        ),
        name="weight_gradients",
    )(*args)


def turn_kernel(hidden, target):
    target[...] = hidden[...].T


def turn_hidden(hidden):
    return pl.pallas_call(
        turn_kernel,
        out_shape=jax.ShapeDtypeStruct(hidden.shape[::-1], LOW),
        in_specs=[vmem()],
        out_specs=vmem(),
        compiler_params=pltpu.CompilerParams(vmem_limit_bytes=32 * MIB),
        cost_estimate=pl.CostEstimate(flops=0, bytes_accessed=2 * MIB, transcendentals=0),
        name="turn_hidden",
    )(hidden)


def head_kernel(grads, hidden, cosine, sine, time_cosine, time_sine, product, total):
    step = pl.program_id(0)

    @pl.when(step == 0)
    def _():
        total[...] = jnp.zeros(total.shape, WIDE)

    cos = cosine[...] + time_cosine[0]
    sin = -(sine[...] + time_sine[0])
    block = jnp.concatenate(
        [turned(grads[0, i].astype(WIDE), cos, sin).astype(LOW) for i in range(2)] + [grads[0, 2]],
        axis=1,
    )
    total[...] += dot(hidden[0], block)

    @pl.when(step == pl.num_programs(0) - 1)
    def _():
        product[...] = total[...].astype(LOW)


def head_gradients(grads, hidden_all, tables, after):
    frames, unused, count, lanes = grads.shape
    frame = pl.BlockSpec((1, 1, lanes), lambda f: (f, 0, 0))
    return pl.pallas_call(
        behind(head_kernel, len(after)),
        grid=(frames,),
        out_shape=jax.ShapeDtypeStruct((D, 3 * lanes), LOW),
        in_specs=anywhere(len(after)) + [
            pl.BlockSpec((1, 3, count, lanes), lambda f: (f, 0, 0, 0)),
            pl.BlockSpec((1, D, count), lambda f: (f, 0, 0)),
            whole((count, lanes)), whole((count, lanes)), frame, frame,
        ],
        out_specs=whole((D, 3 * lanes)),
        scratch_shapes=[pltpu.VMEM((D, 3 * lanes), WIDE)],
        compiler_params=pltpu.CompilerParams(vmem_limit_bytes=32 * MIB),
        cost_estimate=pl.CostEstimate(
            flops=6 * frames * count * D * lanes, bytes_accessed=12 * MIB, transcendentals=0
        ),
        name="head_gradients",
    )(*after, grads, hidden_all, *tables)


def output_kernel(
    grads, w_query, w_key, w_value, cosine, sine, tokens, mod, grad_middle,
    grad_tokens, grad_shift, grad_scale, total
):
    step = pl.program_id(0)
    groups = grads.shape[0]

    @pl.when(step == 0)
    def _():
        total[...] = jnp.zeros(total.shape, WIDE)

    dh = total[...]
    for i, weight in enumerate((w_query, w_key, w_value)):
        block = jnp.concatenate([grads[g, i] for g in range(groups)], axis=1)
        if i < 2:
            block = turned(block.astype(WIDE), cosine[...], -sine[...]).astype(LOW)
        dh = dh + dot(block, weight[...], ROWS_ROWS)
    total[...] = dh

    @pl.when(step == pl.num_programs(0) - 1)
    def _():
        dh = total[...]
        n, inverse = normalize(tokens[...].astype(WIDE))
        grad_scale[...] = column_sum(dh * n)
        grad_shift[...] = column_sum(dh)
        grad_tokens[...] = (
            grad_middle[...] + norm_backward(dh * (1.0 + part(mod, SCALE_ONE)), n, inverse)
        ).astype(LOW)


def input_gradients(grads, w_query, w_key, w_value, cosine, sine, tokens, mod, grad_middle, after):
    frames, unused, count, lanes = grads.shape
    wide = 256
    groups = wide // lanes
    flat = whole((count, D))
    row = whole((1, D))
    weight = pl.BlockSpec((D, wide), lambda c: (0, c))
    rows = jax.ShapeDtypeStruct((1, D), WIDE)
    return pl.pallas_call(
        behind(output_kernel, len(after)),
        grid=(D // wide,),
        out_shape=[jax.ShapeDtypeStruct((count, D), LOW), rows, rows],
        in_specs=anywhere(len(after)) + [
            pl.BlockSpec((groups, 3, count, lanes), lambda c: (c, 0, 0, 0)),
            weight, weight, weight, whole(cosine.shape), whole(sine.shape),
            flat, whole((1, 6 * D)), flat,
        ],
        out_specs=[flat, row, row],
        scratch_shapes=[pltpu.VMEM((count, D), WIDE)],
        compiler_params=pltpu.CompilerParams(vmem_limit_bytes=48 * MIB),
        cost_estimate=pl.CostEstimate(
            flops=6 * count * D * D, bytes_accessed=14 * MIB, transcendentals=0
        ),
        name="input_gradients",
    )(*after, grads, w_query, w_key, w_value, cosine, sine, tokens, mod, grad_middle)


def halves_kernel(mine, keep_give, came_give, keep_hold, came_hold, give, hold):
    give[0, 0] = (keep_give[0, 0, 0].astype(WIDE) + came_give[0, 0, 0].astype(WIDE)).astype(LOW)
    hold[0, 0] = (keep_hold[0, 0, 0].astype(WIDE) + came_hold[0, 0, 0].astype(WIDE)).astype(LOW)


def add_halves(keep, came, axis, mine, after):
    shape = keep.shape
    lead, trail = math.prod(shape[:axis]), math.prod(shape[axis + 1 : -2])
    rest = shape[:axis] + shape[axis + 1 :]
    block = (1, 1, 1) + shape[-2:]
    view = (lead, 2, trail) + shape[-2:]

    def part_of(other):
        def index(a, b, mine, *unused):
            return (a, 1 - mine[0] if other else mine[0], b, 0, 0)

        return pl.BlockSpec(block, index)

    out = pl.BlockSpec((1, 1) + shape[-2:], lambda a, b, *unused: (a, b, 0, 0))
    out_shape = jax.ShapeDtypeStruct((lead, trail) + shape[-2:], LOW)

    def ordered(mine, *refs):
        halves_kernel(mine, *refs[len(after) :])

    keep, came = keep.reshape(view), came.reshape(view)
    give, hold = pl.pallas_call(
        ordered,
        grid_spec=pltpu.PrefetchScalarGridSpec(
            num_scalar_prefetch=1,
            grid=(lead, trail),
            in_specs=anywhere(len(after)) + [part_of(True)] * 2 + [part_of(False)] * 2,
            out_specs=[out, out],
        ),
        out_shape=[out_shape, out_shape],
        cost_estimate=pl.CostEstimate(
            flops=keep.size, bytes_accessed=6 * keep.size, transcendentals=0
        ),
        name="add_halves",
    )(mine, *after, keep, came, keep, came)
    return give.reshape(rest), hold.reshape(rest)


def total_kernel(keep, came, total):
    total[...] = keep[...].astype(WIDE) + came[...].astype(WIDE)


def add_last(keep, came, after):
    return pl.pallas_call(
        behind(total_kernel, len(after)),
        out_shape=jax.ShapeDtypeStruct(keep.shape, WIDE),
        in_specs=anywhere(len(after)) + [vmem()] * 2,
        out_specs=vmem(),
        name="add_last",
    )(*after, keep, came)


def same_kernel(*unused):
    pass


def order_after(array, after):
    return pl.pallas_call(
        same_kernel,
        out_shape=jax.ShapeDtypeStruct(array.shape, array.dtype),
        in_specs=anywhere(len(after) + 1),
        out_specs=anywhere(1)[0],
        input_output_aliases={len(after): 0},
        name="order_after",
    )(*after, array)


def pack_kernel(*refs):
    *vectors, codes, packed = refs
    at = 0
    for vector in vectors:
        packed[:, at : at + D] = jnp.broadcast_to(vector[...], (packed.shape[0], D))
        at += D
    packed[:, at:] = codes[...]


def pack(vectors, codes, after):
    return pl.pallas_call(
        behind(pack_kernel, len(after)),
        out_shape=jax.ShapeDtypeStruct((codes.shape[0], len(vectors) * D + codes.shape[1]), WIDE),
        in_specs=anywhere(len(after)) + [vmem()] * (len(vectors) + 1),
        out_specs=vmem(),
        name="pack",
    )(*after, *vectors, codes)


def sinusoid(levels):
    half_size = D // 2
    freq_table = 10000.0 ** (-jnp.arange(half_size, dtype=WIDE) / half_size)
    angle_table = levels.astype(WIDE)[..., None] * freq_table
    return jnp.concatenate([jnp.cos(angle_table), jnp.sin(angle_table)], axis=-1)


def turn_tables(positions, heads):
    count = next(position.shape[0] for position in positions if position is not None)
    cosines, sines = [], []
    for position, part_size in zip(positions, (HD // 4, 3 * HD // 8, 3 * HD // 8)):
        half_size = part_size // 2
        if position is None:
            cosine = sine = jnp.zeros((count, half_size), WIDE)
        else:
            freq_table = 10000.0 ** (-jnp.arange(half_size, dtype=WIDE) / half_size)
            angle_table = position[:, None] * freq_table
            cosine = jnp.cos(angle_table)
            sine = jnp.sin(angle_table)
        cosines += [cosine, cosine]
        sines += [-sine, sine]
    return (
        jnp.concatenate(cosines * heads, axis=-1),
        jnp.concatenate(sines * heads, axis=-1),
    )


def shards(
    block_in, block_map, noise_level, w_query, w_key, w_value, w_proj, w_up, w_down, w_mod, cotangent
):
    frames = lax.axis_size("frames")
    sides = lax.axis_size("side")
    row_total = lax.axis_size("half") * sides
    frame_slot = lax.axis_index("frames")
    half = lax.axis_index("half")
    side = lax.axis_index("side")
    across = ("half", "side")
    everyone = ("frames",) + across
    devices = frames * row_total
    clips = block_in.shape[1]
    local_rows = block_in.shape[2]
    lanes = D // frames
    heads = max(lanes // HD, 1)
    order = jnp.argsort(block_map).astype(jnp.int32)
    slot = frame_slot.astype(jnp.int32).reshape(1)

    def tie(*arrays):
        return lax.optimization_barrier(arrays)

    def clip_tokens(tokens, clip):
        return lax.dynamic_index_in_dim(tokens[0], clip, 0, keepdims=False).reshape(-1, D)

    def other_half(array):
        return lax.ppermute(array, "half", [(0, 1), (1, 0)])

    def return_clip(own, came, kind):
        first = jnp.where(half == 0, own, came).astype(kind)
        second = jnp.where(half == 0, came, own).astype(kind)
        return jnp.stack([first, second]).reshape(1, clips, local_rows, PC, D)

    def swap_groups(grouped):
        return lax.all_to_all(grouped, "frames", split_axis=0, concat_axis=0, tiled=True)

    def pass_on(array, step):
        return lax.ppermute(array, "side", [(i, (i + step) % sides) for i in range(sides)])

    def flip(array, bit):
        return lax.ppermute(array, "frames", [(i, i ^ (1 << bit)) for i in range(frames)])

    def add(left, right):
        return (left.astype(WIDE) + right.astype(WIDE)).astype(LOW)

    class Reduction:
        def __init__(self, send, bits):
            self.came = flip(send, 0)
            self.bits = list(bits)
            self.left = sorted(bits, reverse=True)
            self.row_bits = [("side", bit) for bit in range(sides.bit_length() - 1)] + [("half", 0)]
            self.row_left = [("half", 0)] + self.row_bits[:-1][::-1]
            self.going = None

        def start(self, keep):
            rest = (row_total, -1) + keep.shape[-1:]
            self.shape = (2,) * (len(self.left) + len(self.row_left))
            self.keep = keep.reshape(self.shape + rest[1:])

        def advance(self, after=()):
            came = self.came.reshape(self.keep.shape)
            if self.bits:
                bit = self.bits.pop(0)
                axis = self.left.index(bit)
                self.left.remove(bit)
                name, mine = "frames", 0
            else:
                name, bit = self.row_bits.pop(0)
                axis = self.row_left.index((name, bit))
                self.row_left.remove((name, bit))
                mine = (lax.axis_index(name) >> bit) & 1

            mine = jnp.asarray(mine, jnp.int32).reshape(1)
            self.going, self.keep = add_halves(self.keep, came, axis, mine, after)
            size = lax.axis_size(name)
            self.came = lax.ppermute(self.going, name, [(i, i ^ (1 << bit)) for i in range(size)])

        def finish(self, after):
            while self.bits or self.row_bits:
                self.advance(after)
            return add_last(self.keep, self.came, after)

    high_bits = list(range(1, frames.bit_length() - 1))

    source_own = clip_tokens(block_in, half)
    source_came = other_half(clip_tokens(block_in, 1 - half))
    grad_going, source_came = tie(clip_tokens(cotangent, 1 - half), source_came)
    grad_came = other_half(grad_going)
    source = jnp.concatenate([source_own, source_came])
    half_count = source_own.shape[0]

    level = jnp.where(half == 0, noise_level[:, 0], noise_level[:, -1])
    embed = jax.nn.silu(sinusoid(level)).astype(LOW)
    mod = jnp.dot(embed, w_mod, preferred_element_type=WIDE)

    blocks = jnp.stack([half, 1 - half])[:, None, None]
    rows = (blocks * sides + side) * local_rows + jnp.arange(local_rows)[None, :, None]
    row_pos = jnp.broadcast_to(rows, (clips, local_rows, PC)).reshape(-1).astype(WIDE)
    col_pos = jnp.broadcast_to(jnp.arange(PC), (clips, local_rows, PC)).reshape(-1).astype(WIDE)
    place_cosine, place_sine = turn_tables((None, row_pos, col_pos), heads)
    time_cosine, time_sine = turn_tables((block_map.astype(WIDE), None, None), heads)
    cosine = place_cosine + time_cosine[frame_slot]
    sine = place_sine + time_sine[frame_slot]
    tables = (place_cosine, place_sine, time_cosine[:, None], time_sine[:, None])

    hidden_one, query, pair = input_projections(
        source, mod, w_query, w_key, w_value, cosine, sine, frames
    )
    pair = swap_groups(pair)
    query = swap_groups(query)
    hidden_all = lax.all_gather(turn_hidden(hidden_one), "frames", axis=0)
    grad_result = jnp.concatenate([clip_tokens(cotangent, half), grad_came])
    pulled, scaled_turned = pull_down(grad_result, mod, w_down)

    pairs = [pair] + [pass_on(pair, step) for step in range(1, sides)]
    state = None
    for step in range(sides):
        state = attention_forward(order, state, query, pairs[step], step == sides - 1)
    attn_heads, log_total = state
    attn = swap_groups(attn_heads)

    (
        middle, hidden_two, active, grad_up_in, grad_middle, grad_branch, grad_attn,
        grad_gate_one, grad_shift_two, grad_scale_two,
    ) = middle_block(attn, source, grad_result, mod, w_proj, w_up, pulled)
    grad_attn = swap_groups(grad_attn)
    inputs = (slot, active, grad_up_in, hidden_two, scaled_turned, attn, grad_branch, row_total)
    down_send, up_send = weight_gradients(*inputs, None)
    down = Reduction(down_send, high_bits)
    up = Reduction(up_send, high_bits[::-1])
    result, grad_gate_two, down_keep, up_keep = weight_gradients(
        *inputs, (middle, grad_result, mod, w_down)
    )
    down.start(down_keep)
    up.start(up_keep)

    def spread(vectors, after):
        packed = pack(vectors, codes, after)
        return lax.all_to_all(packed, everyone, split_axis=0, concat_axis=0, tiled=True)

    def mod_gradient(came):
        share_of = D // devices
        return jnp.einsum(
            "nd,ne->de",
            came[:, -share_of:],
            came[:, :-share_of],
            precision=lax.Precision.HIGHEST,
        )

    codes = embed.astype(WIDE).reshape(devices, D // devices)
    dq = None
    arrived = []
    cut = frames * 3 // 8
    calls = [(step, span) for step in range(sides - 1, -1, -1) for span in (0, 1)]
    for index, (step, span) in enumerate(calls):
        after = ()
        if index == 0:
            down.advance()
            up.advance()
            after = (down.going, up.going)
            out_came = other_half(result[half_count:])
        elif index == 1:
            mod_came = spread(
                [grad_gate_one, grad_shift_two, grad_scale_two, grad_gate_two], (dq, partial)
            )
        elif index == 2:
            down.advance((dq,))
            up.advance((dq,))
            after = (down.going, up.going, mod_came, out_came)
        elif index == 3:
            down.advance((dq,))
            up.advance((dq,))
            after = (down.going, up.going)
        begin, end = ((0, cut), (cut, frames))[span]
        last = index == len(calls) - 1
        came = None
        if last and arrived:
            came = arrived[0]
            for more in arrived[1:]:
                came = add(came, more)
        answer = attention_backward(
            order, dq, None if span == 0 else partial, came, query, pairs[step], grad_attn,
            attn_heads, log_total, begin, end, last, after,
        )
        if last:
            grads = answer[0]
        else:
            dq, partial = answer
            if span == 1:
                arrived.append(pass_on(partial, -step))
    grads = order_after(grads, (down.came, up.came))
    grads_back = swap_groups(grads)
    down.advance((grads,))
    up.advance((grads,))
    head_product = head_gradients(grads, hidden_all, tables, (down.going, up.going))
    head_product = order_after(head_product, (grads_back, down.came, up.came))
    product = lax.all_to_all(
        head_product.reshape(devices, D // devices, 3 * lanes),
        everyone, split_axis=0, concat_axis=0, tiled=True,
    )
    product = jnp.sum(
        product.reshape(frames, row_total, D // devices, 3, lanes).astype(WIDE), axis=1
    )
    product = jnp.transpose(product, (2, 1, 0, 3)).reshape(3, D // devices, D)
    grad_source, grad_shift_one, grad_scale_one = input_gradients(
        grads_back, w_query, w_key, w_value, cosine, sine, source, mod, grad_middle,
        (head_product,),
    )
    in_came = other_half(grad_source[half_count:])
    late_came = spread([grad_shift_one, grad_scale_one], (product,))

    grad_down = down.finish((grad_source,)).reshape(D, FF // devices).T
    up_proj = up.finish((grad_source,)).reshape(D // devices, FF + D)
    grad_mod = jnp.concatenate([mod_gradient(late_came), mod_gradient(mod_came)], axis=-1)
    return (
        return_clip(result[:half_count], out_came, LOW),
        return_clip(grad_source[:half_count], in_came, WIDE),
        product[0], product[1], product[2],
        up_proj[:, FF:], up_proj[:, :FF], grad_down, grad_mod,
    )


def solution(mesh):
    frames, rows = mesh.shape["frames"], mesh.shape["rows"]
    clips = 2
    split = Mesh(
        mesh.devices.reshape(frames, clips, rows // clips), ("frames", "half", "side")
    )
    tokens = P("frames", None, ("half", "side"), None, None)
    shared = P(("frames", "half", "side"), None)
    return jax.shard_map(
        shards,
        mesh=split,
        in_specs=(tokens, P(), P("frames", None), P(), P(), P(), P(), P(), P(), P(), tokens),
        out_specs=(tokens, tokens) + (shared,) * 7,
        check_vma=False,
    )
```

```python
import functools
import math

import jax
import jax.numpy as jnp
import numpy as np
from jax import lax
from jax.experimental import pallas as pl
from jax.experimental.pallas import tpu as pltpu
from jax.sharding import Mesh, PartitionSpec as P

D = 1024
H = 16
HD = 64
FF = 4096
PR = 32
PC = 32

norm_eps = 1e-06
LOW = jnp.bfloat16
WIDE = jnp.float32
MIB = 2**20
SCALE2 = math.log2(math.e) / math.sqrt(HD)
SAFE_LOG2 = 100.0
FORWARD_GROUP = 4
BACKWARD_GROUP = 2
ROWS_ROWS = (((1,), (1,)), ((), ()))
ROWS_COLS = (((1,), (0,)), ((), ()))
SHIFT_ONE, SCALE_ONE, GATE_ONE, SHIFT_TWO, SCALE_TWO, GATE_TWO = range(6)


def dot(left, right, dims=ROWS_COLS):
    return lax.dot_general(left, right, dims, preferred_element_type=WIDE)


def exact_dot(left, right, dims=ROWS_COLS):
    return lax.dot_general(
        left, right, dims, preferred_element_type=WIDE, precision=lax.Precision.HIGHEST
    )


def vmem():
    return pl.BlockSpec(memory_space=pltpu.VMEM)


def smem():
    return pl.BlockSpec(memory_space=pltpu.SMEM)


def whole(shape):
    return pl.BlockSpec(shape, lambda *unused: (0,) * len(shape))


def behind(kernel, count):
    def ordered(*refs):
        return kernel(*refs[count:])

    return ordered


def anywhere(count):
    return [pl.BlockSpec(memory_space=pl.ANY)] * count


def column_sum(values):
    return jnp.sum(values, axis=0, keepdims=True)


def head_masks(rows, lanes, heads):
    lane = lax.broadcasted_iota(jnp.int32, (rows, lanes), 1)
    return [lane // HD == h for h in range(heads)]


def square_norm(values, masks):
    squared = values.astype(WIDE)
    squared = squared * squared
    return [
        jnp.max(jnp.sum(jnp.where(mask, squared, 0.0), axis=1, keepdims=True)) for mask in masks
    ]


def split_sources(refs, parts, own):
    trios, refs = refs[:parts], refs[parts:]
    if own:
        return trios, trios, refs
    return trios, refs[:parts], refs[parts:]


def joined(refs, slot, place):
    return jnp.concatenate([ref[slot, place] for ref in refs], axis=0)


def forward_kernel(order, flag_in, *refs, parts, own, first, last, heads):
    trios, pairs, refs = split_sources(refs, parts, own)
    frames, unused, few, lanes = trios[0].shape
    tokens = few * parts
    if not first:
        num_in, sum_in, top_in = refs[:3]
        refs = refs[3:]
    if last:
        attn_out, log_out = refs[:2]
        refs = refs[2:]
    else:
        flag_out, num_out, sum_out, top_out = refs[:4]
        refs = refs[4:]
    queries, keys, values, accs = refs
    group = accs.shape[1] // tokens
    masks = head_masks(tokens, lanes, heads)
    one = jnp.ones((tokens, lanes), LOW)
    zero = jnp.zeros((tokens, lanes), LOW)
    width = 2 * HD
    bound = jnp.float32(0.0)
    q_top = [jnp.float32(0.0)] * heads
    k_top = [jnp.float32(0.0)] * heads
    for t in range(frames):
        slot = order[t]
        k = joined(pairs, slot, 0)
        v = joined(pairs, slot, 1)
        queries[t] = joined(trios, slot, 2)
        q_top = [jnp.maximum(a, b) for a, b in zip(q_top, square_norm(queries[t], masks))]
        k_top = [jnp.maximum(a, b) for a, b in zip(k_top, square_norm(k, masks))]
        for h in range(heads):
            keys[h, t] = jnp.where(masks[h], k, zero)
            if heads == 2:
                values[h, t] = jnp.where(masks[h], v, one)
            else:
                values[h, t] = jnp.concatenate([v, one], axis=1)
    for a, b in zip(q_top, k_top):
        bound = jnp.maximum(bound, a * b)
    fast = bound * (SCALE2 * SCALE2) <= SAFE_LOG2 * SAFE_LOG2
    if not first:
        fast = jnp.logical_and(fast, flag_in[0] == 1)
    if not last:
        flag_out[0] = jnp.where(fast, 1, 0).astype(jnp.int32)
    low_lane = lax.broadcasted_iota(jnp.int32, (tokens, lanes), 1) < HD
    pick = lax.broadcasted_iota(jnp.int32, (8, lanes), 1) == HD * lax.broadcasted_iota(
        jnp.int32, (8, lanes), 0
    )
    pick = jnp.where(pick, 1.0, 0.0).astype(WIDE)

    def split(num, total):
        if heads == 2:
            turned = pltpu.roll(total, HD, 1)
            return [jnp.where(low_lane, num, turned), jnp.where(low_lane, turned, num)]
        return [jnp.concatenate([num, total], axis=1)]

    def join(accs):
        if heads == 2:
            num = jnp.where(low_lane, accs[0], accs[1])
            total = jnp.where(low_lane, accs[1], accs[0])
            return num, pltpu.roll(total, HD, 1)
        return accs[0][:, :HD], accs[0][:, HD:]

    def start(slot):
        if first:
            return [jnp.zeros((tokens, width), WIDE) for _ in range(heads)]
        return split(num_in[slot], sum_in[slot])

    def store(slot, accs, top):
        num, total = join(accs)
        if last:
            attn_out[slot] = (num / total).astype(LOW)
            logs = jnp.log2(total)
            if top is not None:
                logs = logs + top
            log_out[slot] = exact_dot(pick, logs, ROWS_ROWS)
        else:
            num_out[slot] = num
            sum_out[slot] = total
            top_out[slot] = jnp.zeros((tokens, lanes), WIDE) if top is None else top

    @pl.when(fast)
    def _():
        def outer(g, unused):
            base = g * group
            q = queries[pl.ds(base, group)].reshape(group * tokens, lanes)
            for i in range(group):
                for h, value in enumerate(start(order[base + i])):
                    accs[h, i * tokens : (i + 1) * tokens] = value

            def tile(j, skip):
                rows = slice(skip * tokens, group * tokens)
                for h in range(heads):
                    s = dot(q[rows], keys[h, j], ROWS_ROWS)
                    p = jnp.exp2(s * SCALE2).astype(LOW)
                    accs[h, rows] += dot(p, values[h, j])

            def inner(j, unused):
                tile(j, 0)
                return unused

            lax.fori_loop(0, base + 1, inner, 0)
            for skip in range(1, group):
                tile(base + skip, skip)
            for i in range(group):
                rows = slice(i * tokens, (i + 1) * tokens)
                store(order[base + i], [accs[h, rows] for h in range(heads)], None)
            return unused

        lax.fori_loop(0, frames // group, outer, 0)

    @pl.when(jnp.logical_not(fast))
    def _():
        def outer(t, unused):
            slot = order[t]
            q = queries[t]

            def inner(j, state):
                sums, tops = state
                new_accs, new_tops = [], []
                for h in range(heads):
                    s = dot(q, keys[h, j], ROWS_ROWS) * SCALE2
                    top = jnp.maximum(tops[h], jnp.max(s, axis=1, keepdims=True))
                    p = jnp.exp2(s - top).astype(LOW)
                    keep = jnp.exp2(tops[h] - top)
                    new_accs.append(sums[h] * keep + dot(p, values[h, j]))
                    new_tops.append(top)
                return new_accs, new_tops

            if first:
                tops = [jnp.full((tokens, 1), -1e30, WIDE)] * heads
            else:
                tops = [top_in[slot][:, h * HD : h * HD + 1] for h in range(heads)]
            sums, tops = lax.fori_loop(0, t + 1, inner, (start(slot), tops))
            top = jnp.broadcast_to(tops[0], (tokens, lanes))
            if heads == 2:
                top = jnp.where(low_lane, top, jnp.broadcast_to(tops[1], (tokens, lanes)))
            store(slot, sums, top)
            return unused

        lax.fori_loop(0, frames, outer, 0)


def attention_forward(order, state, trios, pairs, last, after):
    frames, unused, few, lanes = trios[0].shape
    parts, own = len(trios), pairs is None
    tokens = few * parts
    sources = tuple(trios) + (() if own else tuple(pairs))
    heads = lanes // HD
    first = state is None
    wide = jax.ShapeDtypeStruct((frames, tokens, lanes), WIDE)
    if last:
        out_shape = [
            jax.ShapeDtypeStruct((frames, tokens, lanes), LOW),
            jax.ShapeDtypeStruct((frames, 8, tokens), WIDE),
        ]
        out_specs = [vmem()] * 2
    else:
        out_shape = [jax.ShapeDtypeStruct((1,), jnp.int32), wide, wide, wide]
        out_specs = [smem()] + [vmem()] * 3
    flag = jnp.zeros((1,), jnp.int32) if first else state[0]
    rest = () if first else tuple(state[1:])
    work = heads * frames * (frames + 1) // 2 * tokens * tokens
    return pl.pallas_call(
        behind(
            functools.partial(
                forward_kernel, parts=parts, own=own, first=first, last=last, heads=heads
            ),
            len(after),
        ),
        out_shape=out_shape,
        in_specs=anywhere(len(after)) + [smem(), smem()]
        + [vmem()] * (len(sources) + len(rest)),
        out_specs=out_specs,
        scratch_shapes=[
            pltpu.VMEM((frames, tokens, lanes), LOW),
            pltpu.VMEM((heads, frames, tokens, lanes), LOW),
            pltpu.VMEM((heads, frames, tokens, max(lanes, 2 * HD)), LOW),
            pltpu.VMEM((heads, FORWARD_GROUP * tokens, max(lanes, 2 * HD)), WIDE),
        ],
        compiler_params=pltpu.CompilerParams(vmem_limit_bytes=56 * MIB),
        cost_estimate=pl.CostEstimate(
            flops=work * 4 * HD * 8, bytes_accessed=16 * MIB, transcendentals=work
        ),
        name="attention_forward",
    )(*after, order, flag, *sources, *rest)


def backward_kernel(
    order, grad, out, lse, *refs, parts, own, first, last, begin, end, came, heads
):
    trios, pairs, refs = split_sources(refs, parts, own)
    frames, tokens, lanes = grad.shape
    if not first:
        dq_in = refs[0]
        refs = refs[1:]
    if begin > 0:
        pair_in = refs[0]
        refs = refs[1:]
    if came:
        pair_came = refs[0]
        refs = refs[1:]
    if last:
        final, queries, grads, delta, logs, keys, values, key_turned, dk, dv, dq_sum = refs
        places = (1, 2)
    else:
        dq_sum, final, queries, grads, delta, logs, keys, values, key_turned, dk, dv = refs
        places = (0, 1)
    group = dk.shape[0] // tokens
    masks = head_masks(tokens, lanes, heads)
    zero = jnp.zeros((tokens, lanes), LOW)
    lane8 = lax.broadcasted_iota(jnp.int32, (8, lanes), 1) // HD
    pick = jnp.where(lane8 == lax.broadcasted_iota(jnp.int32, (8, lanes), 0), 1.0, 0.0)
    for t in range(frames):
        slot = order[t]
        q = joined(trios, slot, 2)
        g = grad[slot]
        k = joined(pairs, slot, 0)
        for h in range(heads):
            queries[h, t] = jnp.where(masks[h], q, zero)
            grads[h, t] = jnp.where(masks[h], g, zero)
        keys[t] = k
        values[t] = joined(pairs, slot, 1)
        key_turned[t // group, :, (t % group) * tokens : (t % group + 1) * tokens] = k.T
        logs[t] = lse[slot]
        delta[t] = exact_dot(
            pick.astype(WIDE), g.astype(WIDE) * out[slot].astype(WIDE), ROWS_ROWS
        )
        dq_sum[t] = jnp.zeros((lanes, tokens), WIDE) if first else dq_in[t]
        if begin > 0:
            for i in range(2):
                old = pair_in[t, i]
                if came:
                    old = (old.astype(WIDE) + pair_came[t, i].astype(WIDE)).astype(LOW)
                final[t, places[i]] = old
    group_masks = head_masks(group * tokens, lanes, heads)
    group_zero = jnp.zeros((group * tokens, lanes), LOW)

    def outer(index, unused):
        base = index * group
        k = keys[pl.ds(base, group)].reshape(group * tokens, lanes)
        v = values[pl.ds(base, group)].reshape(group * tokens, lanes)
        ks = [jnp.where(mask, k, group_zero) for mask in group_masks]
        vs = [jnp.where(mask, v, group_zero) for mask in group_masks]
        dk[...] = jnp.zeros(dk.shape, WIDE)
        dv[...] = jnp.zeros(dv.shape, WIDE)

        def tile(j, count):
            rows = slice(0, count * tokens)
            for h in range(heads):
                q = queries[h, j]
                g = grads[h, j]
                s = dot(ks[h][rows], q, ROWS_ROWS)
                p = jnp.exp2(s * SCALE2 - logs[j, h : h + 1, :])
                dp = dot(vs[h][rows], g, ROWS_ROWS)
                ds = (p * (dp - delta[j, h : h + 1, :])).astype(LOW)
                dv[rows] += dot(p.astype(LOW), g)
                dk[rows] += dot(ds, q)
                span = slice(h * HD, (h + 1) * HD)
                dq_sum[j, span, :] += dot(key_turned[index, span, rows], ds)

        def inner(j, unused):
            tile(j, group)
            return unused

        for count in range(1, group):
            tile(base + count - 1, count)
        lax.fori_loop(base + group - 1, frames, inner, 0)
        for i in range(group):
            rows = slice(i * tokens, (i + 1) * tokens)
            slot = order[base + i]
            part_k = dk[rows] * (1.0 / math.sqrt(HD))
            part_v = dv[rows]
            if came:
                part_k = part_k + pair_came[slot, 0].astype(WIDE)
                part_v = part_v + pair_came[slot, 1].astype(WIDE)
            final[slot, places[0]] = part_k.astype(LOW)
            final[slot, places[1]] = part_v.astype(LOW)
        return unused

    lax.fori_loop(begin // group, end // group, outer, 0)
    if last:
        for t in range(frames):
            final[order[t], 0] = (dq_sum[t].T * (1.0 / math.sqrt(HD))).astype(LOW)


def attention_backward(
    order, dq, partial, came, trios, pairs, grad, out, lse, begin, end, last, after
):
    frames, tokens, lanes = grad.shape
    parts, own = len(trios), pairs is None
    sources = tuple(trios) + (() if own else tuple(pairs))
    heads = lanes // HD
    first = dq is None
    sums = (frames, lanes, tokens)
    extra = tuple(
        array for array in (dq, partial if begin > 0 else None, came) if array is not None
    )
    steps = sum(frames - t for t in range(begin, end))
    work = heads * steps * tokens * tokens
    scratch = [
        pltpu.VMEM((heads, frames, tokens, lanes), LOW),
        pltpu.VMEM((heads, frames, tokens, lanes), LOW),
        pltpu.VMEM((frames, 8, tokens), WIDE),
        pltpu.VMEM((frames, 8, tokens), WIDE),
        pltpu.VMEM((frames, tokens, lanes), LOW),
        pltpu.VMEM((frames, tokens, lanes), LOW),
        pltpu.VMEM((frames // BACKWARD_GROUP, lanes, BACKWARD_GROUP * tokens), LOW),
        pltpu.VMEM((BACKWARD_GROUP * tokens, lanes), WIDE),
        pltpu.VMEM((BACKWARD_GROUP * tokens, lanes), WIDE),
    ]
    if last:
        out_shape = [jax.ShapeDtypeStruct((frames, 3, tokens, lanes), LOW)]
        scratch.append(pltpu.VMEM(sums, WIDE))
    else:
        out_shape = [
            jax.ShapeDtypeStruct(sums, WIDE), jax.ShapeDtypeStruct((frames, 2, tokens, lanes), LOW)
        ]
    return pl.pallas_call(
        behind(
            functools.partial(
                backward_kernel, parts=parts, own=own, first=first, last=last, begin=begin,
                end=end, came=came is not None, heads=heads,
            ),
            len(after),
        ),
        out_shape=out_shape,
        in_specs=anywhere(len(after)) + [smem()]
        + [vmem()] * (3 + len(sources) + len(extra)),
        out_specs=[vmem()] * len(out_shape),
        scratch_shapes=scratch,
        compiler_params=pltpu.CompilerParams(vmem_limit_bytes=56 * MIB),
        cost_estimate=pl.CostEstimate(
            flops=work * 10 * HD * 5, bytes_accessed=16 * MIB, transcendentals=work
        ),
        name="attention_backward",
    )(*after, order, grad, out, lse, *sources, *extra)


def normalize(values):
    centered = values - jnp.mean(values, axis=-1, keepdims=True)
    inverse = lax.rsqrt(jnp.mean(centered * centered, axis=-1, keepdims=True) + norm_eps)
    return (centered * inverse, inverse)


def norm_backward(grad_normed, normed, inverse):
    mean_grad = jnp.mean(grad_normed, axis=-1, keepdims=True)
    mean_prod = jnp.mean(grad_normed * normed, axis=-1, keepdims=True)
    return inverse * (grad_normed - mean_grad - normed * mean_prod)


def part(mod, index):
    return mod[0:1, index * D : (index + 1) * D]


def swap_halves(values):
    lanes = values.shape[1]
    lane = lax.broadcasted_iota(jnp.int32, values.shape, 1) % HD
    eight, twelve = HD // 8, 3 * HD // 16
    quarter, last = HD // 4, HD // 4 + 2 * twelve

    def ahead(step):
        return pltpu.roll(values, lanes - step, 1)

    def behind(step):
        return pltpu.roll(values, step, 1)

    first_half = ((lane >= quarter) & (lane < quarter + twelve)) | (
        (lane >= last) & (lane < last + twelve)
    )
    short = jnp.where(lane < eight, ahead(eight), behind(eight))
    long = jnp.where(first_half, ahead(twelve), behind(twelve))
    return jnp.where(lane < quarter, short, long)


def turned(values, cosine, sine):
    wide = cosine.shape[1]
    pieces = []
    for at in range(0, values.shape[1], wide):
        block = values[:, at : at + wide]
        pieces.append(block * cosine + swap_halves(block) * sine)
    return pieces[0] if len(pieces) == 1 else jnp.concatenate(pieces, axis=1)


def input_kernel(tokens, mod, w_query, w_key, w_value, cosine, sine, hidden, trio):
    @pl.when(pl.program_id(0) == 0)
    def _():
        normed, unused = normalize(tokens[...].astype(WIDE))
        hidden[...] = (normed * (1.0 + part(mod, SCALE_ONE)) + part(mod, SHIFT_ONE)).astype(LOW)

    groups, unused, unused, lanes = trio.shape
    h = hidden[...]
    cos, sin = cosine[...], sine[...]
    k = turned(dot(h, w_key[...]), cos, sin).astype(LOW)
    v = dot(h, w_value[...]).astype(LOW)
    q = turned(dot(h, w_query[...]), cos, sin).astype(LOW)
    for g in range(groups):
        span = slice(g * lanes, (g + 1) * lanes)
        trio[g, 0] = k[:, span]
        trio[g, 1] = v[:, span]
        trio[g, 2] = q[:, span]


def input_projections(tokens, mod, w_query, w_key, w_value, cosine, sine, frames):
    count = tokens.shape[0]
    lanes = D // frames
    wide = 256
    groups = wide // lanes
    weight = pl.BlockSpec((D, wide), lambda c: (0, c))
    trio = pl.BlockSpec((groups, 3, count, lanes), lambda c: (c, 0, 0, 0))
    return pl.pallas_call(
        input_kernel,
        grid=(D // wide,),
        out_shape=[
            jax.ShapeDtypeStruct((count, D), LOW),
            jax.ShapeDtypeStruct((frames, 3, count, lanes), LOW),
        ],
        in_specs=[whole((count, D)), whole((1, 6 * D)), weight, weight, weight]
        + [whole(cosine.shape)] * 2,
        out_specs=[whole((count, D)), trio],
        compiler_params=pltpu.CompilerParams(vmem_limit_bytes=48 * MIB),
        cost_estimate=pl.CostEstimate(
            flops=6 * count * D * D, bytes_accessed=12 * MIB, transcendentals=0
        ),
        name="input_projections",
    )(tokens, mod, w_query, w_key, w_value, cosine, sine)


def pull_kernel(cotangent, mod, w_down, pulled, scaled_turned, scaled):
    @pl.when(pl.program_id(0) == 0)
    def _():
        scaled[...] = (part(mod, GATE_TWO) * cotangent[...].astype(WIDE)).astype(LOW)
        scaled_turned[...] = scaled[...].T

    pulled[...] = dot(scaled[...], w_down[...], ROWS_ROWS).astype(LOW)


def pull_down(cotangent, mod, w_down):
    count = cotangent.shape[0]
    wide = 512
    return pl.pallas_call(
        pull_kernel,
        grid=(FF // wide,),
        out_shape=[
            jax.ShapeDtypeStruct((count, FF), LOW), jax.ShapeDtypeStruct((D, count), LOW)
        ],
        in_specs=[
            whole((count, D)), whole((1, 6 * D)), pl.BlockSpec((wide, D), lambda c: (c, 0))
        ],
        out_specs=[pl.BlockSpec((count, wide), lambda c: (0, c)), whole((D, count))],
        scratch_shapes=[pltpu.VMEM((count, D), LOW)],
        compiler_params=pltpu.CompilerParams(vmem_limit_bytes=32 * MIB),
        cost_estimate=pl.CostEstimate(
            flops=2 * count * D * FF, bytes_accessed=14 * MIB, transcendentals=0
        ),
        name="pull_down",
    )(cotangent, mod, w_down)


def middle_kernel(
    attn, tokens, cotangent, mod, w_proj, w_up, pulled,
    middle, hidden, active, grad_up_in, grad_middle, grad_branch, grad_attn,
    grad_gate, grad_shift, grad_scale, branch, normed, inverse, total
):
    step = pl.program_id(0)
    frames, count, lanes = attn.shape

    @pl.when(step == 0)
    def _():
        for f in range(frames):
            hidden[:, f * lanes : (f + 1) * lanes] = attn[f]
        product = dot(hidden[...], w_proj[...])
        branch[...] = product
        mid = tokens[...].astype(WIDE) + part(mod, GATE_ONE) * product
        middle[...] = mid
        n, inv = normalize(mid)
        normed[...] = n
        inverse[...] = inv
        hidden[...] = (n * (1.0 + part(mod, SCALE_TWO)) + part(mod, SHIFT_TWO)).astype(LOW)
        total[...] = jnp.zeros(total.shape, WIDE)

    weight = w_up[...]
    u = dot(hidden[...], weight)
    rate = math.sqrt(2.0 / math.pi)
    square = u * u
    bend = jnp.tanh(rate * (u + 0.044715 * (u * square)))
    half = 0.5 * (1.0 + bend)
    active[...] = (u * half).astype(LOW)
    slope = half + (0.5 * rate) * u * (1.0 - bend * bend) * (1.0 + (3 * 0.044715) * square)
    du = (pulled[...].astype(WIDE) * slope).astype(LOW)
    grad_up_in[...] = du
    total[...] += dot(du, weight, ROWS_ROWS)

    @pl.when(step == pl.num_programs(0) - 1)
    def _():
        dh = total[...]
        n = normed[...]
        grad_scale[...] = column_sum(dh * n)
        grad_shift[...] = column_sum(dh)
        dx = cotangent[...].astype(WIDE) + norm_backward(
            dh * (1.0 + part(mod, SCALE_TWO)), n, inverse[...]
        )
        grad_middle[...] = dx
        grad_gate[...] = column_sum(dx * branch[...])
        dy = (part(mod, GATE_ONE) * dx).astype(LOW)
        grad_branch[...] = dy
        back = dot(dy, w_proj[...], ROWS_ROWS).astype(LOW)
        for f in range(frames):
            grad_attn[f] = back[:, f * lanes : (f + 1) * lanes]


def middle_block(attn, tokens, cotangent, mod, w_proj, w_up, pulled):
    frames, count, lanes = attn.shape
    wide = 512
    flat = whole((count, D))
    row = whole((1, D))
    columns = pl.BlockSpec((count, wide), lambda c: (0, c))
    heads = whole(attn.shape)

    def of(shape, kind):
        return jax.ShapeDtypeStruct(shape, kind)

    return pl.pallas_call(
        middle_kernel,
        grid=(FF // wide,),
        out_shape=[
            of((count, D), WIDE), of((count, D), LOW), of((count, FF), LOW), of((count, FF), LOW),
            of((count, D), WIDE), of((count, D), LOW), of(attn.shape, LOW),
            of((1, D), WIDE), of((1, D), WIDE), of((1, D), WIDE),
        ],
        in_specs=[
            heads, flat, flat, whole((1, 6 * D)), whole((D, D)),
            pl.BlockSpec((D, wide), lambda c: (0, c)), columns,
        ],
        out_specs=[flat, flat, columns, columns, flat, flat, heads, row, row, row],
        scratch_shapes=[
            pltpu.VMEM((count, D), WIDE), pltpu.VMEM((count, D), WIDE),
            pltpu.VMEM((count, 1), WIDE), pltpu.VMEM((count, D), WIDE),
        ],
        compiler_params=pltpu.CompilerParams(vmem_limit_bytes=56 * MIB),
        cost_estimate=pl.CostEstimate(
            flops=2 * count * D * (2 * FF + 2 * D), bytes_accessed=30 * MIB,
            transcendentals=count * FF,
        ),
        name="middle_block",
    )(attn, tokens, cotangent, mod, w_proj, w_up, pulled)


def weights_kernel(
    slot, active, grad_up_in, hidden, scaled_turned, attn, grad_branch, *refs, keep
):
    step = pl.program_id(0)
    frames, count, lanes = attn.shape
    half = frames // 2
    wide = D // frames
    if keep:
        activity, middle, cotangent, mod, w_down = refs[:5]
        out, grad_gate, down_out, up_out, hidden_turned, attn_turned, flat, total = refs[5:]
    else:
        down_out, up_out, hidden_turned, attn_turned, flat = refs
    chunks, narrow = down_out.shape[1], down_out.shape[3]

    @pl.when(step == 0)
    def _():
        for f in range(frames):
            flat[:, f * lanes : (f + 1) * lanes] = attn[f]
        for f in range(frames):
            place = lax.bitwise_xor(f, slot[0])

            @pl.when(place % 2 == (0 if keep else 1))
            def _():
                span = slice(f * wide, (f + 1) * wide)
                hidden_turned[place // 2] = hidden[:, span].T
                attn_turned[place // 2] = flat[:, span].T

        if keep:
            total[...] = jnp.zeros(total.shape, WIDE)

    @pl.when(step < half)
    def _():
        if keep:
            total[...] += dot(activity[...], w_down[...])
        down = dot(scaled_turned[...], active[...]).astype(LOW)
        for r in range(chunks):
            down_out[0, r] = down[:, r * narrow : (r + 1) * narrow]
        up = dot(hidden_turned[...].reshape(D // 2, count), grad_up_in[...]).astype(LOW)
        up_out[...] = up.reshape(half, wide, up.shape[1])

    @pl.when(step >= half)
    def _():
        proj = dot(attn_turned[...].reshape(D // 2, count), grad_branch[...]).astype(LOW)
        up_out[...] = proj.reshape(half, wide, proj.shape[1])

    if keep:
        @pl.when(step == half - 1)
        def _():
            z = total[...]
            out[...] = (middle[...] + part(mod, GATE_TWO) * z).astype(LOW)
            grad_gate[...] = column_sum(cotangent[...].astype(WIDE) * z)


def weight_gradients(
    slot, active, grad_up_in, hidden, scaled_turned, attn, grad_branch, rows, finish
):
    frames, count, lanes = attn.shape
    keep = finish is not None
    half = frames // 2
    narrow = FF // frames
    wide = FF // half
    extra = D // wide

    def down_block(i, slot):
        place = 2 * jnp.minimum(i, half - 1) + (0 if keep else 1)
        return lax.bitwise_xor(place, slot[0])

    def up_block(i, slot):
        return jnp.minimum(i, half - 1)

    flat = whole((count, D))
    down = (1, rows, D, narrow // rows)
    in_specs = [
        pl.BlockSpec((count, narrow), lambda i, slot: (0, down_block(i, slot))),
        pl.BlockSpec((count, wide), lambda i, slot: (0, up_block(i, slot))),
        flat, whole((D, count)), whole(attn.shape),
        pl.BlockSpec((count, wide), lambda i, slot: (0, jnp.maximum(i - half, 0))),
    ]
    out_specs = [
        pl.BlockSpec(down, lambda i, slot: (jnp.minimum(i, half - 1), 0, 0, 0)),
        pl.BlockSpec((half, D // frames, wide), lambda i, slot: (0, 0, i)),
    ]
    out_shape = [
        jax.ShapeDtypeStruct((half, rows, D, narrow // rows), LOW),
        jax.ShapeDtypeStruct((half, D // frames, FF + D), LOW),
    ]
    scratch = [
        pltpu.VMEM((half, D // frames, count), LOW), pltpu.VMEM((half, D // frames, count), LOW),
        pltpu.VMEM((count, D), LOW),
    ]
    args = (slot, active, grad_up_in, hidden, scaled_turned, attn, grad_branch)
    if keep:
        args += (active,) + tuple(finish)
        in_specs += [
            pl.BlockSpec((count, wide), lambda i, slot: (0, up_block(i, slot))),
            flat, flat, whole((1, 6 * D)),
            pl.BlockSpec((wide, D), lambda i, slot: (up_block(i, slot), 0)),
        ]
        out_specs = [flat, whole((1, D))] + out_specs
        out_shape = [
            jax.ShapeDtypeStruct((count, D), LOW), jax.ShapeDtypeStruct((1, D), WIDE)
        ] + out_shape
        scratch.append(pltpu.VMEM((count, D), WIDE))
    return pl.pallas_call(
        functools.partial(weights_kernel, keep=keep),
        grid_spec=pltpu.PrefetchScalarGridSpec(
            num_scalar_prefetch=1, grid=(half + extra,),
            in_specs=in_specs, out_specs=out_specs, scratch_shapes=scratch,
        ),
        out_shape=out_shape,
        compiler_params=pltpu.CompilerParams(vmem_limit_bytes=56 * MIB),
        cost_estimate=pl.CostEstimate(
            flops=count * D * (2 * FF + D + (2 * FF if keep else 0)), bytes_accessed=24 * MIB,
            transcendentals=0,
        ),
        name="weight_gradients",
    )(*args)


def turn_kernel(*refs):
    *parts, target = refs
    target[...] = jnp.concatenate([part[...] for part in parts], axis=0).T


def turn_hidden(parts):
    count = sum(part.shape[0] for part in parts)
    return pl.pallas_call(
        turn_kernel,
        out_shape=jax.ShapeDtypeStruct((D, count), LOW),
        in_specs=[vmem()] * len(parts),
        out_specs=vmem(),
        compiler_params=pltpu.CompilerParams(vmem_limit_bytes=32 * MIB),
        cost_estimate=pl.CostEstimate(flops=0, bytes_accessed=2 * MIB, transcendentals=0),
        name="turn_hidden",
    )(*parts)


def head_kernel(grads, hidden, cosine, sine, time_cosine, time_sine, product, total):
    step = pl.program_id(0)

    @pl.when(step == 0)
    def _():
        total[...] = jnp.zeros(total.shape, WIDE)

    cos = cosine[...] + time_cosine[0]
    sin = -(sine[...] + time_sine[0])
    block = jnp.concatenate(
        [turned(grads[0, i].astype(WIDE), cos, sin).astype(LOW) for i in range(2)] + [grads[0, 2]],
        axis=1,
    )
    total[...] += dot(hidden[0], block)

    @pl.when(step == pl.num_programs(0) - 1)
    def _():
        product[...] = total[...].astype(LOW)


def head_gradients(grads, hidden_all, tables, after):
    frames, unused, count, lanes = grads.shape
    frame = pl.BlockSpec((1, 1, lanes), lambda f: (f, 0, 0))
    return pl.pallas_call(
        behind(head_kernel, len(after)),
        grid=(frames,),
        out_shape=jax.ShapeDtypeStruct((D, 3 * lanes), LOW),
        in_specs=anywhere(len(after)) + [
            pl.BlockSpec((1, 3, count, lanes), lambda f: (f, 0, 0, 0)),
            pl.BlockSpec((1, D, count), lambda f: (f, 0, 0)),
            whole((count, lanes)), whole((count, lanes)), frame, frame,
        ],
        out_specs=whole((D, 3 * lanes)),
        scratch_shapes=[pltpu.VMEM((D, 3 * lanes), WIDE)],
        compiler_params=pltpu.CompilerParams(vmem_limit_bytes=32 * MIB),
        cost_estimate=pl.CostEstimate(
            flops=6 * frames * count * D * lanes, bytes_accessed=12 * MIB, transcendentals=0
        ),
        name="head_gradients",
    )(*after, grads, hidden_all, *tables)


def output_kernel(
    grads, w_query, w_key, w_value, cosine, sine, tokens, mod, grad_middle,
    grad_tokens, grad_shift, grad_scale, total
):
    step = pl.program_id(0)
    groups = grads.shape[0]

    @pl.when(step == 0)
    def _():
        total[...] = jnp.zeros(total.shape, WIDE)

    dh = total[...]
    for i, weight in enumerate((w_query, w_key, w_value)):
        block = jnp.concatenate([grads[g, i] for g in range(groups)], axis=1)
        if i < 2:
            block = turned(block.astype(WIDE), cosine[...], -sine[...]).astype(LOW)
        dh = dh + dot(block, weight[...], ROWS_ROWS)
    total[...] = dh

    @pl.when(step == pl.num_programs(0) - 1)
    def _():
        dh = total[...]
        n, inverse = normalize(tokens[...].astype(WIDE))
        grad_scale[...] = column_sum(dh * n)
        grad_shift[...] = column_sum(dh)
        grad_tokens[...] = (
            grad_middle[...] + norm_backward(dh * (1.0 + part(mod, SCALE_ONE)), n, inverse)
        ).astype(LOW)


def input_gradients(grads, w_query, w_key, w_value, cosine, sine, tokens, mod, grad_middle, after):
    frames, unused, count, lanes = grads.shape
    wide = 256
    groups = wide // lanes
    flat = whole((count, D))
    row = whole((1, D))
    weight = pl.BlockSpec((D, wide), lambda c: (0, c))
    rows = jax.ShapeDtypeStruct((1, D), WIDE)
    return pl.pallas_call(
        behind(output_kernel, len(after)),
        grid=(D // wide,),
        out_shape=[jax.ShapeDtypeStruct((count, D), LOW), rows, rows],
        in_specs=anywhere(len(after)) + [
            pl.BlockSpec((groups, 3, count, lanes), lambda c: (c, 0, 0, 0)),
            weight, weight, weight, whole(cosine.shape), whole(sine.shape),
            flat, whole((1, 6 * D)), flat,
        ],
        out_specs=[flat, row, row],
        scratch_shapes=[pltpu.VMEM((count, D), WIDE)],
        compiler_params=pltpu.CompilerParams(vmem_limit_bytes=48 * MIB),
        cost_estimate=pl.CostEstimate(
            flops=6 * count * D * D, bytes_accessed=14 * MIB, transcendentals=0
        ),
        name="input_gradients",
    )(*after, grads, w_query, w_key, w_value, cosine, sine, tokens, mod, grad_middle)


def halves_kernel(mine, keep_give, came_give, keep_hold, came_hold, give, hold):
    give[0] = (keep_give[0, 0].astype(WIDE) + came_give[0, 0].astype(WIDE)).astype(LOW)
    hold[0] = (keep_hold[0, 0].astype(WIDE) + came_hold[0, 0].astype(WIDE)).astype(LOW)


def add_halves(keep, came, axis, mine, after):
    shape = keep.shape
    lead, trail = math.prod(shape[:axis]), math.prod(shape[axis + 1 : -2])
    rest = shape[:axis] + shape[axis + 1 :]
    many = 2 if trail % 2 == 0 else 1
    block = (1, 1, many) + shape[-2:]
    view = (lead, 2, trail) + shape[-2:]

    def part_of(other):
        def index(a, b, mine, *unused):
            return (a, 1 - mine[0] if other else mine[0], b, 0, 0)

        return pl.BlockSpec(block, index)

    out = pl.BlockSpec((1, many) + shape[-2:], lambda a, b, *unused: (a, b, 0, 0))
    out_shape = jax.ShapeDtypeStruct((lead, trail) + shape[-2:], LOW)

    def ordered(mine, *refs):
        halves_kernel(mine, *refs[len(after) :])

    keep, came = keep.reshape(view), came.reshape(view)
    give, hold = pl.pallas_call(
        ordered,
        grid_spec=pltpu.PrefetchScalarGridSpec(
            num_scalar_prefetch=1,
            grid=(lead, trail // many),
            in_specs=anywhere(len(after)) + [part_of(True)] * 2 + [part_of(False)] * 2,
            out_specs=[out, out],
        ),
        out_shape=[out_shape, out_shape],
        cost_estimate=pl.CostEstimate(
            flops=keep.size, bytes_accessed=6 * keep.size, transcendentals=0
        ),
        name="add_halves",
    )(mine, *after, keep, came, keep, came)
    return give.reshape(rest), hold.reshape(rest)


def total_kernel(keep, came, total):
    total[...] = keep[...].astype(WIDE) + came[...].astype(WIDE)


def add_last(keep, came, after):
    return pl.pallas_call(
        behind(total_kernel, len(after)),
        out_shape=jax.ShapeDtypeStruct(keep.shape, WIDE),
        in_specs=anywhere(len(after)) + [vmem()] * 2,
        out_specs=vmem(),
        name="add_last",
    )(*after, keep, came)


def same_kernel(*unused):
    pass


def order_after(array, after):
    return pl.pallas_call(
        same_kernel,
        out_shape=jax.ShapeDtypeStruct(array.shape, array.dtype),
        in_specs=anywhere(len(after) + 1),
        out_specs=anywhere(1)[0],
        input_output_aliases={len(after): 0},
        name="order_after",
    )(*after, array)


def pack_kernel(*refs):
    *vectors, codes, packed = refs
    at = 0
    for vector in vectors:
        packed[:, at : at + D] = jnp.broadcast_to(vector[...], (packed.shape[0], D))
        at += D
    packed[:, at:] = codes[...]


def pack(vectors, codes, after):
    return pl.pallas_call(
        behind(pack_kernel, len(after)),
        out_shape=jax.ShapeDtypeStruct((codes.shape[0], len(vectors) * D + codes.shape[1]), WIDE),
        in_specs=anywhere(len(after)) + [vmem()] * (len(vectors) + 1),
        out_specs=vmem(),
        name="pack",
    )(*after, *vectors, codes)


def rotary_rates(lanes):
    rates, parts, signs = [], [], []
    for index, size in enumerate((HD // 4, 3 * HD // 8, 3 * HD // 8)):
        half = size // 2
        rate = 10000.0 ** (-np.arange(half, dtype=np.float32) / np.float32(half))
        rates += [rate, rate]
        parts += [np.full(size, index)]
        signs += [-np.ones(half), np.ones(half)]
    rows = [np.concatenate(rows).astype(np.float32) for rows in (rates, parts, signs)]
    return np.tile(np.stack(rows), (1, lanes // HD))


def tables_kernel(places, times, rates, place_cosine, place_sine, time_cosine, time_sine, cosine, sine, *, local):
    count, lanes = cosine.shape
    frames = time_cosine.shape[0]
    rate, parts, sign = rates[0:1], rates[1:2], rates[2:3]
    token = lax.broadcasted_iota(jnp.int32, (count, lanes), 0)
    few = local * PC
    row = jnp.where(token < few, places[0], places[1] - local) + token // PC
    spot = jnp.where(parts == 1.0, row, token % PC).astype(WIDE)
    timed = parts == 0.0
    cos = jnp.where(timed, 0.0, jnp.cos(spot * rate))
    sin = jnp.where(timed, 0.0, jnp.sin(spot * rate) * sign)
    place_cosine[...] = cos
    place_sine[...] = sin
    for f in range(frames):
        angle = times[f].astype(WIDE) * rate
        time_cosine[f] = jnp.where(timed, jnp.cos(angle), 0.0)
        time_sine[f] = jnp.where(timed, jnp.sin(angle) * sign, 0.0)
    cosine[...] = cos + time_cosine[places[2]]
    sine[...] = sin + time_sine[places[2]]


def rotary_tables(places, times, count, local, lanes):
    flat = jax.ShapeDtypeStruct((count, lanes), WIDE)
    timed = jax.ShapeDtypeStruct((times.shape[0], 1, lanes), WIDE)
    return pl.pallas_call(
        functools.partial(tables_kernel, local=local),
        out_shape=[flat, flat, timed, timed, flat, flat],
        in_specs=[smem(), smem(), vmem()],
        out_specs=[vmem()] * 6,
        name="rotary_tables",
    )(places, times, jnp.asarray(rotary_rates(lanes)))


def sinusoid(levels):
    half_size = D // 2
    freq_table = 10000.0 ** (-jnp.arange(half_size, dtype=WIDE) / half_size)
    angle_table = levels.astype(WIDE)[..., None] * freq_table
    return jnp.concatenate([jnp.cos(angle_table), jnp.sin(angle_table)], axis=-1)


def shards(
    block_in, block_map, noise_level, w_query, w_key, w_value, w_proj, w_up, w_down, w_mod, cotangent
):
    frames = lax.axis_size("frames")
    sides = lax.axis_size("side")
    row_total = lax.axis_size("half") * sides
    frame_slot = lax.axis_index("frames")
    half = lax.axis_index("half")
    side = lax.axis_index("side")
    across = ("half", "side")
    everyone = ("frames",) + across
    devices = frames * row_total
    clips = block_in.shape[1]
    local_rows = block_in.shape[2]
    lanes = D // frames
    order = jnp.argsort(block_map).astype(jnp.int32)
    slot = frame_slot.astype(jnp.int32).reshape(1)

    def clip_tokens(tokens, clip):
        return lax.dynamic_index_in_dim(tokens[0], clip, 0, keepdims=False).reshape(-1, D)

    def other_half(array):
        return lax.ppermute(array, "half", [(0, 1), (1, 0)])

    def return_clip(own, came, kind):
        first = jnp.where(half == 0, own, came).astype(kind)
        second = jnp.where(half == 0, came, own).astype(kind)
        return jnp.stack([first, second]).reshape(1, clips, local_rows, PC, D)

    def swap_groups(grouped):
        return lax.all_to_all(grouped, "frames", split_axis=0, concat_axis=0, tiled=True)

    def pass_on(array, step):
        return lax.ppermute(array, "side", [(i, (i + step) % sides) for i in range(sides)])

    def flip(array, bit):
        return lax.ppermute(array, "frames", [(i, i ^ (1 << bit)) for i in range(frames)])

    def add(left, right):
        return (left.astype(WIDE) + right.astype(WIDE)).astype(LOW)

    class Reduction:
        def __init__(self, send, bits):
            self.came = flip(send, 0)
            self.bits = list(bits)
            self.left = sorted(bits, reverse=True)
            self.row_bits = [("side", bit) for bit in range(sides.bit_length() - 1)] + [("half", 0)]
            self.row_left = [("half", 0)] + self.row_bits[:-1][::-1]
            self.going = None

        def start(self, keep):
            rest = (row_total, -1) + keep.shape[-1:]
            self.shape = (2,) * (len(self.left) + len(self.row_left))
            self.keep = keep.reshape(self.shape + rest[1:])

        def advance(self, after=()):
            came = self.came.reshape(self.keep.shape)
            if self.bits:
                bit = self.bits.pop(0)
                axis = self.left.index(bit)
                self.left.remove(bit)
                name, mine = "frames", 0
            else:
                name, bit = self.row_bits.pop(0)
                axis = self.row_left.index((name, bit))
                self.row_left.remove((name, bit))
                mine = (lax.axis_index(name) >> bit) & 1

            mine = jnp.asarray(mine, jnp.int32).reshape(1)
            self.going, self.keep = add_halves(self.keep, came, axis, mine, after)
            size = lax.axis_size(name)
            self.came = lax.ppermute(self.going, name, [(i, i ^ (1 << bit)) for i in range(size)])

        def finish(self, after):
            while self.bits or self.row_bits:
                self.advance(after)
            return add_last(self.keep, self.came, after)

    high_bits = list(range(1, frames.bit_length() - 1))

    source_own = clip_tokens(block_in, half)
    source_came = other_half(clip_tokens(block_in, 1 - half))
    source = jnp.concatenate([source_own, source_came])
    half_count = source_own.shape[0]

    level = jnp.where(half == 0, noise_level[:, 0], noise_level[:, -1])
    embed = jax.nn.silu(sinusoid(level)).astype(LOW)
    mod = jnp.dot(embed, w_mod, preferred_element_type=WIDE)

    places = jnp.stack(
        [(half * sides + side) * local_rows, ((1 - half) * sides + side) * local_rows, frame_slot]
    ).astype(jnp.int32)
    tables = rotary_tables(places, block_map, 2 * half_count, local_rows, max(lanes, HD))
    cosine, sine = tables[4:]
    tables = tables[:4]

    hidden, trios = [], []
    for at, tokens in ((0, source_own), (half_count, source_came)):
        rows = slice(at, at + half_count)
        h, trio = input_projections(
            tokens, mod, w_query, w_key, w_value, cosine[rows], sine[rows], frames
        )
        hidden.append(h)
        trios.append(swap_groups(order_after(trio, (source_came,)) if at == 0 else trio))
    hidden_all = lax.all_gather(turn_hidden(hidden), "frames", axis=0)
    pairs = [None] + [
        [pass_on(trio[:, :2], step) for trio in trios] for step in range(1, sides)
    ]
    state = None
    passed = tuple(trios) if sides == 1 else tuple(pairs[-1])
    grad_came = other_half(order_after(clip_tokens(cotangent, 1 - half), passed))
    grad_result = jnp.concatenate([clip_tokens(cotangent, half), grad_came])
    pulled, scaled_turned = pull_down(grad_result, mod, w_down)
    for step in range(sides):
        state = attention_forward(order, state, trios, pairs[step], step == sides - 1, ())
    attn_heads, log_total = state
    attn = swap_groups(attn_heads)

    (
        middle, hidden_two, active, grad_up_in, grad_middle, grad_branch, grad_attn,
        grad_gate_one, grad_shift_two, grad_scale_two,
    ) = middle_block(attn, source, grad_result, mod, w_proj, w_up, pulled)
    grad_attn = swap_groups(grad_attn)
    inputs = (slot, active, grad_up_in, hidden_two, scaled_turned, attn, grad_branch, row_total)
    down_send, up_send = weight_gradients(*inputs, None)
    down = Reduction(down_send, high_bits)
    up = Reduction(up_send, high_bits[::-1])
    result, grad_gate_two, down_keep, up_keep = weight_gradients(
        *inputs, (middle, grad_result, mod, w_down)
    )
    down.start(down_keep)
    up.start(up_keep)

    def spread(vectors, after):
        packed = pack(vectors, codes, after)
        return lax.all_to_all(packed, everyone, split_axis=0, concat_axis=0, tiled=True)

    def mod_gradient(codes, vectors):
        return lax.dot_general(
            codes, vectors, (((0,), (0,)), ((), ())), precision=lax.Precision.HIGHEST
        )

    codes = embed.astype(WIDE).reshape(devices, D // devices)
    dq = None
    arrived = []
    cut = max(frames // 4 // BACKWARD_GROUP, 1) * BACKWARD_GROUP
    calls = [(step, span) for step in range(sides - 1, -1, -1) for span in (0, 1)]
    for index, (step, span) in enumerate(calls):
        after = ()
        if index == 0:
            down.advance()
            up.advance()
            after = (down.going, up.going)
            out_came = other_half(result[half_count:])
        elif index == 1:
            mod_came = spread(
                [grad_gate_one, grad_shift_two, grad_scale_two, grad_gate_two], (dq, partial)
            )
        elif index == 2:
            down.advance((dq,))
            up.advance((dq,))
            after = (down.going, up.going, mod_came, out_came)
        elif index == 3:
            down.advance((dq,))
            up.advance((dq,))
            after = (down.going, up.going)
        begin, end = ((0, cut), (cut, frames))[span]
        last = index == len(calls) - 1
        came = None
        if last and arrived:
            came = arrived[0]
            for more in arrived[1:]:
                came = add(came, more)
        answer = attention_backward(
            order, dq, None if span == 0 else partial, came, trios, pairs[step], grad_attn,
            attn_heads, log_total, begin, end, last, after,
        )
        if last:
            grads = answer[0]
        else:
            dq, partial = answer
            if span == 1:
                arrived.append(pass_on(partial, -step))
    grads = order_after(grads, (down.came, up.came))
    grads_back = swap_groups(grads)
    down.advance((grads,))
    up.advance((grads,))
    head_product = head_gradients(grads, hidden_all, tables, (down.going, up.going))
    head_product = order_after(head_product, (grads_back, down.came, up.came))
    product = lax.all_to_all(
        head_product.reshape(devices, D // devices, 3 * lanes),
        everyone, split_axis=0, concat_axis=0, tiled=True,
    )
    grad_source, grad_shift_one, grad_scale_one = input_gradients(
        grads_back, w_query, w_key, w_value, cosine, sine, source, mod, grad_middle,
        (head_product,),
    )
    in_came = other_half(grad_source[half_count:])
    total = jnp.sum(
        product.reshape(frames, row_total, D // devices, 3, lanes).astype(WIDE), axis=1
    )
    total = jnp.transpose(total, (2, 1, 0, 3)).reshape(3, D // devices, D)
    late = jnp.concatenate([grad_shift_one, grad_scale_one], axis=-1).reshape(1, -1, 128)
    late = jnp.broadcast_to(late, (devices,) + late.shape[1:])
    late_came = lax.all_to_all(order_after(late, (product,)), everyone, split_axis=0, concat_axis=0, tiled=True)
    all_codes = mod_came[:, 4 * D :]

    grad_down = down.finish((grad_source,)).reshape(D, FF // devices).T
    up_proj = up.finish((grad_source,)).reshape(D // devices, FF + D)
    grad_mod = jnp.concatenate(
        [
            mod_gradient(all_codes, late_came.reshape(devices, 2 * D)),
            mod_gradient(all_codes, mod_came[:, : 4 * D]),
        ],
        axis=-1,
    )
    return (
        return_clip(result[:half_count], out_came, LOW),
        return_clip(grad_source[:half_count], in_came, WIDE),
        total[0], total[1], total[2],
        up_proj[:, FF:], up_proj[:, :FF], grad_down, grad_mod,
    )


def solution(mesh):
    frames, rows = mesh.shape["frames"], mesh.shape["rows"]
    clips = 2
    split = Mesh(
        mesh.devices.reshape(frames, clips, rows // clips), ("frames", "half", "side")
    )
    tokens = P("frames", None, ("half", "side"), None, None)
    shared = P(("frames", "half", "side"), None)
    return jax.shard_map(
        shards,
        mesh=split,
        in_specs=(tokens, P(), P("frames", None), P(), P(), P(), P(), P(), P(), P(), tokens),
        out_specs=(tokens, tokens) + (shared,) * 7,
        check_vma=False,
    )
```

```python
import functools
import math

import jax
import jax.numpy as jnp
import numpy as np
from jax import lax
from jax.experimental import pallas as pl
from jax.experimental.pallas import tpu as pltpu
from jax.sharding import Mesh, PartitionSpec as P

D = 1024
H = 16
HD = 64
FF = 4096
PR = 32
PC = 32

norm_eps = 1e-06
LOW = jnp.bfloat16
WIDE = jnp.float32
MIB = 2**20
SCALE2 = math.log2(math.e) / math.sqrt(HD)
SAFE_LOG2 = 100.0
FORWARD_GROUP = 4
BACKWARD_GROUP = 4
ROWS_ROWS = (((1,), (1,)), ((), ()))
ROWS_COLS = (((1,), (0,)), ((), ()))
SHIFT_ONE, SCALE_ONE, GATE_ONE, SHIFT_TWO, SCALE_TWO, GATE_TWO = range(6)


def dot(left, right, dims=ROWS_COLS):
    return lax.dot_general(left, right, dims, preferred_element_type=WIDE)


def exact_dot(left, right, dims=ROWS_COLS):
    return lax.dot_general(
        left, right, dims, preferred_element_type=WIDE, precision=lax.Precision.HIGHEST
    )


def vmem():
    return pl.BlockSpec(memory_space=pltpu.VMEM)


def smem():
    return pl.BlockSpec(memory_space=pltpu.SMEM)


def whole(shape):
    return pl.BlockSpec(shape, lambda *unused: (0,) * len(shape))


def behind(kernel, count):
    def ordered(*refs):
        return kernel(*refs[count:])

    return ordered


def anywhere(count):
    return [pl.BlockSpec(memory_space=pl.ANY)] * count


def column_sum(values):
    return jnp.sum(values, axis=0, keepdims=True)


def head_masks(rows, lanes, heads):
    lane = lax.broadcasted_iota(jnp.int32, (rows, lanes), 1)
    return [lane // HD == h for h in range(heads)]


def square_norm(values, masks):
    squared = values.astype(WIDE)
    squared = squared * squared
    return [
        jnp.max(jnp.sum(jnp.where(mask, squared, 0.0), axis=1, keepdims=True)) for mask in masks
    ]


def split_sources(refs, parts, own):
    trios, refs = refs[:parts], refs[parts:]
    if own:
        return trios, trios, refs
    return trios, refs[:parts], refs[parts:]


def joined(refs, slot, place):
    return jnp.concatenate([ref[slot, place] for ref in refs], axis=0)


def forward_kernel(order, flag_in, *refs, parts, own, first, last, heads):
    trios, pairs, refs = split_sources(refs, parts, own)
    frames, unused, few, lanes = trios[0].shape
    tokens = few * parts
    if not first:
        num_in, sum_in, top_in = refs[:3]
        refs = refs[3:]
    if last:
        attn_out, log_out = refs[:2]
        refs = refs[2:]
    else:
        flag_out, num_out, sum_out, top_out = refs[:4]
        refs = refs[4:]
    queries, keys, values, accs = refs
    group = accs.shape[1] // tokens
    masks = head_masks(tokens, lanes, heads)
    one = jnp.ones((tokens, lanes), LOW)
    zero = jnp.zeros((tokens, lanes), LOW)
    width = 2 * HD
    bound = jnp.float32(0.0)
    q_top = [jnp.float32(0.0)] * heads
    k_top = [jnp.float32(0.0)] * heads
    for t in range(frames):
        slot = order[t]
        k = joined(pairs, slot, 0)
        v = joined(pairs, slot, 1)
        queries[t] = joined(trios, slot, 2)
        q_top = [jnp.maximum(a, b) for a, b in zip(q_top, square_norm(queries[t], masks))]
        k_top = [jnp.maximum(a, b) for a, b in zip(k_top, square_norm(k, masks))]
        for h in range(heads):
            keys[h, t] = jnp.where(masks[h], k, zero)
            if heads == 2:
                values[h, t] = jnp.where(masks[h], v, one)
            else:
                values[h, t] = jnp.concatenate([v, one], axis=1)
    for a, b in zip(q_top, k_top):
        bound = jnp.maximum(bound, a * b)
    fast = bound * (SCALE2 * SCALE2) <= SAFE_LOG2 * SAFE_LOG2
    if not first:
        fast = jnp.logical_and(fast, flag_in[0] == 1)
    if not last:
        flag_out[0] = jnp.where(fast, 1, 0).astype(jnp.int32)
    low_lane = lax.broadcasted_iota(jnp.int32, (tokens, lanes), 1) < HD
    pick = lax.broadcasted_iota(jnp.int32, (8, lanes), 1) == HD * lax.broadcasted_iota(
        jnp.int32, (8, lanes), 0
    )
    pick = jnp.where(pick, 1.0, 0.0).astype(WIDE)

    def split(num, total):
        if heads == 2:
            turned = pltpu.roll(total, HD, 1)
            return [jnp.where(low_lane, num, turned), jnp.where(low_lane, turned, num)]
        return [jnp.concatenate([num, total], axis=1)]

    def join(accs):
        if heads == 2:
            num = jnp.where(low_lane, accs[0], accs[1])
            total = jnp.where(low_lane, accs[1], accs[0])
            return num, pltpu.roll(total, HD, 1)
        return accs[0][:, :HD], accs[0][:, HD:]

    def start(slot):
        if first:
            return [jnp.zeros((tokens, width), WIDE) for _ in range(heads)]
        return split(num_in[slot], sum_in[slot])

    def store(slot, accs, top):
        num, total = join(accs)
        if last:
            attn_out[slot] = (num / total).astype(LOW)
            logs = jnp.log2(total)
            if top is not None:
                logs = logs + top
            log_out[slot] = exact_dot(pick, logs, ROWS_ROWS)
        else:
            num_out[slot] = num
            sum_out[slot] = total
            top_out[slot] = jnp.zeros((tokens, lanes), WIDE) if top is None else top

    @pl.when(fast)
    def _():
        def outer(g, unused):
            base = g * group
            q = queries[pl.ds(base, group)].reshape(group * tokens, lanes)
            for i in range(group):
                for h, value in enumerate(start(order[base + i])):
                    accs[h, i * tokens : (i + 1) * tokens] = value

            def tile(j, skip):
                rows = slice(skip * tokens, group * tokens)
                for h in range(heads):
                    s = dot(q[rows], keys[h, j], ROWS_ROWS)
                    p = jnp.exp2(s * SCALE2).astype(LOW)
                    accs[h, rows] += dot(p, values[h, j])

            def inner(j, unused):
                tile(j, 0)
                return unused

            lax.fori_loop(0, base + 1, inner, 0)
            for skip in range(1, group):
                tile(base + skip, skip)
            for i in range(group):
                rows = slice(i * tokens, (i + 1) * tokens)
                store(order[base + i], [accs[h, rows] for h in range(heads)], None)
            return unused

        lax.fori_loop(0, frames // group, outer, 0)

    @pl.when(jnp.logical_not(fast))
    def _():
        def outer(t, unused):
            slot = order[t]
            q = queries[t]

            def inner(j, state):
                sums, tops = state
                new_accs, new_tops = [], []
                for h in range(heads):
                    s = dot(q, keys[h, j], ROWS_ROWS) * SCALE2
                    top = jnp.maximum(tops[h], jnp.max(s, axis=1, keepdims=True))
                    p = jnp.exp2(s - top).astype(LOW)
                    keep = jnp.exp2(tops[h] - top)
                    new_accs.append(sums[h] * keep + dot(p, values[h, j]))
                    new_tops.append(top)
                return new_accs, new_tops

            if first:
                tops = [jnp.full((tokens, 1), -1e30, WIDE)] * heads
            else:
                tops = [top_in[slot][:, h * HD : h * HD + 1] for h in range(heads)]
            sums, tops = lax.fori_loop(0, t + 1, inner, (start(slot), tops))
            top = jnp.broadcast_to(tops[0], (tokens, lanes))
            if heads == 2:
                top = jnp.where(low_lane, top, jnp.broadcast_to(tops[1], (tokens, lanes)))
            store(slot, sums, top)
            return unused

        lax.fori_loop(0, frames, outer, 0)


def attention_forward(order, state, trios, pairs, last, after):
    frames, unused, few, lanes = trios[0].shape
    parts, own = len(trios), pairs is None
    tokens = few * parts
    sources = tuple(trios) + (() if own else tuple(pairs))
    heads = lanes // HD
    first = state is None
    wide = jax.ShapeDtypeStruct((frames, tokens, lanes), WIDE)
    if last:
        out_shape = [
            jax.ShapeDtypeStruct((frames, tokens, lanes), LOW),
            jax.ShapeDtypeStruct((frames, 8, tokens), WIDE),
        ]
        out_specs = [vmem()] * 2
    else:
        out_shape = [jax.ShapeDtypeStruct((1,), jnp.int32), wide, wide, wide]
        out_specs = [smem()] + [vmem()] * 3
    flag = jnp.zeros((1,), jnp.int32) if first else state[0]
    rest = () if first else tuple(state[1:])
    work = heads * frames * (frames + 1) // 2 * tokens * tokens
    return pl.pallas_call(
        behind(
            functools.partial(
                forward_kernel, parts=parts, own=own, first=first, last=last, heads=heads
            ),
            len(after),
        ),
        out_shape=out_shape,
        in_specs=anywhere(len(after)) + [smem(), smem()]
        + [vmem()] * (len(sources) + len(rest)),
        out_specs=out_specs,
        scratch_shapes=[
            pltpu.VMEM((frames, tokens, lanes), LOW),
            pltpu.VMEM((heads, frames, tokens, lanes), LOW),
            pltpu.VMEM((heads, frames, tokens, max(lanes, 2 * HD)), LOW),
            pltpu.VMEM((heads, FORWARD_GROUP * tokens, max(lanes, 2 * HD)), WIDE),
        ],
        compiler_params=pltpu.CompilerParams(vmem_limit_bytes=56 * MIB),
        cost_estimate=pl.CostEstimate(
            flops=work * 4 * HD * 8, bytes_accessed=16 * MIB, transcendentals=work
        ),
        name="attention_forward",
    )(*after, order, flag, *sources, *rest)


def backward_kernel(order, grad, out, lse, *refs, parts, sources, first, last, came, heads):
    trios, pairs, refs = refs[:parts], refs[parts : parts + sources], refs[parts + sources :]
    frames, tokens, lanes = grad.shape
    size = pairs[0].shape[2]
    few = size * sources
    if not first:
        dq_in = refs[0]
        refs = refs[1:]
    if came:
        pair_came = refs[0]
        refs = refs[1:]
    if not last:
        dq_sum, refs = refs[0], refs[1:]
    finals, refs = refs[:sources], refs[sources:]
    queries, grads, delta, logs, keys, values, key_turned, dk, dv = refs[:9]
    if last:
        dq_sum = refs[9]
    places = (parts, parts + 1) if last else (0, 1)
    group = dk.shape[0] // few
    masks = head_masks(tokens, lanes, heads)
    zero = jnp.zeros((tokens, lanes), LOW)
    lane8 = lax.broadcasted_iota(jnp.int32, (8, lanes), 1) // HD
    pick = jnp.where(lane8 == lax.broadcasted_iota(jnp.int32, (8, lanes), 0), 1.0, 0.0)
    for t in range(frames):
        slot = order[t]
        q = joined(trios, slot, 2)
        g = grad[slot]
        k = joined(pairs, slot, 0)
        for h in range(heads):
            queries[h, t] = jnp.where(masks[h], q, zero)
            grads[h, t] = jnp.where(masks[h], g, zero)
        keys[t] = k
        values[t] = joined(pairs, slot, 1)
        key_turned[t // group, :, (t % group) * few : (t % group + 1) * few] = k.T
        logs[t] = lse[slot]
        delta[t] = exact_dot(
            pick.astype(WIDE), g.astype(WIDE) * out[slot].astype(WIDE), ROWS_ROWS
        )
        dq_sum[t] = jnp.zeros((lanes, tokens), WIDE) if first else dq_in[t]
    group_masks = head_masks(group * few, lanes, heads)
    group_zero = jnp.zeros((group * few, lanes), LOW)

    def outer(index, unused):
        base = index * group
        k = keys[pl.ds(base, group)].reshape(group * few, lanes)
        v = values[pl.ds(base, group)].reshape(group * few, lanes)
        ks = [jnp.where(mask, k, group_zero) for mask in group_masks]
        vs = [jnp.where(mask, v, group_zero) for mask in group_masks]
        dk[...] = jnp.zeros(dk.shape, WIDE)
        dv[...] = jnp.zeros(dv.shape, WIDE)

        def tile(j, count):
            rows = slice(0, count * few)
            for h in range(heads):
                q = queries[h, j]
                g = grads[h, j]
                s = dot(ks[h][rows], q, ROWS_ROWS)
                p = jnp.exp2(s * SCALE2 - logs[j, h : h + 1, :])
                dp = dot(vs[h][rows], g, ROWS_ROWS)
                ds = (p * (dp - delta[j, h : h + 1, :])).astype(LOW)
                dv[rows] += dot(p.astype(LOW), g)
                dk[rows] += dot(ds, q)
                span = slice(h * HD, (h + 1) * HD)
                dq_sum[j, span, :] += dot(key_turned[index, span, rows], ds)

        def inner(j, unused):
            tile(j, group)
            return unused

        for count in range(1, group):
            tile(base + count - 1, count)
        lax.fori_loop(base + group - 1, frames, inner, 0)
        for i in range(group):
            rows = slice(i * few, (i + 1) * few)
            slot = order[base + i]
            part_k = dk[rows] * (1.0 / math.sqrt(HD))
            part_v = dv[rows]
            if came:
                part_k = part_k + pair_came[slot, 0].astype(WIDE)
                part_v = part_v + pair_came[slot, 1].astype(WIDE)
            for n, final in enumerate(finals):
                span = slice(n * size, (n + 1) * size)
                final[slot, places[0]] = part_k[span].astype(LOW)
                final[slot, places[1]] = part_v[span].astype(LOW)
        return unused

    lax.fori_loop(0, frames // group, outer, 0)
    if last:
        for t in range(frames):
            dq = (dq_sum[t].T * (1.0 / math.sqrt(HD))).astype(LOW)
            for i in range(parts):
                finals[0][order[t], i] = dq[i * size : (i + 1) * size]


def attention_backward(order, dq, came, trios, pairs, grad, out, lse, last, after):
    frames, tokens, lanes = grad.shape
    size = pairs[0].shape[2]
    few = size * len(pairs)
    parts = len(trios)
    heads = lanes // HD
    first = dq is None
    sums = (frames, lanes, tokens)
    extra = tuple(array for array in (dq, came) if array is not None)
    work = heads * frames * (frames + 1) // 2 * tokens * few
    rows = BACKWARD_GROUP * few
    scratch = [
        pltpu.VMEM((heads, frames, tokens, lanes), LOW),
        pltpu.VMEM((heads, frames, tokens, lanes), LOW),
        pltpu.VMEM((frames, 8, tokens), WIDE),
        pltpu.VMEM((frames, 8, tokens), WIDE),
        pltpu.VMEM((frames, few, lanes), LOW),
        pltpu.VMEM((frames, few, lanes), LOW),
        pltpu.VMEM((frames // BACKWARD_GROUP, lanes, rows), LOW),
        pltpu.VMEM((rows, lanes), WIDE),
        pltpu.VMEM((rows, lanes), WIDE),
    ]
    pair_shape = jax.ShapeDtypeStruct((frames, (parts if last else 0) + 2, size, lanes), LOW)
    if last:
        out_shape = [pair_shape]
        scratch.append(pltpu.VMEM(sums, WIDE))
    else:
        out_shape = [jax.ShapeDtypeStruct(sums, WIDE)] + [pair_shape] * len(pairs)
    return pl.pallas_call(
        behind(
            functools.partial(
                backward_kernel, parts=parts, sources=len(pairs), first=first, last=last,
                came=came is not None, heads=heads,
            ),
            len(after),
        ),
        out_shape=out_shape,
        in_specs=anywhere(len(after)) + [smem()] + [vmem()] * (3 + parts + len(pairs) + len(extra)),
        out_specs=[vmem()] * len(out_shape),
        scratch_shapes=scratch,
        compiler_params=pltpu.CompilerParams(vmem_limit_bytes=56 * MIB),
        cost_estimate=pl.CostEstimate(
            flops=work * 10 * HD * 5, bytes_accessed=16 * MIB, transcendentals=work
        ),
        name="attention_backward",
    )(*after, order, grad, out, lse, *trios, *pairs, *extra)


def normalize(values):
    centered = values - jnp.mean(values, axis=-1, keepdims=True)
    inverse = lax.rsqrt(jnp.mean(centered * centered, axis=-1, keepdims=True) + norm_eps)
    return (centered * inverse, inverse)


def norm_backward(grad_normed, normed, inverse):
    mean_grad = jnp.mean(grad_normed, axis=-1, keepdims=True)
    mean_prod = jnp.mean(grad_normed * normed, axis=-1, keepdims=True)
    return inverse * (grad_normed - mean_grad - normed * mean_prod)


def part(mod, index):
    return mod[0:1, index * D : (index + 1) * D]


def swap_halves(values):
    lanes = values.shape[1]
    lane = lax.broadcasted_iota(jnp.int32, values.shape, 1) % HD
    eight, twelve = HD // 8, 3 * HD // 16
    quarter, last = HD // 4, HD // 4 + 2 * twelve

    def ahead(step):
        return pltpu.roll(values, lanes - step, 1)

    def behind(step):
        return pltpu.roll(values, step, 1)

    first_half = ((lane >= quarter) & (lane < quarter + twelve)) | (
        (lane >= last) & (lane < last + twelve)
    )
    short = jnp.where(lane < eight, ahead(eight), behind(eight))
    long = jnp.where(first_half, ahead(twelve), behind(twelve))
    return jnp.where(lane < quarter, short, long)


def turned(values, cosine, sine):
    wide = cosine.shape[1]
    pieces = []
    for at in range(0, values.shape[1], wide):
        block = values[:, at : at + wide]
        pieces.append(block * cosine + swap_halves(block) * sine)
    return pieces[0] if len(pieces) == 1 else jnp.concatenate(pieces, axis=1)


def input_kernel(tokens, mod, w_query, w_key, w_value, cosine, sine, hidden, trio):
    @pl.when(pl.program_id(0) == 0)
    def _():
        normed, unused = normalize(tokens[...].astype(WIDE))
        hidden[...] = (normed * (1.0 + part(mod, SCALE_ONE)) + part(mod, SHIFT_ONE)).astype(LOW)

    groups, unused, unused, lanes = trio.shape
    h = hidden[...]
    cos, sin = cosine[...], sine[...]
    k = turned(dot(h, w_key[...]), cos, sin).astype(LOW)
    v = dot(h, w_value[...]).astype(LOW)
    q = turned(dot(h, w_query[...]), cos, sin).astype(LOW)
    for g in range(groups):
        span = slice(g * lanes, (g + 1) * lanes)
        trio[g, 0] = k[:, span]
        trio[g, 1] = v[:, span]
        trio[g, 2] = q[:, span]


def input_projections(tokens, mod, w_query, w_key, w_value, cosine, sine, frames):
    count = tokens.shape[0]
    lanes = D // frames
    wide = 256
    groups = wide // lanes
    weight = pl.BlockSpec((D, wide), lambda c: (0, c))
    trio = pl.BlockSpec((groups, 3, count, lanes), lambda c: (c, 0, 0, 0))
    return pl.pallas_call(
        input_kernel,
        grid=(D // wide,),
        out_shape=[
            jax.ShapeDtypeStruct((count, D), LOW),
            jax.ShapeDtypeStruct((frames, 3, count, lanes), LOW),
        ],
        in_specs=[whole((count, D)), whole((1, 6 * D)), weight, weight, weight]
        + [whole(cosine.shape)] * 2,
        out_specs=[whole((count, D)), trio],
        compiler_params=pltpu.CompilerParams(vmem_limit_bytes=48 * MIB),
        cost_estimate=pl.CostEstimate(
            flops=6 * count * D * D, bytes_accessed=12 * MIB, transcendentals=0
        ),
        name="input_projections",
    )(tokens, mod, w_query, w_key, w_value, cosine, sine)


def pull_kernel(cotangent, mod, w_down, pulled, scaled_turned, scaled):
    @pl.when(pl.program_id(0) == 0)
    def _():
        scaled[...] = (part(mod, GATE_TWO) * cotangent[...].astype(WIDE)).astype(LOW)
        scaled_turned[...] = scaled[...].T

    pulled[...] = dot(scaled[...], w_down[...], ROWS_ROWS).astype(LOW)


def pull_down(cotangent, mod, w_down):
    count = cotangent.shape[0]
    wide = 512
    return pl.pallas_call(
        pull_kernel,
        grid=(FF // wide,),
        out_shape=[
            jax.ShapeDtypeStruct((count, FF), LOW), jax.ShapeDtypeStruct((D, count), LOW)
        ],
        in_specs=[
            whole((count, D)), whole((1, 6 * D)), pl.BlockSpec((wide, D), lambda c: (c, 0))
        ],
        out_specs=[pl.BlockSpec((count, wide), lambda c: (0, c)), whole((D, count))],
        scratch_shapes=[pltpu.VMEM((count, D), LOW)],
        compiler_params=pltpu.CompilerParams(vmem_limit_bytes=32 * MIB),
        cost_estimate=pl.CostEstimate(
            flops=2 * count * D * FF, bytes_accessed=14 * MIB, transcendentals=0
        ),
        name="pull_down",
    )(cotangent, mod, w_down)


def middle_kernel(
    attn, tokens, cotangent, mod, w_proj, w_up, pulled,
    middle, hidden, active, grad_up_in, grad_middle, grad_branch, grad_attn,
    grad_gate, grad_shift, grad_scale, branch, normed, inverse, total
):
    step = pl.program_id(0)
    frames, count, lanes = attn.shape

    @pl.when(step == 0)
    def _():
        for f in range(frames):
            hidden[:, f * lanes : (f + 1) * lanes] = attn[f]
        product = dot(hidden[...], w_proj[...])
        branch[...] = product
        mid = tokens[...].astype(WIDE) + part(mod, GATE_ONE) * product
        middle[...] = mid
        n, inv = normalize(mid)
        normed[...] = n
        inverse[...] = inv
        hidden[...] = (n * (1.0 + part(mod, SCALE_TWO)) + part(mod, SHIFT_TWO)).astype(LOW)
        total[...] = jnp.zeros(total.shape, WIDE)

    weight = w_up[...]
    u = dot(hidden[...], weight)
    rate = math.sqrt(2.0 / math.pi)
    square = u * u
    bend = jnp.tanh(rate * (u + 0.044715 * (u * square)))
    half = 0.5 * (1.0 + bend)
    active[...] = (u * half).astype(LOW)
    slope = half + (0.5 * rate) * u * (1.0 - bend * bend) * (1.0 + (3 * 0.044715) * square)
    du = (pulled[...].astype(WIDE) * slope).astype(LOW)
    grad_up_in[...] = du
    total[...] += dot(du, weight, ROWS_ROWS)

    @pl.when(step == pl.num_programs(0) - 1)
    def _():
        dh = total[...]
        n = normed[...]
        grad_scale[...] = column_sum(dh * n)
        grad_shift[...] = column_sum(dh)
        dx = cotangent[...].astype(WIDE) + norm_backward(
            dh * (1.0 + part(mod, SCALE_TWO)), n, inverse[...]
        )
        grad_middle[...] = dx
        grad_gate[...] = column_sum(dx * branch[...])
        dy = (part(mod, GATE_ONE) * dx).astype(LOW)
        grad_branch[...] = dy
        back = dot(dy, w_proj[...], ROWS_ROWS).astype(LOW)
        for f in range(frames):
            grad_attn[f] = back[:, f * lanes : (f + 1) * lanes]


def middle_block(attn, tokens, cotangent, mod, w_proj, w_up, pulled):
    frames, count, lanes = attn.shape
    wide = 512
    flat = whole((count, D))
    row = whole((1, D))
    columns = pl.BlockSpec((count, wide), lambda c: (0, c))
    heads = whole(attn.shape)

    def of(shape, kind):
        return jax.ShapeDtypeStruct(shape, kind)

    return pl.pallas_call(
        middle_kernel,
        grid=(FF // wide,),
        out_shape=[
            of((count, D), WIDE), of((count, D), LOW), of((count, FF), LOW), of((count, FF), LOW),
            of((count, D), WIDE), of((count, D), LOW), of(attn.shape, LOW),
            of((1, D), WIDE), of((1, D), WIDE), of((1, D), WIDE),
        ],
        in_specs=[
            heads, flat, flat, whole((1, 6 * D)), whole((D, D)),
            pl.BlockSpec((D, wide), lambda c: (0, c)), columns,
        ],
        out_specs=[flat, flat, columns, columns, flat, flat, heads, row, row, row],
        scratch_shapes=[
            pltpu.VMEM((count, D), WIDE), pltpu.VMEM((count, D), WIDE),
            pltpu.VMEM((count, 1), WIDE), pltpu.VMEM((count, D), WIDE),
        ],
        compiler_params=pltpu.CompilerParams(vmem_limit_bytes=56 * MIB),
        cost_estimate=pl.CostEstimate(
            flops=2 * count * D * (2 * FF + 2 * D), bytes_accessed=30 * MIB,
            transcendentals=count * FF,
        ),
        name="middle_block",
    )(attn, tokens, cotangent, mod, w_proj, w_up, pulled)


def weights_kernel(
    slot, active, grad_up_in, hidden, scaled_turned, attn, grad_branch, *refs, keep
):
    step = pl.program_id(0)
    frames, count, lanes = attn.shape
    half = frames // 2
    wide = D // frames
    if keep:
        activity, middle, cotangent, mod, w_down = refs[:5]
        out, grad_gate, down_out, up_out, hidden_turned, attn_turned, flat, total = refs[5:]
    else:
        down_out, up_out, hidden_turned, attn_turned, flat = refs
    chunks, narrow = down_out.shape[1], down_out.shape[3]

    @pl.when(step == 0)
    def _():
        for f in range(frames):
            flat[:, f * lanes : (f + 1) * lanes] = attn[f]
        for f in range(frames):
            place = lax.bitwise_xor(f, slot[0])

            @pl.when(place % 2 == (0 if keep else 1))
            def _():
                span = slice(f * wide, (f + 1) * wide)
                hidden_turned[place // 2] = hidden[:, span].T
                attn_turned[place // 2] = flat[:, span].T

        if keep:
            total[...] = jnp.zeros(total.shape, WIDE)

    @pl.when(step < half)
    def _():
        if keep:
            total[...] += dot(activity[...], w_down[...])
        down = dot(scaled_turned[...], active[...]).astype(LOW)
        for r in range(chunks):
            down_out[0, r] = down[:, r * narrow : (r + 1) * narrow]
        up = dot(hidden_turned[...].reshape(D // 2, count), grad_up_in[...]).astype(LOW)
        up_out[...] = up.reshape(half, wide, up.shape[1])

    @pl.when(step >= half)
    def _():
        proj = dot(attn_turned[...].reshape(D // 2, count), grad_branch[...]).astype(LOW)
        up_out[...] = proj.reshape(half, wide, proj.shape[1])

    if keep:
        @pl.when(step == half - 1)
        def _():
            z = total[...]
            out[...] = (middle[...] + part(mod, GATE_TWO) * z).astype(LOW)
            grad_gate[...] = column_sum(cotangent[...].astype(WIDE) * z)


def weight_gradients(
    slot, active, grad_up_in, hidden, scaled_turned, attn, grad_branch, rows, finish
):
    frames, count, lanes = attn.shape
    keep = finish is not None
    half = frames // 2
    narrow = FF // frames
    wide = FF // half
    extra = D // wide

    def down_block(i, slot):
        place = 2 * jnp.minimum(i, half - 1) + (0 if keep else 1)
        return lax.bitwise_xor(place, slot[0])

    def up_block(i, slot):
        return jnp.minimum(i, half - 1)

    flat = whole((count, D))
    down = (1, rows, D, narrow // rows)
    in_specs = [
        pl.BlockSpec((count, narrow), lambda i, slot: (0, down_block(i, slot))),
        pl.BlockSpec((count, wide), lambda i, slot: (0, up_block(i, slot))),
        flat, whole((D, count)), whole(attn.shape),
        pl.BlockSpec((count, wide), lambda i, slot: (0, jnp.maximum(i - half, 0))),
    ]
    out_specs = [
        pl.BlockSpec(down, lambda i, slot: (jnp.minimum(i, half - 1), 0, 0, 0)),
        pl.BlockSpec((half, D // frames, wide), lambda i, slot: (0, 0, i)),
    ]
    out_shape = [
        jax.ShapeDtypeStruct((half, rows, D, narrow // rows), LOW),
        jax.ShapeDtypeStruct((half, D // frames, FF + D), LOW),
    ]
    scratch = [
        pltpu.VMEM((half, D // frames, count), LOW), pltpu.VMEM((half, D // frames, count), LOW),
        pltpu.VMEM((count, D), LOW),
    ]
    args = (slot, active, grad_up_in, hidden, scaled_turned, attn, grad_branch)
    if keep:
        args += (active,) + tuple(finish)
        in_specs += [
            pl.BlockSpec((count, wide), lambda i, slot: (0, up_block(i, slot))),
            flat, flat, whole((1, 6 * D)),
            pl.BlockSpec((wide, D), lambda i, slot: (up_block(i, slot), 0)),
        ]
        out_specs = [flat, whole((1, D))] + out_specs
        out_shape = [
            jax.ShapeDtypeStruct((count, D), LOW), jax.ShapeDtypeStruct((1, D), WIDE)
        ] + out_shape
        scratch.append(pltpu.VMEM((count, D), WIDE))
    return pl.pallas_call(
        functools.partial(weights_kernel, keep=keep),
        grid_spec=pltpu.PrefetchScalarGridSpec(
            num_scalar_prefetch=1, grid=(half + extra,),
            in_specs=in_specs, out_specs=out_specs, scratch_shapes=scratch,
        ),
        out_shape=out_shape,
        compiler_params=pltpu.CompilerParams(vmem_limit_bytes=56 * MIB),
        cost_estimate=pl.CostEstimate(
            flops=count * D * (2 * FF + D + (2 * FF if keep else 0)), bytes_accessed=24 * MIB,
            transcendentals=0,
        ),
        name="weight_gradients",
    )(*args)


def turn_kernel(*refs):
    *parts, target = refs
    target[...] = jnp.concatenate([part[...] for part in parts], axis=0).T


def turn_hidden(parts):
    count = sum(part.shape[0] for part in parts)
    return pl.pallas_call(
        turn_kernel,
        out_shape=jax.ShapeDtypeStruct((D, count), LOW),
        in_specs=[vmem()] * len(parts),
        out_specs=vmem(),
        compiler_params=pltpu.CompilerParams(vmem_limit_bytes=32 * MIB),
        cost_estimate=pl.CostEstimate(flops=0, bytes_accessed=2 * MIB, transcendentals=0),
        name="turn_hidden",
    )(*parts)


def three_gradients(early, late, at):
    q = jnp.concatenate([late[at, 0], late[at, 1]], axis=0)
    k = jnp.concatenate([early[at, 0], late[at, 2]], axis=0)
    v = jnp.concatenate([early[at, 1], late[at, 3]], axis=0)
    return q, k, v


def head_kernel(early, grads, hidden, cosine, sine, time_cosine, time_sine, product, total):
    step = pl.program_id(0)

    @pl.when(step == 0)
    def _():
        total[...] = jnp.zeros(total.shape, WIDE)

    cos = cosine[...] + time_cosine[0]
    sin = -(sine[...] + time_sine[0])
    q, k, v = three_gradients(early, grads, 0)
    block = jnp.concatenate(
        [turned(q.astype(WIDE), cos, sin).astype(LOW), turned(k.astype(WIDE), cos, sin).astype(LOW), v],
        axis=1,
    )
    total[...] += dot(hidden[0], block)

    @pl.when(step == pl.num_programs(0) - 1)
    def _():
        product[...] = total[...].astype(LOW)


def head_gradients(early, grads, hidden_all, tables, after):
    frames, unused, few, lanes = grads.shape
    count = 2 * few
    frame = pl.BlockSpec((1, 1, lanes), lambda f: (f, 0, 0))
    return pl.pallas_call(
        behind(head_kernel, len(after)),
        grid=(frames,),
        out_shape=jax.ShapeDtypeStruct((D, 3 * lanes), LOW),
        in_specs=anywhere(len(after)) + [
            pl.BlockSpec((1, 2, few, lanes), lambda f: (f, 0, 0, 0)),
            pl.BlockSpec((1, 4, few, lanes), lambda f: (f, 0, 0, 0)),
            pl.BlockSpec((1, D, count), lambda f: (f, 0, 0)),
            whole((count, lanes)), whole((count, lanes)), frame, frame,
        ],
        out_specs=whole((D, 3 * lanes)),
        scratch_shapes=[pltpu.VMEM((D, 3 * lanes), WIDE)],
        compiler_params=pltpu.CompilerParams(vmem_limit_bytes=32 * MIB),
        cost_estimate=pl.CostEstimate(
            flops=6 * frames * count * D * lanes, bytes_accessed=12 * MIB, transcendentals=0
        ),
        name="head_gradients",
    )(*after, early, grads, hidden_all, *tables)


def output_kernel(
    early, grads, w_query, w_key, w_value, cosine, sine, tokens, mod, grad_middle,
    grad_tokens, grad_shift, grad_scale, total
):
    step = pl.program_id(0)
    groups = grads.shape[0]

    @pl.when(step == 0)
    def _():
        total[...] = jnp.zeros(total.shape, WIDE)

    dh = total[...]
    blocks = [three_gradients(early, grads, g) for g in range(groups)]
    for i, weight in enumerate((w_query, w_key, w_value)):
        block = jnp.concatenate([three[i] for three in blocks], axis=1)
        if i < 2:
            block = turned(block.astype(WIDE), cosine[...], -sine[...]).astype(LOW)
        dh = dh + dot(block, weight[...], ROWS_ROWS)
    total[...] = dh

    @pl.when(step == pl.num_programs(0) - 1)
    def _():
        dh = total[...]
        n, inverse = normalize(tokens[...].astype(WIDE))
        grad_scale[...] = column_sum(dh * n)
        grad_shift[...] = column_sum(dh)
        grad_tokens[...] = (
            grad_middle[...] + norm_backward(dh * (1.0 + part(mod, SCALE_ONE)), n, inverse)
        ).astype(LOW)


def input_gradients(early, grads, w_query, w_key, w_value, cosine, sine, tokens, mod, grad_middle, after):
    frames, unused, few, lanes = grads.shape
    count = 2 * few
    wide = 256
    groups = wide // lanes
    flat = whole((count, D))
    row = whole((1, D))
    weight = pl.BlockSpec((D, wide), lambda c: (0, c))
    rows = jax.ShapeDtypeStruct((1, D), WIDE)
    return pl.pallas_call(
        behind(output_kernel, len(after)),
        grid=(D // wide,),
        out_shape=[jax.ShapeDtypeStruct((count, D), LOW), rows, rows],
        in_specs=anywhere(len(after)) + [
            pl.BlockSpec((groups, 2, few, lanes), lambda c: (c, 0, 0, 0)),
            pl.BlockSpec((groups, 4, few, lanes), lambda c: (c, 0, 0, 0)),
            weight, weight, weight, whole(cosine.shape), whole(sine.shape),
            flat, whole((1, 6 * D)), flat,
        ],
        out_specs=[flat, row, row],
        scratch_shapes=[pltpu.VMEM((count, D), WIDE)],
        compiler_params=pltpu.CompilerParams(vmem_limit_bytes=48 * MIB),
        cost_estimate=pl.CostEstimate(
            flops=6 * count * D * D, bytes_accessed=14 * MIB, transcendentals=0
        ),
        name="input_gradients",
    )(*after, early, grads, w_query, w_key, w_value, cosine, sine, tokens, mod, grad_middle)


def halves_kernel(mine, keep_give, came_give, keep_hold, came_hold, give, hold):
    give[0] = (keep_give[0, 0].astype(WIDE) + came_give[0, 0].astype(WIDE)).astype(LOW)
    hold[0] = (keep_hold[0, 0].astype(WIDE) + came_hold[0, 0].astype(WIDE)).astype(LOW)


def add_halves(keep, came, axis, mine, after):
    shape = keep.shape
    lead, trail = math.prod(shape[:axis]), math.prod(shape[axis + 1 : -2])
    rest = shape[:axis] + shape[axis + 1 :]
    many = 2 if trail % 2 == 0 else 1
    block = (1, 1, many) + shape[-2:]
    view = (lead, 2, trail) + shape[-2:]

    def part_of(other):
        def index(a, b, mine, *unused):
            return (a, 1 - mine[0] if other else mine[0], b, 0, 0)

        return pl.BlockSpec(block, index)

    out = pl.BlockSpec((1, many) + shape[-2:], lambda a, b, *unused: (a, b, 0, 0))
    out_shape = jax.ShapeDtypeStruct((lead, trail) + shape[-2:], LOW)

    def ordered(mine, *refs):
        halves_kernel(mine, *refs[len(after) :])

    keep, came = keep.reshape(view), came.reshape(view)
    give, hold = pl.pallas_call(
        ordered,
        grid_spec=pltpu.PrefetchScalarGridSpec(
            num_scalar_prefetch=1,
            grid=(lead, trail // many),
            in_specs=anywhere(len(after)) + [part_of(True)] * 2 + [part_of(False)] * 2,
            out_specs=[out, out],
        ),
        out_shape=[out_shape, out_shape],
        cost_estimate=pl.CostEstimate(
            flops=keep.size, bytes_accessed=6 * keep.size, transcendentals=0
        ),
        name="add_halves",
    )(mine, *after, keep, came, keep, came)
    return give.reshape(rest), hold.reshape(rest)


def total_kernel(keep, came, total):
    total[...] = keep[...].astype(WIDE) + came[...].astype(WIDE)


def add_last(keep, came, after):
    return pl.pallas_call(
        behind(total_kernel, len(after)),
        out_shape=jax.ShapeDtypeStruct(keep.shape, WIDE),
        in_specs=anywhere(len(after)) + [vmem()] * 2,
        out_specs=vmem(),
        name="add_last",
    )(*after, keep, came)


def same_kernel(*unused):
    pass


def order_after(array, after):
    return pl.pallas_call(
        same_kernel,
        out_shape=jax.ShapeDtypeStruct(array.shape, array.dtype),
        in_specs=anywhere(len(after) + 1),
        out_specs=anywhere(1)[0],
        input_output_aliases={len(after): 0},
        name="order_after",
    )(*after, array)


def pack_kernel(*refs):
    *vectors, codes, packed = refs
    at = 0
    for vector in vectors:
        packed[:, at : at + D] = jnp.broadcast_to(vector[...], (packed.shape[0], D))
        at += D
    packed[:, at:] = codes[...]


def pack(vectors, codes, after):
    return pl.pallas_call(
        behind(pack_kernel, len(after)),
        out_shape=jax.ShapeDtypeStruct((codes.shape[0], len(vectors) * D + codes.shape[1]), WIDE),
        in_specs=anywhere(len(after)) + [vmem()] * (len(vectors) + 1),
        out_specs=vmem(),
        name="pack",
    )(*after, *vectors, codes)


def rotary_rates(lanes):
    rates, parts, signs = [], [], []
    for index, size in enumerate((HD // 4, 3 * HD // 8, 3 * HD // 8)):
        half = size // 2
        rate = 10000.0 ** (-np.arange(half, dtype=np.float32) / np.float32(half))
        rates += [rate, rate]
        parts += [np.full(size, index)]
        signs += [-np.ones(half), np.ones(half)]
    rows = [np.concatenate(rows).astype(np.float32) for rows in (rates, parts, signs)]
    return np.tile(np.stack(rows), (1, lanes // HD))


def tables_kernel(places, times, rates, place_cosine, place_sine, time_cosine, time_sine, cosine, sine, *, local):
    count, lanes = cosine.shape
    frames = time_cosine.shape[0]
    rate, parts, sign = rates[0:1], rates[1:2], rates[2:3]
    token = lax.broadcasted_iota(jnp.int32, (count, lanes), 0)
    few = local * PC
    row = jnp.where(token < few, places[0], places[1] - local) + token // PC
    spot = jnp.where(parts == 1.0, row, token % PC).astype(WIDE)
    timed = parts == 0.0
    cos = jnp.where(timed, 0.0, jnp.cos(spot * rate))
    sin = jnp.where(timed, 0.0, jnp.sin(spot * rate) * sign)
    place_cosine[...] = cos
    place_sine[...] = sin
    for f in range(frames):
        angle = times[f].astype(WIDE) * rate
        time_cosine[f] = jnp.where(timed, jnp.cos(angle), 0.0)
        time_sine[f] = jnp.where(timed, jnp.sin(angle) * sign, 0.0)
    cosine[...] = cos + time_cosine[places[2]]
    sine[...] = sin + time_sine[places[2]]


def rotary_tables(places, times, count, local, lanes):
    flat = jax.ShapeDtypeStruct((count, lanes), WIDE)
    timed = jax.ShapeDtypeStruct((times.shape[0], 1, lanes), WIDE)
    return pl.pallas_call(
        functools.partial(tables_kernel, local=local),
        out_shape=[flat, flat, timed, timed, flat, flat],
        in_specs=[smem(), smem(), vmem()],
        out_specs=[vmem()] * 6,
        name="rotary_tables",
    )(places, times, jnp.asarray(rotary_rates(lanes)))


def columns_kernel(product, *totals):
    frames, rows, unused, width = product.shape
    lanes = width // 3
    for f in range(frames):
        total = jnp.sum(product[f].astype(WIDE), axis=0)
        for i, target in enumerate(totals):
            target[:, f * lanes : (f + 1) * lanes] = total[:, i * lanes : (i + 1) * lanes]


def sum_columns(product):
    shape = jax.ShapeDtypeStruct((product.shape[2], D), WIDE)
    return pl.pallas_call(
        columns_kernel,
        out_shape=[shape] * 3,
        in_specs=[vmem()],
        out_specs=[vmem()] * 3,
        name="sum_columns",
    )(product)


def mod_kernel(early, late, out):
    kept = late.shape[1] * late.shape[2]
    vectors = 6 * D - kept
    codes = early[:, vectors:]
    by_rows = (((0,), (0,)), ((), ()))
    out[:, kept:] = exact_dot(codes, early[:, :vectors], by_rows)
    wide = late.shape[2]
    for c in range(late.shape[1]):
        out[:, c * wide : (c + 1) * wide] = exact_dot(codes, late[:, c, :], by_rows)


def mod_gradient(early, late):
    kept = late.shape[1] * late.shape[2]
    part_rows = early.shape[1] - (6 * D - kept)
    return pl.pallas_call(
        mod_kernel,
        out_shape=jax.ShapeDtypeStruct((part_rows, 6 * D), WIDE),
        in_specs=[vmem()] * 2,
        out_specs=vmem(),
        name="mod_gradient",
    )(early, late)


def sinusoid(levels):
    half_size = D // 2
    freq_table = 10000.0 ** (-jnp.arange(half_size, dtype=WIDE) / half_size)
    angle_table = levels.astype(WIDE)[..., None] * freq_table
    return jnp.concatenate([jnp.cos(angle_table), jnp.sin(angle_table)], axis=-1)


def shards(
    block_in, block_map, noise_level, w_query, w_key, w_value, w_proj, w_up, w_down, w_mod, cotangent
):
    frames = lax.axis_size("frames")
    sides = lax.axis_size("side")
    row_total = lax.axis_size("half") * sides
    frame_slot = lax.axis_index("frames")
    half = lax.axis_index("half")
    side = lax.axis_index("side")
    across = ("half", "side")
    everyone = ("frames",) + across
    devices = frames * row_total
    clips = block_in.shape[1]
    local_rows = block_in.shape[2]
    lanes = D // frames
    order = jnp.argsort(block_map).astype(jnp.int32)
    slot = frame_slot.astype(jnp.int32).reshape(1)

    def clip_tokens(tokens, clip):
        return lax.dynamic_index_in_dim(tokens[0], clip, 0, keepdims=False).reshape(-1, D)

    def other_half(array):
        return lax.ppermute(array, "half", [(0, 1), (1, 0)])

    def return_clip(own, came, kind):
        first = jnp.where(half == 0, own, came).astype(kind)
        second = jnp.where(half == 0, came, own).astype(kind)
        return jnp.stack([first, second]).reshape(1, clips, local_rows, PC, D)

    def swap_groups(grouped):
        return lax.all_to_all(grouped, "frames", split_axis=0, concat_axis=0, tiled=True)

    def pass_on(array, step):
        return lax.ppermute(array, "side", [(i, (i + step) % sides) for i in range(sides)])

    def flip(array, bit):
        return lax.ppermute(array, "frames", [(i, i ^ (1 << bit)) for i in range(frames)])

    def add(left, right):
        return (left.astype(WIDE) + right.astype(WIDE)).astype(LOW)

    class Reduction:
        def __init__(self, send, bits):
            self.came = flip(send, 0)
            self.bits = list(bits)
            self.left = sorted(bits, reverse=True)
            self.row_bits = [("side", bit) for bit in range(sides.bit_length() - 1)] + [("half", 0)]
            self.row_left = [("half", 0)] + self.row_bits[:-1][::-1]
            self.going = None

        def start(self, keep):
            rest = (row_total, -1) + keep.shape[-1:]
            self.shape = (2,) * (len(self.left) + len(self.row_left))
            self.keep = keep.reshape(self.shape + rest[1:])

        def advance(self, after=()):
            came = self.came.reshape(self.keep.shape)
            if self.bits:
                bit = self.bits.pop(0)
                axis = self.left.index(bit)
                self.left.remove(bit)
                name, mine = "frames", 0
            else:
                name, bit = self.row_bits.pop(0)
                axis = self.row_left.index((name, bit))
                self.row_left.remove((name, bit))
                mine = (lax.axis_index(name) >> bit) & 1

            mine = jnp.asarray(mine, jnp.int32).reshape(1)
            self.going, self.keep = add_halves(self.keep, came, axis, mine, after)
            size = lax.axis_size(name)
            self.came = lax.ppermute(self.going, name, [(i, i ^ (1 << bit)) for i in range(size)])

        def finish(self, after):
            while self.bits or self.row_bits:
                self.advance(after)
            return add_last(self.keep, self.came, after)

    high_bits = list(range(1, frames.bit_length() - 1))

    source_own = clip_tokens(block_in, half)
    source_came = other_half(clip_tokens(block_in, 1 - half))
    source = jnp.concatenate([source_own, source_came])
    half_count = source_own.shape[0]

    level = jnp.where(half == 0, noise_level[:, 0], noise_level[:, -1])
    embed = jax.nn.silu(sinusoid(level)).astype(LOW)
    mod = jnp.dot(embed, w_mod, preferred_element_type=WIDE)

    places = jnp.stack(
        [(half * sides + side) * local_rows, ((1 - half) * sides + side) * local_rows, frame_slot]
    ).astype(jnp.int32)
    tables = rotary_tables(places, block_map, 2 * half_count, local_rows, max(lanes, HD))
    cosine, sine = tables[4:]
    tables = tables[:4]

    hidden, trios = [], []
    for at, tokens in ((0, source_own), (half_count, source_came)):
        rows = slice(at, at + half_count)
        h, trio = input_projections(
            tokens, mod, w_query, w_key, w_value, cosine[rows], sine[rows], frames
        )
        hidden.append(h)
        trios.append(swap_groups(order_after(trio, (source_came,)) if at == 0 else trio))
    hidden_all = lax.all_gather(turn_hidden(hidden), "frames", axis=0)
    pairs = [None] + [
        [pass_on(trio[:, :2], step) for trio in trios] for step in range(1, sides)
    ]
    state = None
    passed = tuple(trios) if sides == 1 else tuple(pairs[-1])
    grad_came = other_half(order_after(clip_tokens(cotangent, 1 - half), passed))
    grad_result = jnp.concatenate([clip_tokens(cotangent, half), grad_came])
    pulled, scaled_turned = pull_down(grad_result, mod, w_down)
    for step in range(sides):
        state = attention_forward(order, state, trios, pairs[step], step == sides - 1, ())
    attn_heads, log_total = state
    attn = swap_groups(attn_heads)

    (
        middle, hidden_two, active, grad_up_in, grad_middle, grad_branch, grad_attn,
        grad_gate_one, grad_shift_two, grad_scale_two,
    ) = middle_block(attn, source, grad_result, mod, w_proj, w_up, pulled)
    grad_attn = swap_groups(grad_attn)
    inputs = (slot, active, grad_up_in, hidden_two, scaled_turned, attn, grad_branch, row_total)
    down_send, up_send = weight_gradients(*inputs, None)
    down = Reduction(down_send, high_bits)
    up = Reduction(up_send, high_bits[::-1])
    result, grad_gate_two, down_keep, up_keep = weight_gradients(
        *inputs, (middle, grad_result, mod, w_down)
    )
    down.start(down_keep)
    up.start(up_keep)

    def spread(vectors, after):
        packed = pack(vectors, codes, after)
        return lax.all_to_all(packed, everyone, split_axis=0, concat_axis=0, tiled=True)

    codes = embed.astype(WIDE).reshape(devices, D // devices)
    dq = None
    arrived = [None, None]

    def backward(dq, pairs, came, last, after):
        return attention_backward(
            order, dq, came, trios, pairs, grad_attn, attn_heads, log_total, last, after
        )

    down.advance()
    up.advance()
    mod_came = spread(
        [grad_gate_one, grad_shift_two, grad_scale_two, grad_gate_two],
        (grad_attn, down.going, up.going),
    )
    out_came = other_half(result[half_count:])
    after = (down.going, up.going)
    for step in range(sides - 1, 0, -1):
        dq, *partials = backward(dq, pairs[step], None, False, after)
        after = ()
        for which, partial in enumerate(partials):
            came = pass_on(partial, -step)
            arrived[which] = came if arrived[which] is None else add(arrived[which], came)
    down.advance((dq,))
    up.advance((dq,))
    dq, early = backward(dq, trios[:1], None, False, (down.going, up.going, out_came, mod_came))
    down.advance((dq,))
    up.advance((dq,))
    early = add(early, arrived[0])
    (grads,) = backward(dq, trios[1:], arrived[1], True, (down.going, up.going, early))

    early_back = swap_groups(early)
    grads = order_after(grads, (down.came, up.came, early_back))
    grads_back = swap_groups(grads)
    down.advance((grads,))
    up.advance((grads,))
    head_product = head_gradients(early, grads, hidden_all, tables, (down.going, up.going))
    ordered = order_after(head_product, (grads_back, down.came, up.came))
    product = lax.all_to_all(
        ordered.reshape(devices, D // devices, 3 * lanes),
        everyone, split_axis=0, concat_axis=0, tiled=True,
    )
    grad_source, grad_shift_one, grad_scale_one = input_gradients(
        early_back, grads_back, w_query, w_key, w_value, cosine, sine, source, mod, grad_middle,
        (head_product,),
    )
    in_came = other_half(grad_source[half_count:])
    totals = sum_columns(product.reshape(frames, row_total, D // devices, 3 * lanes))
    late = jnp.concatenate([grad_shift_one, grad_scale_one], axis=-1).reshape(1, -1, 128)
    late = jnp.broadcast_to(late, (devices,) + late.shape[1:])
    late_came = lax.all_to_all(order_after(late, (product,)), everyone, split_axis=0, concat_axis=0, tiled=True)

    grad_down = down.finish((grad_source,)).reshape(D, FF // devices).T
    up_proj = up.finish((grad_source,)).reshape(D // devices, FF + D)
    grad_mod = mod_gradient(mod_came, late_came)
    return (
        return_clip(result[:half_count], out_came, LOW),
        return_clip(grad_source[:half_count], in_came, WIDE),
        *totals,
        up_proj[:, FF:], up_proj[:, :FF], grad_down, grad_mod,
    )


def solution(mesh):
    frames, rows = mesh.shape["frames"], mesh.shape["rows"]
    clips = 2
    split = Mesh(
        mesh.devices.reshape(frames, clips, rows // clips), ("frames", "half", "side")
    )
    tokens = P("frames", None, ("half", "side"), None, None)
    shared = P(("frames", "half", "side"), None)
    return jax.shard_map(
        shards,
        mesh=split,
        in_specs=(tokens, P(), P("frames", None), P(), P(), P(), P(), P(), P(), P(), tokens),
        out_specs=(tokens, tokens) + (shared,) * 7,
        check_vma=False,
    )
```

```python
import functools
import math

import jax
import jax.numpy as jnp
import numpy as np
from jax import lax
from jax.experimental import pallas as pl
from jax.experimental.pallas import tpu as pltpu
from jax.sharding import Mesh, PartitionSpec as P

D = 1024
H = 16
HD = 64
FF = 4096
PR = 32
PC = 32

norm_eps = 1e-06
LOW = jnp.bfloat16
WIDE = jnp.float32
MIB = 2**20
SCALE2 = math.log2(math.e) / math.sqrt(HD)
SAFE_LOG2 = 100.0
FORWARD_GROUP = 4
BACKWARD_GROUP = 4
ROWS_ROWS = (((1,), (1,)), ((), ()))
ROWS_COLS = (((1,), (0,)), ((), ()))
SHIFT_ONE, SCALE_ONE, GATE_ONE, SHIFT_TWO, SCALE_TWO, GATE_TWO = range(6)


def dot(left, right, dims=ROWS_COLS):
    return lax.dot_general(left, right, dims, preferred_element_type=WIDE)


def exact_dot(left, right, dims=ROWS_COLS):
    return lax.dot_general(
        left, right, dims, preferred_element_type=WIDE, precision=lax.Precision.HIGHEST
    )


def vmem():
    return pl.BlockSpec(memory_space=pltpu.VMEM)


def smem():
    return pl.BlockSpec(memory_space=pltpu.SMEM)


def whole(shape):
    return pl.BlockSpec(shape, lambda *unused: (0,) * len(shape))


def behind(kernel, count):
    def ordered(*refs):
        return kernel(*refs[count:])

    return ordered


def anywhere(count):
    return [pl.BlockSpec(memory_space=pl.ANY)] * count


def column_sum(values):
    return jnp.sum(values, axis=0, keepdims=True)


def head_masks(rows, lanes, heads):
    lane = lax.broadcasted_iota(jnp.int32, (rows, lanes), 1)
    return [lane // HD == h for h in range(heads)]


def square_norm(values, masks):
    squared = values.astype(WIDE)
    squared = squared * squared
    return [
        jnp.max(jnp.sum(jnp.where(mask, squared, 0.0), axis=1, keepdims=True)) for mask in masks
    ]


def split_sources(refs, parts, own):
    trios, refs = refs[:parts], refs[parts:]
    if own:
        return trios, trios, refs
    return trios, refs[:parts], refs[parts:]


def joined(refs, slot, place):
    return jnp.concatenate([ref[slot, place] for ref in refs], axis=0)


def forward_kernel(order, flag_in, *refs, parts, own, first, last, heads):
    trios, pairs, refs = split_sources(refs, parts, own)
    frames, unused, few, lanes = trios[0].shape
    tokens = few * parts
    if not first:
        num_in, sum_in, top_in = refs[:3]
        refs = refs[3:]
    if last:
        attn_out, log_out = refs[:2]
        refs = refs[2:]
    else:
        flag_out, num_out, sum_out, top_out = refs[:4]
        refs = refs[4:]
    queries, keys, values, accs = refs
    group = accs.shape[1] // tokens
    masks = head_masks(tokens, lanes, heads)
    one = jnp.ones((tokens, lanes), LOW)
    zero = jnp.zeros((tokens, lanes), LOW)
    width = 2 * HD
    bound = jnp.float32(0.0)
    q_top = [jnp.float32(0.0)] * heads
    k_top = [jnp.float32(0.0)] * heads
    for t in range(frames):
        slot = order[t]
        k = joined(pairs, slot, 0)
        v = joined(pairs, slot, 1)
        queries[t] = joined(trios, slot, 2)
        q_top = [jnp.maximum(a, b) for a, b in zip(q_top, square_norm(queries[t], masks))]
        k_top = [jnp.maximum(a, b) for a, b in zip(k_top, square_norm(k, masks))]
        for h in range(heads):
            keys[h, t] = jnp.where(masks[h], k, zero)
            if heads == 2:
                values[h, t] = jnp.where(masks[h], v, one)
            else:
                values[h, t] = jnp.concatenate([v, one], axis=1)
    for a, b in zip(q_top, k_top):
        bound = jnp.maximum(bound, a * b)
    fast = bound * (SCALE2 * SCALE2) <= SAFE_LOG2 * SAFE_LOG2
    if not first:
        fast = jnp.logical_and(fast, flag_in[0] == 1)
    if not last:
        flag_out[0] = jnp.where(fast, 1, 0).astype(jnp.int32)
    low_lane = lax.broadcasted_iota(jnp.int32, (tokens, lanes), 1) < HD
    pick = lax.broadcasted_iota(jnp.int32, (8, lanes), 1) == HD * lax.broadcasted_iota(
        jnp.int32, (8, lanes), 0
    )
    pick = jnp.where(pick, 1.0, 0.0).astype(WIDE)

    def split(num, total):
        if heads == 2:
            turned = pltpu.roll(total, HD, 1)
            return [jnp.where(low_lane, num, turned), jnp.where(low_lane, turned, num)]
        return [jnp.concatenate([num, total], axis=1)]

    def join(accs):
        if heads == 2:
            num = jnp.where(low_lane, accs[0], accs[1])
            total = jnp.where(low_lane, accs[1], accs[0])
            return num, pltpu.roll(total, HD, 1)
        return accs[0][:, :HD], accs[0][:, HD:]

    def start(slot):
        if first:
            return [jnp.zeros((tokens, width), WIDE) for _ in range(heads)]
        return split(num_in[slot], sum_in[slot])

    def store(slot, accs, top):
        num, total = join(accs)
        if last:
            attn_out[slot] = (num / total).astype(LOW)
            logs = jnp.log2(total)
            if top is not None:
                logs = logs + top
            log_out[slot] = exact_dot(pick, logs, ROWS_ROWS)
        else:
            num_out[slot] = num
            sum_out[slot] = total
            top_out[slot] = jnp.zeros((tokens, lanes), WIDE) if top is None else top

    @pl.when(fast)
    def _():
        def outer(g, unused):
            base = g * group
            q = queries[pl.ds(base, group)].reshape(group * tokens, lanes)
            for i in range(group):
                for h, value in enumerate(start(order[base + i])):
                    accs[h, i * tokens : (i + 1) * tokens] = value

            def tile(j, skip):
                rows = slice(skip * tokens, group * tokens)
                for h in range(heads):
                    s = dot(q[rows], keys[h, j], ROWS_ROWS)
                    p = jnp.exp2(s * SCALE2).astype(LOW)
                    accs[h, rows] += dot(p, values[h, j])

            def inner(j, unused):
                tile(j, 0)
                return unused

            lax.fori_loop(0, base + 1, inner, 0)
            for skip in range(1, group):
                tile(base + skip, skip)
            for i in range(group):
                rows = slice(i * tokens, (i + 1) * tokens)
                store(order[base + i], [accs[h, rows] for h in range(heads)], None)
            return unused

        lax.fori_loop(0, frames // group, outer, 0)

    @pl.when(jnp.logical_not(fast))
    def _():
        def outer(t, unused):
            slot = order[t]
            q = queries[t]

            def inner(j, state):
                sums, tops = state
                new_accs, new_tops = [], []
                for h in range(heads):
                    s = dot(q, keys[h, j], ROWS_ROWS) * SCALE2
                    top = jnp.maximum(tops[h], jnp.max(s, axis=1, keepdims=True))
                    p = jnp.exp2(s - top).astype(LOW)
                    keep = jnp.exp2(tops[h] - top)
                    new_accs.append(sums[h] * keep + dot(p, values[h, j]))
                    new_tops.append(top)
                return new_accs, new_tops

            if first:
                tops = [jnp.full((tokens, 1), -1e30, WIDE)] * heads
            else:
                tops = [top_in[slot][:, h * HD : h * HD + 1] for h in range(heads)]
            sums, tops = lax.fori_loop(0, t + 1, inner, (start(slot), tops))
            top = jnp.broadcast_to(tops[0], (tokens, lanes))
            if heads == 2:
                top = jnp.where(low_lane, top, jnp.broadcast_to(tops[1], (tokens, lanes)))
            store(slot, sums, top)
            return unused

        lax.fori_loop(0, frames, outer, 0)


def attention_forward(order, state, trios, pairs, last, after):
    frames, unused, few, lanes = trios[0].shape
    parts, own = len(trios), pairs is None
    tokens = few * parts
    sources = tuple(trios) + (() if own else tuple(pairs))
    heads = lanes // HD
    first = state is None
    wide = jax.ShapeDtypeStruct((frames, tokens, lanes), WIDE)
    if last:
        out_shape = [
            jax.ShapeDtypeStruct((frames, tokens, lanes), LOW),
            jax.ShapeDtypeStruct((frames, 8, tokens), WIDE),
        ]
        out_specs = [vmem()] * 2
    else:
        out_shape = [jax.ShapeDtypeStruct((1,), jnp.int32), wide, wide, wide]
        out_specs = [smem()] + [vmem()] * 3
    flag = jnp.zeros((1,), jnp.int32) if first else state[0]
    rest = () if first else tuple(state[1:])
    work = heads * frames * (frames + 1) // 2 * tokens * tokens
    return pl.pallas_call(
        behind(
            functools.partial(
                forward_kernel, parts=parts, own=own, first=first, last=last, heads=heads
            ),
            len(after),
        ),
        out_shape=out_shape,
        in_specs=anywhere(len(after)) + [smem(), smem()]
        + [vmem()] * (len(sources) + len(rest)),
        out_specs=out_specs,
        scratch_shapes=[
            pltpu.VMEM((frames, tokens, lanes), LOW),
            pltpu.VMEM((heads, frames, tokens, lanes), LOW),
            pltpu.VMEM((heads, frames, tokens, max(lanes, 2 * HD)), LOW),
            pltpu.VMEM((heads, FORWARD_GROUP * tokens, max(lanes, 2 * HD)), WIDE),
        ],
        compiler_params=pltpu.CompilerParams(vmem_limit_bytes=56 * MIB),
        cost_estimate=pl.CostEstimate(
            flops=work * 4 * HD * 8, bytes_accessed=16 * MIB, transcendentals=work
        ),
        name="attention_forward",
    )(*after, order, flag, *sources, *rest)


def backward_kernel(order, grad, out, lse, *refs, parts, sources, first, last, came, heads):
    trios, pairs, refs = refs[:parts], refs[parts : parts + sources], refs[parts + sources :]
    frames, tokens, lanes = grad.shape
    size = pairs[0].shape[2]
    few = size * sources
    if not first:
        dq_in = refs[0]
        refs = refs[1:]
    if came:
        pair_came = refs[0]
        refs = refs[1:]
    if not last:
        dq_sum, refs = refs[0], refs[1:]
    finals, refs = refs[:sources], refs[sources:]
    queries, grads, delta, logs, keys, values, key_turned, dk, dv = refs[:9]
    if last:
        dq_sum = refs[9]
    places = (parts, parts + 1) if last else (0, 1)
    group = dk.shape[0] // few
    masks = head_masks(tokens, lanes, heads)
    zero = jnp.zeros((tokens, lanes), LOW)
    lane8 = lax.broadcasted_iota(jnp.int32, (8, lanes), 1) // HD
    pick = jnp.where(lane8 == lax.broadcasted_iota(jnp.int32, (8, lanes), 0), 1.0, 0.0)
    for t in range(frames):
        slot = order[t]
        q = joined(trios, slot, 2)
        g = grad[slot]
        k = joined(pairs, slot, 0)
        for h in range(heads):
            queries[h, t] = jnp.where(masks[h], q, zero)
            grads[h, t] = jnp.where(masks[h], g, zero)
        keys[t] = k
        values[t] = joined(pairs, slot, 1)
        key_turned[t // group, :, (t % group) * few : (t % group + 1) * few] = k.T
        logs[t] = lse[slot]
        delta[t] = exact_dot(
            pick.astype(WIDE), g.astype(WIDE) * out[slot].astype(WIDE), ROWS_ROWS
        )
        dq_sum[t] = jnp.zeros((lanes, tokens), WIDE) if first else dq_in[t]
    group_masks = head_masks(group * few, lanes, heads)
    group_zero = jnp.zeros((group * few, lanes), LOW)

    def outer(index, unused):
        base = index * group
        k = keys[pl.ds(base, group)].reshape(group * few, lanes)
        v = values[pl.ds(base, group)].reshape(group * few, lanes)
        ks = [jnp.where(mask, k, group_zero) for mask in group_masks]
        vs = [jnp.where(mask, v, group_zero) for mask in group_masks]
        dk[...] = jnp.zeros(dk.shape, WIDE)
        dv[...] = jnp.zeros(dv.shape, WIDE)

        def tile(j, count):
            rows = slice(0, count * few)
            for h in range(heads):
                q = queries[h, j]
                g = grads[h, j]
                s = dot(ks[h][rows], q, ROWS_ROWS)
                p = jnp.exp2(s * SCALE2 - logs[j, h : h + 1, :])
                dp = dot(vs[h][rows], g, ROWS_ROWS)
                ds = (p * (dp - delta[j, h : h + 1, :])).astype(LOW)
                dv[rows] += dot(p.astype(LOW), g)
                dk[rows] += dot(ds, q)
                span = slice(h * HD, (h + 1) * HD)
                dq_sum[j, span, :] += dot(key_turned[index, span, rows], ds)

        def inner(j, unused):
            tile(j, group)
            return unused

        for count in range(1, group):
            tile(base + count - 1, count)
        lax.fori_loop(base + group - 1, frames, inner, 0)
        for i in range(group):
            rows = slice(i * few, (i + 1) * few)
            slot = order[base + i]
            part_k = dk[rows] * (1.0 / math.sqrt(HD))
            part_v = dv[rows]
            if came:
                part_k = part_k + pair_came[slot, 0].astype(WIDE)
                part_v = part_v + pair_came[slot, 1].astype(WIDE)
            for n, final in enumerate(finals):
                span = slice(n * size, (n + 1) * size)
                final[slot, places[0]] = part_k[span].astype(LOW)
                final[slot, places[1]] = part_v[span].astype(LOW)
        return unused

    lax.fori_loop(0, frames // group, outer, 0)
    if last:
        for t in range(frames):
            dq = (dq_sum[t].T * (1.0 / math.sqrt(HD))).astype(LOW)
            for i in range(parts):
                finals[0][order[t], i] = dq[i * size : (i + 1) * size]


def attention_backward(order, dq, came, trios, pairs, grad, out, lse, last, after):
    frames, tokens, lanes = grad.shape
    size = pairs[0].shape[2]
    few = size * len(pairs)
    parts = len(trios)
    heads = lanes // HD
    first = dq is None
    sums = (frames, lanes, tokens)
    extra = tuple(array for array in (dq, came) if array is not None)
    work = heads * frames * (frames + 1) // 2 * tokens * few
    rows = BACKWARD_GROUP * few
    scratch = [
        pltpu.VMEM((heads, frames, tokens, lanes), LOW),
        pltpu.VMEM((heads, frames, tokens, lanes), LOW),
        pltpu.VMEM((frames, 8, tokens), WIDE),
        pltpu.VMEM((frames, 8, tokens), WIDE),
        pltpu.VMEM((frames, few, lanes), LOW),
        pltpu.VMEM((frames, few, lanes), LOW),
        pltpu.VMEM((frames // BACKWARD_GROUP, lanes, rows), LOW),
        pltpu.VMEM((rows, lanes), WIDE),
        pltpu.VMEM((rows, lanes), WIDE),
    ]
    pair_shape = jax.ShapeDtypeStruct((frames, (parts if last else 0) + 2, size, lanes), LOW)
    if last:
        out_shape = [pair_shape]
        scratch.append(pltpu.VMEM(sums, WIDE))
    else:
        out_shape = [jax.ShapeDtypeStruct(sums, WIDE)] + [pair_shape] * len(pairs)
    return pl.pallas_call(
        behind(
            functools.partial(
                backward_kernel, parts=parts, sources=len(pairs), first=first, last=last,
                came=came is not None, heads=heads,
            ),
            len(after),
        ),
        out_shape=out_shape,
        in_specs=anywhere(len(after)) + [smem()] + [vmem()] * (3 + parts + len(pairs) + len(extra)),
        out_specs=[vmem()] * len(out_shape),
        scratch_shapes=scratch,
        compiler_params=pltpu.CompilerParams(vmem_limit_bytes=56 * MIB),
        cost_estimate=pl.CostEstimate(
            flops=work * 10 * HD * 5, bytes_accessed=16 * MIB, transcendentals=work
        ),
        name="attention_backward",
    )(*after, order, grad, out, lse, *trios, *pairs, *extra)


def normalize(values):
    centered = values - jnp.mean(values, axis=-1, keepdims=True)
    inverse = lax.rsqrt(jnp.mean(centered * centered, axis=-1, keepdims=True) + norm_eps)
    return (centered * inverse, inverse)


def norm_backward(grad_normed, normed, inverse):
    mean_grad = jnp.mean(grad_normed, axis=-1, keepdims=True)
    mean_prod = jnp.mean(grad_normed * normed, axis=-1, keepdims=True)
    return inverse * (grad_normed - mean_grad - normed * mean_prod)


def part(mod, index):
    return mod[0:1, index * D : (index + 1) * D]


def swap_halves(values):
    lanes = values.shape[1]
    lane = lax.broadcasted_iota(jnp.int32, values.shape, 1) % HD
    eight, twelve = HD // 8, 3 * HD // 16
    quarter, last = HD // 4, HD // 4 + 2 * twelve

    def ahead(step):
        return pltpu.roll(values, lanes - step, 1)

    def behind(step):
        return pltpu.roll(values, step, 1)

    first_half = ((lane >= quarter) & (lane < quarter + twelve)) | (
        (lane >= last) & (lane < last + twelve)
    )
    short = jnp.where(lane < eight, ahead(eight), behind(eight))
    long = jnp.where(first_half, ahead(twelve), behind(twelve))
    return jnp.where(lane < quarter, short, long)


def turned(values, cosine, sine):
    wide = cosine.shape[1]
    pieces = []
    for at in range(0, values.shape[1], wide):
        block = values[:, at : at + wide]
        pieces.append(block * cosine + swap_halves(block) * sine)
    return pieces[0] if len(pieces) == 1 else jnp.concatenate(pieces, axis=1)


def input_kernel(tokens, mod, w_query, w_key, w_value, cosine, sine, hidden, trio):
    @pl.when(pl.program_id(0) == 0)
    def _():
        normed, unused = normalize(tokens[...].astype(WIDE))
        hidden[...] = (normed * (1.0 + part(mod, SCALE_ONE)) + part(mod, SHIFT_ONE)).astype(LOW)

    groups, unused, unused, lanes = trio.shape
    h = hidden[...]
    cos, sin = cosine[...], sine[...]
    k = turned(dot(h, w_key[...]), cos, sin).astype(LOW)
    v = dot(h, w_value[...]).astype(LOW)
    q = turned(dot(h, w_query[...]), cos, sin).astype(LOW)
    for g in range(groups):
        span = slice(g * lanes, (g + 1) * lanes)
        trio[g, 0] = k[:, span]
        trio[g, 1] = v[:, span]
        trio[g, 2] = q[:, span]


def input_projections(tokens, mod, w_query, w_key, w_value, cosine, sine, frames):
    count = tokens.shape[0]
    lanes = D // frames
    wide = 256
    groups = wide // lanes
    weight = pl.BlockSpec((D, wide), lambda c: (0, c))
    trio = pl.BlockSpec((groups, 3, count, lanes), lambda c: (c, 0, 0, 0))
    return pl.pallas_call(
        input_kernel,
        grid=(D // wide,),
        out_shape=[
            jax.ShapeDtypeStruct((count, D), LOW),
            jax.ShapeDtypeStruct((frames, 3, count, lanes), LOW),
        ],
        in_specs=[whole((count, D)), whole((1, 6 * D)), weight, weight, weight]
        + [whole(cosine.shape)] * 2,
        out_specs=[whole((count, D)), trio],
        compiler_params=pltpu.CompilerParams(vmem_limit_bytes=48 * MIB),
        cost_estimate=pl.CostEstimate(
            flops=6 * count * D * D, bytes_accessed=12 * MIB, transcendentals=0
        ),
        name="input_projections",
    )(tokens, mod, w_query, w_key, w_value, cosine, sine)


def pull_kernel(cotangent, mod, w_down, pulled, scaled_turned, scaled):
    @pl.when(pl.program_id(0) == 0)
    def _():
        scaled[...] = (part(mod, GATE_TWO) * cotangent[...].astype(WIDE)).astype(LOW)
        scaled_turned[...] = scaled[...].T

    pulled[...] = dot(scaled[...], w_down[...], ROWS_ROWS).astype(LOW)


def pull_down(cotangent, mod, w_down):
    count = cotangent.shape[0]
    wide = 512
    return pl.pallas_call(
        pull_kernel,
        grid=(FF // wide,),
        out_shape=[
            jax.ShapeDtypeStruct((count, FF), LOW), jax.ShapeDtypeStruct((D, count), LOW)
        ],
        in_specs=[
            whole((count, D)), whole((1, 6 * D)), pl.BlockSpec((wide, D), lambda c: (c, 0))
        ],
        out_specs=[pl.BlockSpec((count, wide), lambda c: (0, c)), whole((D, count))],
        scratch_shapes=[pltpu.VMEM((count, D), LOW)],
        compiler_params=pltpu.CompilerParams(vmem_limit_bytes=32 * MIB),
        cost_estimate=pl.CostEstimate(
            flops=2 * count * D * FF, bytes_accessed=14 * MIB, transcendentals=0
        ),
        name="pull_down",
    )(cotangent, mod, w_down)


def middle_kernel(
    attn, tokens, cotangent, mod, w_proj, w_up, pulled,
    middle, hidden, active, grad_up_in, grad_middle, grad_branch, grad_attn,
    grad_gate, grad_shift, grad_scale, branch, normed, inverse, total
):
    step = pl.program_id(0)
    frames, count, lanes = attn.shape

    @pl.when(step == 0)
    def _():
        for f in range(frames):
            hidden[:, f * lanes : (f + 1) * lanes] = attn[f]
        product = dot(hidden[...], w_proj[...])
        branch[...] = product
        mid = tokens[...].astype(WIDE) + part(mod, GATE_ONE) * product
        middle[...] = mid
        n, inv = normalize(mid)
        normed[...] = n
        inverse[...] = inv
        hidden[...] = (n * (1.0 + part(mod, SCALE_TWO)) + part(mod, SHIFT_TWO)).astype(LOW)
        total[...] = jnp.zeros(total.shape, WIDE)

    weight = w_up[...]
    u = dot(hidden[...], weight)
    rate = math.sqrt(2.0 / math.pi)
    square = u * u
    bend = jnp.tanh(rate * (u + 0.044715 * (u * square)))
    half = 0.5 * (1.0 + bend)
    active[...] = (u * half).astype(LOW)
    slope = half + (0.5 * rate) * u * (1.0 - bend * bend) * (1.0 + (3 * 0.044715) * square)
    du = (pulled[...].astype(WIDE) * slope).astype(LOW)
    grad_up_in[...] = du
    total[...] += dot(du, weight, ROWS_ROWS)

    @pl.when(step == pl.num_programs(0) - 1)
    def _():
        dh = total[...]
        n = normed[...]
        grad_scale[...] = column_sum(dh * n)
        grad_shift[...] = column_sum(dh)
        dx = cotangent[...].astype(WIDE) + norm_backward(
            dh * (1.0 + part(mod, SCALE_TWO)), n, inverse[...]
        )
        grad_middle[...] = dx
        grad_gate[...] = column_sum(dx * branch[...])
        dy = (part(mod, GATE_ONE) * dx).astype(LOW)
        grad_branch[...] = dy
        back = dot(dy, w_proj[...], ROWS_ROWS).astype(LOW)
        for f in range(frames):
            grad_attn[f] = back[:, f * lanes : (f + 1) * lanes]


def middle_block(attn, tokens, cotangent, mod, w_proj, w_up, pulled):
    frames, count, lanes = attn.shape
    wide = 512
    flat = whole((count, D))
    row = whole((1, D))
    columns = pl.BlockSpec((count, wide), lambda c: (0, c))
    heads = whole(attn.shape)

    def of(shape, kind):
        return jax.ShapeDtypeStruct(shape, kind)

    return pl.pallas_call(
        middle_kernel,
        grid=(FF // wide,),
        out_shape=[
            of((count, D), WIDE), of((count, D), LOW), of((count, FF), LOW), of((count, FF), LOW),
            of((count, D), WIDE), of((count, D), LOW), of(attn.shape, LOW),
            of((1, D), WIDE), of((1, D), WIDE), of((1, D), WIDE),
        ],
        in_specs=[
            heads, flat, flat, whole((1, 6 * D)), whole((D, D)),
            pl.BlockSpec((D, wide), lambda c: (0, c)), columns,
        ],
        out_specs=[flat, flat, columns, columns, flat, flat, heads, row, row, row],
        scratch_shapes=[
            pltpu.VMEM((count, D), WIDE), pltpu.VMEM((count, D), WIDE),
            pltpu.VMEM((count, 1), WIDE), pltpu.VMEM((count, D), WIDE),
        ],
        compiler_params=pltpu.CompilerParams(vmem_limit_bytes=56 * MIB),
        cost_estimate=pl.CostEstimate(
            flops=2 * count * D * (2 * FF + 2 * D), bytes_accessed=30 * MIB,
            transcendentals=count * FF,
        ),
        name="middle_block",
    )(attn, tokens, cotangent, mod, w_proj, w_up, pulled)


def weights_kernel(
    slot, active, grad_up_in, hidden, scaled_turned, attn, grad_branch, *refs, keep
):
    step = pl.program_id(0)
    frames, count, lanes = attn.shape
    half = frames // 2
    wide = D // frames
    if keep:
        activity, middle, cotangent, mod, w_down = refs[:5]
        out, grad_gate, down_out, up_out, hidden_turned, attn_turned, flat, total = refs[5:]
    else:
        down_out, up_out, hidden_turned, attn_turned, flat = refs
    chunks, narrow = down_out.shape[1], down_out.shape[3]

    @pl.when(step == 0)
    def _():
        for f in range(frames):
            flat[:, f * lanes : (f + 1) * lanes] = attn[f]
        for f in range(frames):
            place = lax.bitwise_xor(f, slot[0])

            @pl.when(place % 2 == (0 if keep else 1))
            def _():
                span = slice(f * wide, (f + 1) * wide)
                hidden_turned[place // 2] = hidden[:, span].T
                attn_turned[place // 2] = flat[:, span].T

        if keep:
            total[...] = jnp.zeros(total.shape, WIDE)

    @pl.when(step < half)
    def _():
        if keep:
            total[...] += dot(activity[...], w_down[...])
        down = dot(scaled_turned[...], active[...]).astype(LOW)
        for r in range(chunks):
            down_out[0, r] = down[:, r * narrow : (r + 1) * narrow]
        up = dot(hidden_turned[...].reshape(D // 2, count), grad_up_in[...]).astype(LOW)
        up_out[...] = up.reshape(half, wide, up.shape[1])

    @pl.when(step >= half)
    def _():
        proj = dot(attn_turned[...].reshape(D // 2, count), grad_branch[...]).astype(LOW)
        up_out[...] = proj.reshape(half, wide, proj.shape[1])

    if keep:
        @pl.when(step == half - 1)
        def _():
            z = total[...]
            out[...] = (middle[...] + part(mod, GATE_TWO) * z).astype(LOW)
            grad_gate[...] = column_sum(cotangent[...].astype(WIDE) * z)


def weight_gradients(
    slot, active, grad_up_in, hidden, scaled_turned, attn, grad_branch, rows, finish
):
    frames, count, lanes = attn.shape
    keep = finish is not None
    half = frames // 2
    narrow = FF // frames
    wide = FF // half
    extra = D // wide

    def down_block(i, slot):
        place = 2 * jnp.minimum(i, half - 1) + (0 if keep else 1)
        return lax.bitwise_xor(place, slot[0])

    def up_block(i, slot):
        return jnp.minimum(i, half - 1)

    flat = whole((count, D))
    down = (1, rows, D, narrow // rows)
    in_specs = [
        pl.BlockSpec((count, narrow), lambda i, slot: (0, down_block(i, slot))),
        pl.BlockSpec((count, wide), lambda i, slot: (0, up_block(i, slot))),
        flat, whole((D, count)), whole(attn.shape),
        pl.BlockSpec((count, wide), lambda i, slot: (0, jnp.maximum(i - half, 0))),
    ]
    out_specs = [
        pl.BlockSpec(down, lambda i, slot: (jnp.minimum(i, half - 1), 0, 0, 0)),
        pl.BlockSpec((half, D // frames, wide), lambda i, slot: (0, 0, i)),
    ]
    out_shape = [
        jax.ShapeDtypeStruct((half, rows, D, narrow // rows), LOW),
        jax.ShapeDtypeStruct((half, D // frames, FF + D), LOW),
    ]
    scratch = [
        pltpu.VMEM((half, D // frames, count), LOW), pltpu.VMEM((half, D // frames, count), LOW),
        pltpu.VMEM((count, D), LOW),
    ]
    args = (slot, active, grad_up_in, hidden, scaled_turned, attn, grad_branch)
    if keep:
        args += (active,) + tuple(finish)
        in_specs += [
            pl.BlockSpec((count, wide), lambda i, slot: (0, up_block(i, slot))),
            flat, flat, whole((1, 6 * D)),
            pl.BlockSpec((wide, D), lambda i, slot: (up_block(i, slot), 0)),
        ]
        out_specs = [flat, whole((1, D))] + out_specs
        out_shape = [
            jax.ShapeDtypeStruct((count, D), LOW), jax.ShapeDtypeStruct((1, D), WIDE)
        ] + out_shape
        scratch.append(pltpu.VMEM((count, D), WIDE))
    return pl.pallas_call(
        functools.partial(weights_kernel, keep=keep),
        grid_spec=pltpu.PrefetchScalarGridSpec(
            num_scalar_prefetch=1, grid=(half + extra,),
            in_specs=in_specs, out_specs=out_specs, scratch_shapes=scratch,
        ),
        out_shape=out_shape,
        compiler_params=pltpu.CompilerParams(vmem_limit_bytes=56 * MIB),
        cost_estimate=pl.CostEstimate(
            flops=count * D * (2 * FF + D + (2 * FF if keep else 0)), bytes_accessed=24 * MIB,
            transcendentals=0,
        ),
        name="weight_gradients",
    )(*args)


def turn_kernel(*refs):
    *parts, target = refs
    target[...] = jnp.concatenate([part[...] for part in parts], axis=0).T


def turn_hidden(parts):
    count = sum(part.shape[0] for part in parts)
    return pl.pallas_call(
        turn_kernel,
        out_shape=jax.ShapeDtypeStruct((D, count), LOW),
        in_specs=[vmem()] * len(parts),
        out_specs=vmem(),
        compiler_params=pltpu.CompilerParams(vmem_limit_bytes=32 * MIB),
        cost_estimate=pl.CostEstimate(flops=0, bytes_accessed=2 * MIB, transcendentals=0),
        name="turn_hidden",
    )(*parts)


def three_gradients(early, late, at):
    q = jnp.concatenate([late[at, 0], late[at, 1]], axis=0)
    k = jnp.concatenate([early[at, 0], late[at, 2]], axis=0)
    v = jnp.concatenate([early[at, 1], late[at, 3]], axis=0)
    return q, k, v


def head_kernel(early, grads, hidden, cosine, sine, time_cosine, time_sine, product, total):
    step = pl.program_id(0)

    @pl.when(step == 0)
    def _():
        total[...] = jnp.zeros(total.shape, WIDE)

    cos = cosine[...] + time_cosine[0]
    sin = -(sine[...] + time_sine[0])
    q, k, v = three_gradients(early, grads, 0)
    block = jnp.concatenate(
        [turned(q.astype(WIDE), cos, sin).astype(LOW), turned(k.astype(WIDE), cos, sin).astype(LOW), v],
        axis=1,
    )
    total[...] += dot(hidden[0], block)

    @pl.when(step == pl.num_programs(0) - 1)
    def _():
        product[...] = total[...].astype(LOW)


def head_gradients(early, grads, hidden_all, tables, after):
    frames, unused, few, lanes = grads.shape
    count = 2 * few
    frame = pl.BlockSpec((1, 1, lanes), lambda f: (f, 0, 0))
    return pl.pallas_call(
        behind(head_kernel, len(after)),
        grid=(frames,),
        out_shape=jax.ShapeDtypeStruct((D, 3 * lanes), LOW),
        in_specs=anywhere(len(after)) + [
            pl.BlockSpec((1, 2, few, lanes), lambda f: (f, 0, 0, 0)),
            pl.BlockSpec((1, 4, few, lanes), lambda f: (f, 0, 0, 0)),
            pl.BlockSpec((1, D, count), lambda f: (f, 0, 0)),
            whole((count, lanes)), whole((count, lanes)), frame, frame,
        ],
        out_specs=whole((D, 3 * lanes)),
        scratch_shapes=[pltpu.VMEM((D, 3 * lanes), WIDE)],
        compiler_params=pltpu.CompilerParams(vmem_limit_bytes=32 * MIB),
        cost_estimate=pl.CostEstimate(
            flops=6 * frames * count * D * lanes, bytes_accessed=12 * MIB, transcendentals=0
        ),
        name="head_gradients",
    )(*after, early, grads, hidden_all, *tables)


def output_kernel(
    early, grads, w_query, w_key, w_value, cosine, sine, tokens, mod, grad_middle,
    grad_tokens, grad_shift, grad_scale, total
):
    step = pl.program_id(0)
    groups = grads.shape[0]

    @pl.when(step == 0)
    def _():
        total[...] = jnp.zeros(total.shape, WIDE)

    dh = total[...]
    blocks = [three_gradients(early, grads, g) for g in range(groups)]
    for i, weight in enumerate((w_query, w_key, w_value)):
        block = jnp.concatenate([three[i] for three in blocks], axis=1)
        if i < 2:
            block = turned(block.astype(WIDE), cosine[...], -sine[...]).astype(LOW)
        dh = dh + dot(block, weight[...], ROWS_ROWS)
    total[...] = dh

    @pl.when(step == pl.num_programs(0) - 1)
    def _():
        dh = total[...]
        n, inverse = normalize(tokens[...].astype(WIDE))
        grad_scale[...] = column_sum(dh * n)
        grad_shift[...] = column_sum(dh)
        grad_tokens[...] = (
            grad_middle[...] + norm_backward(dh * (1.0 + part(mod, SCALE_ONE)), n, inverse)
        ).astype(LOW)


def input_gradients(early, grads, w_query, w_key, w_value, cosine, sine, tokens, mod, grad_middle, after):
    frames, unused, few, lanes = grads.shape
    count = 2 * few
    wide = 256
    groups = wide // lanes
    flat = whole((count, D))
    row = whole((1, D))
    weight = pl.BlockSpec((D, wide), lambda c: (0, c))
    rows = jax.ShapeDtypeStruct((1, D), WIDE)
    return pl.pallas_call(
        behind(output_kernel, len(after)),
        grid=(D // wide,),
        out_shape=[jax.ShapeDtypeStruct((count, D), LOW), rows, rows],
        in_specs=anywhere(len(after)) + [
            pl.BlockSpec((groups, 2, few, lanes), lambda c: (c, 0, 0, 0)),
            pl.BlockSpec((groups, 4, few, lanes), lambda c: (c, 0, 0, 0)),
            weight, weight, weight, whole(cosine.shape), whole(sine.shape),
            flat, whole((1, 6 * D)), flat,
        ],
        out_specs=[flat, row, row],
        scratch_shapes=[pltpu.VMEM((count, D), WIDE)],
        compiler_params=pltpu.CompilerParams(vmem_limit_bytes=48 * MIB),
        cost_estimate=pl.CostEstimate(
            flops=6 * count * D * D, bytes_accessed=14 * MIB, transcendentals=0
        ),
        name="input_gradients",
    )(*after, early, grads, w_query, w_key, w_value, cosine, sine, tokens, mod, grad_middle)


def halves_kernel(mine, keep_give, came_give, keep_hold, came_hold, give, hold):
    give[0] = (keep_give[0, 0].astype(WIDE) + came_give[0, 0].astype(WIDE)).astype(LOW)
    hold[0] = (keep_hold[0, 0].astype(WIDE) + came_hold[0, 0].astype(WIDE)).astype(LOW)


def add_halves(keep, came, axis, mine, after):
    shape = keep.shape
    lead, trail = math.prod(shape[:axis]), math.prod(shape[axis + 1 : -2])
    rest = shape[:axis] + shape[axis + 1 :]
    many = 2 if trail % 2 == 0 else 1
    block = (1, 1, many) + shape[-2:]
    view = (lead, 2, trail) + shape[-2:]

    def part_of(other):
        def index(a, b, mine, *unused):
            return (a, 1 - mine[0] if other else mine[0], b, 0, 0)

        return pl.BlockSpec(block, index)

    out = pl.BlockSpec((1, many) + shape[-2:], lambda a, b, *unused: (a, b, 0, 0))
    out_shape = jax.ShapeDtypeStruct((lead, trail) + shape[-2:], LOW)

    def ordered(mine, *refs):
        halves_kernel(mine, *refs[len(after) :])

    keep, came = keep.reshape(view), came.reshape(view)
    give, hold = pl.pallas_call(
        ordered,
        grid_spec=pltpu.PrefetchScalarGridSpec(
            num_scalar_prefetch=1,
            grid=(lead, trail // many),
            in_specs=anywhere(len(after)) + [part_of(True)] * 2 + [part_of(False)] * 2,
            out_specs=[out, out],
        ),
        out_shape=[out_shape, out_shape],
        cost_estimate=pl.CostEstimate(
            flops=keep.size, bytes_accessed=6 * keep.size, transcendentals=0
        ),
        name="add_halves",
    )(mine, *after, keep, came, keep, came)
    return give.reshape(rest), hold.reshape(rest)


def total_kernel(keep, came, total):
    total[...] = keep[...].astype(WIDE) + came[...].astype(WIDE)


def add_last(keep, came, after):
    return pl.pallas_call(
        behind(total_kernel, len(after)),
        out_shape=jax.ShapeDtypeStruct(keep.shape, WIDE),
        in_specs=anywhere(len(after)) + [vmem()] * 2,
        out_specs=vmem(),
        name="add_last",
    )(*after, keep, came)


def same_kernel(*unused):
    pass


def order_after(array, after):
    return pl.pallas_call(
        same_kernel,
        out_shape=jax.ShapeDtypeStruct(array.shape, array.dtype),
        in_specs=anywhere(len(after) + 1),
        out_specs=anywhere(1)[0],
        input_output_aliases={len(after): 0},
        name="order_after",
    )(*after, array)


def pack_kernel(*refs):
    *vectors, codes, packed = refs
    at = 0
    for vector in vectors:
        packed[:, at : at + D] = jnp.broadcast_to(vector[...], (packed.shape[0], D)).astype(LOW)
        at += D
    packed[:, at:] = codes[...].astype(LOW)


def pack(vectors, codes, after):
    return pl.pallas_call(
        behind(pack_kernel, len(after)),
        out_shape=jax.ShapeDtypeStruct((codes.shape[0], len(vectors) * D + codes.shape[1]), LOW),
        in_specs=anywhere(len(after)) + [vmem()] * (len(vectors) + 1),
        out_specs=vmem(),
        name="pack",
    )(*after, *vectors, codes)


def rotary_rates(lanes):
    rates, parts, signs = [], [], []
    for index, size in enumerate((HD // 4, 3 * HD // 8, 3 * HD // 8)):
        half = size // 2
        rate = 10000.0 ** (-np.arange(half, dtype=np.float32) / np.float32(half))
        rates += [rate, rate]
        parts += [np.full(size, index)]
        signs += [-np.ones(half), np.ones(half)]
    rows = [np.concatenate(rows).astype(np.float32) for rows in (rates, parts, signs)]
    return np.tile(np.stack(rows), (1, lanes // HD))


def tables_kernel(places, times, rates, place_cosine, place_sine, time_cosine, time_sine, cosine, sine, *, local):
    count, lanes = cosine.shape
    frames = time_cosine.shape[0]
    rate, parts, sign = rates[0:1], rates[1:2], rates[2:3]
    token = lax.broadcasted_iota(jnp.int32, (count, lanes), 0)
    few = local * PC
    row = jnp.where(token < few, places[0], places[1] - local) + token // PC
    spot = jnp.where(parts == 1.0, row, token % PC).astype(WIDE)
    timed = parts == 0.0
    cos = jnp.where(timed, 0.0, jnp.cos(spot * rate))
    sin = jnp.where(timed, 0.0, jnp.sin(spot * rate) * sign)
    place_cosine[...] = cos
    place_sine[...] = sin
    for f in range(frames):
        angle = times[f].astype(WIDE) * rate
        time_cosine[f] = jnp.where(timed, jnp.cos(angle), 0.0)
        time_sine[f] = jnp.where(timed, jnp.sin(angle) * sign, 0.0)
    cosine[...] = cos + time_cosine[places[2]]
    sine[...] = sin + time_sine[places[2]]


def rotary_tables(places, times, count, local, lanes):
    flat = jax.ShapeDtypeStruct((count, lanes), WIDE)
    timed = jax.ShapeDtypeStruct((times.shape[0], 1, lanes), WIDE)
    return pl.pallas_call(
        functools.partial(tables_kernel, local=local),
        out_shape=[flat, flat, timed, timed, flat, flat],
        in_specs=[smem(), smem(), vmem()],
        out_specs=[vmem()] * 6,
        name="rotary_tables",
    )(places, times, jnp.asarray(rotary_rates(lanes)))


def columns_kernel(product, *totals):
    frames, rows, unused, width = product.shape
    lanes = width // 3
    for f in range(frames):
        total = jnp.sum(product[f].astype(WIDE), axis=0)
        for i, target in enumerate(totals):
            target[:, f * lanes : (f + 1) * lanes] = total[:, i * lanes : (i + 1) * lanes]


def sum_columns(product):
    shape = jax.ShapeDtypeStruct((product.shape[2], D), WIDE)
    return pl.pallas_call(
        columns_kernel,
        out_shape=[shape] * 3,
        in_specs=[vmem()],
        out_specs=[vmem()] * 3,
        name="sum_columns",
    )(product)


def mod_kernel(early, late, out):
    kept = late.shape[1] * late.shape[2]
    vectors = 6 * D - kept
    first, second = early[...].astype(WIDE), late[...].astype(WIDE)
    codes = first[:, vectors:]
    by_rows = (((0,), (0,)), ((), ()))
    out[:, kept:] = exact_dot(codes, first[:, :vectors], by_rows)
    wide = late.shape[2]
    for c in range(late.shape[1]):
        out[:, c * wide : (c + 1) * wide] = exact_dot(codes, second[:, c, :], by_rows)


def mod_gradient(early, late):
    kept = late.shape[1] * late.shape[2]
    part_rows = early.shape[1] - (6 * D - kept)
    return pl.pallas_call(
        mod_kernel,
        out_shape=jax.ShapeDtypeStruct((part_rows, 6 * D), WIDE),
        in_specs=[vmem()] * 2,
        out_specs=vmem(),
        name="mod_gradient",
    )(early, late)


def sinusoid(levels):
    half_size = D // 2
    freq_table = 10000.0 ** (-jnp.arange(half_size, dtype=WIDE) / half_size)
    angle_table = levels.astype(WIDE)[..., None] * freq_table
    return jnp.concatenate([jnp.cos(angle_table), jnp.sin(angle_table)], axis=-1)


def shards(
    block_in, block_map, noise_level, w_query, w_key, w_value, w_proj, w_up, w_down, w_mod, cotangent
):
    frames = lax.axis_size("frames")
    sides = lax.axis_size("side")
    row_total = lax.axis_size("half") * sides
    frame_slot = lax.axis_index("frames")
    half = lax.axis_index("half")
    side = lax.axis_index("side")
    across = ("half", "side")
    everyone = ("frames",) + across
    devices = frames * row_total
    clips = block_in.shape[1]
    local_rows = block_in.shape[2]
    lanes = D // frames
    order = jnp.argsort(block_map).astype(jnp.int32)
    slot = frame_slot.astype(jnp.int32).reshape(1)

    def clip_tokens(tokens, clip):
        return lax.dynamic_index_in_dim(tokens[0], clip, 0, keepdims=False).reshape(-1, D)

    def other_half(array):
        return lax.ppermute(array, "half", [(0, 1), (1, 0)])

    def return_clip(own, came, kind):
        first = jnp.where(half == 0, own, came).astype(kind)
        second = jnp.where(half == 0, came, own).astype(kind)
        return jnp.stack([first, second]).reshape(1, clips, local_rows, PC, D)

    def swap_groups(grouped):
        return lax.all_to_all(grouped, "frames", split_axis=0, concat_axis=0, tiled=True)

    def pass_on(array, step):
        return lax.ppermute(array, "side", [(i, (i + step) % sides) for i in range(sides)])

    def flip(array, bit):
        return lax.ppermute(array, "frames", [(i, i ^ (1 << bit)) for i in range(frames)])

    def add(left, right):
        return (left.astype(WIDE) + right.astype(WIDE)).astype(LOW)

    class Reduction:
        def __init__(self, send, bits):
            self.came = flip(send, 0)
            self.bits = list(bits)
            self.left = sorted(bits, reverse=True)
            self.row_bits = [("side", bit) for bit in range(sides.bit_length() - 1)] + [("half", 0)]
            self.row_left = [("half", 0)] + self.row_bits[:-1][::-1]
            self.going = None

        def start(self, keep):
            rest = (row_total, -1) + keep.shape[-1:]
            self.shape = (2,) * (len(self.left) + len(self.row_left))
            self.keep = keep.reshape(self.shape + rest[1:])

        def advance(self, after=()):
            came = self.came.reshape(self.keep.shape)
            if self.bits:
                bit = self.bits.pop(0)
                axis = self.left.index(bit)
                self.left.remove(bit)
                name, mine = "frames", 0
            else:
                name, bit = self.row_bits.pop(0)
                axis = self.row_left.index((name, bit))
                self.row_left.remove((name, bit))
                mine = (lax.axis_index(name) >> bit) & 1

            mine = jnp.asarray(mine, jnp.int32).reshape(1)
            self.going, self.keep = add_halves(self.keep, came, axis, mine, after)
            size = lax.axis_size(name)
            self.came = lax.ppermute(self.going, name, [(i, i ^ (1 << bit)) for i in range(size)])

        def finish(self, after):
            while self.bits or self.row_bits:
                self.advance(after)
            return add_last(self.keep, self.came, after)

    high_bits = list(range(1, frames.bit_length() - 1))

    source_own = clip_tokens(block_in, half)
    source_came = other_half(clip_tokens(block_in, 1 - half))
    source = jnp.concatenate([source_own, source_came])
    half_count = source_own.shape[0]

    level = jnp.where(half == 0, noise_level[:, 0], noise_level[:, -1])
    embed = jax.nn.silu(sinusoid(level)).astype(LOW)
    mod = jnp.dot(embed, w_mod, preferred_element_type=WIDE)

    places = jnp.stack(
        [(half * sides + side) * local_rows, ((1 - half) * sides + side) * local_rows, frame_slot]
    ).astype(jnp.int32)
    tables = rotary_tables(places, block_map, 2 * half_count, local_rows, max(lanes, HD))
    cosine, sine = tables[4:]
    tables = tables[:4]

    hidden, trios = [], []
    for at, tokens in ((0, source_own), (half_count, source_came)):
        rows = slice(at, at + half_count)
        h, trio = input_projections(
            tokens, mod, w_query, w_key, w_value, cosine[rows], sine[rows], frames
        )
        hidden.append(h)
        trios.append(swap_groups(order_after(trio, (source_came,)) if at == 0 else trio))
    hidden_all = lax.all_gather(turn_hidden(hidden), "frames", axis=0)
    pairs = [None] + [
        [pass_on(trio[:, :2], step) for trio in trios] for step in range(1, sides)
    ]
    state = None
    passed = tuple(trios) if sides == 1 else tuple(pairs[-1])
    grad_came = other_half(order_after(clip_tokens(cotangent, 1 - half), passed))
    grad_result = jnp.concatenate([clip_tokens(cotangent, half), grad_came])
    pulled, scaled_turned = pull_down(grad_result, mod, w_down)
    for step in range(sides):
        state = attention_forward(order, state, trios, pairs[step], step == sides - 1, ())
    attn_heads, log_total = state
    attn = swap_groups(attn_heads)

    (
        middle, hidden_two, active, grad_up_in, grad_middle, grad_branch, grad_attn,
        grad_gate_one, grad_shift_two, grad_scale_two,
    ) = middle_block(attn, source, grad_result, mod, w_proj, w_up, pulled)
    grad_attn = swap_groups(grad_attn)
    inputs = (slot, active, grad_up_in, hidden_two, scaled_turned, attn, grad_branch, row_total)
    down_send, up_send = weight_gradients(*inputs, None)
    down = Reduction(down_send, high_bits)
    up = Reduction(up_send, high_bits[::-1])
    result, grad_gate_two, down_keep, up_keep = weight_gradients(
        *inputs, (middle, grad_result, mod, w_down)
    )
    down.start(down_keep)
    up.start(up_keep)

    def spread(vectors, after):
        packed = pack(vectors, codes, after)
        return lax.all_to_all(packed, everyone, split_axis=0, concat_axis=0, tiled=True)

    codes = embed.astype(WIDE).reshape(devices, D // devices)
    dq = None
    arrived = [None, None]

    def backward(dq, pairs, came, last, after):
        return attention_backward(
            order, dq, came, trios, pairs, grad_attn, attn_heads, log_total, last, after
        )

    down.advance()
    up.advance()
    mod_came = spread(
        [grad_gate_one, grad_shift_two, grad_scale_two, grad_gate_two],
        (grad_attn, down.going, up.going),
    )
    out_came = other_half(result[half_count:])
    after = (down.going, up.going)
    for step in range(sides - 1, 0, -1):
        dq, *partials = backward(dq, pairs[step], None, False, after)
        after = ()
        for which, partial in enumerate(partials):
            came = pass_on(partial, -step)
            arrived[which] = came if arrived[which] is None else add(arrived[which], came)
    down.advance((dq,))
    up.advance((dq,))
    dq, early = backward(dq, trios[:1], None, False, (down.going, up.going, out_came, mod_came))
    down.advance((dq,))
    up.advance((dq,))
    early = add(early, arrived[0])
    (grads,) = backward(dq, trios[1:], arrived[1], True, (down.going, up.going, early))

    early_back = swap_groups(early)
    grads = order_after(grads, (down.came, up.came, early_back))
    grads_back = swap_groups(grads)
    down.advance((grads,))
    up.advance((grads,))
    head_product = head_gradients(early, grads, hidden_all, tables, (down.going, up.going))
    ordered = order_after(head_product, (grads_back, down.came, up.came))
    product = lax.all_to_all(
        ordered.reshape(devices, D // devices, 3 * lanes),
        everyone, split_axis=0, concat_axis=0, tiled=True,
    )
    grad_source, grad_shift_one, grad_scale_one = input_gradients(
        early_back, grads_back, w_query, w_key, w_value, cosine, sine, source, mod, grad_middle,
        (head_product,),
    )
    in_came = other_half(grad_source[half_count:])
    totals = sum_columns(product.reshape(frames, row_total, D // devices, 3 * lanes))
    late = jnp.concatenate([grad_shift_one, grad_scale_one], axis=-1).reshape(1, -1, 128)
    late = jnp.broadcast_to(late.astype(LOW), (devices,) + late.shape[1:])
    late_came = lax.all_to_all(order_after(late, (product,)), everyone, split_axis=0, concat_axis=0, tiled=True)

    grad_down = down.finish((grad_source,)).reshape(D, FF // devices).T
    up_proj = up.finish((grad_source,)).reshape(D // devices, FF + D)
    grad_mod = mod_gradient(mod_came, late_came)
    return (
        return_clip(result[:half_count], out_came, LOW),
        return_clip(grad_source[:half_count], in_came, WIDE),
        *totals,
        up_proj[:, FF:], up_proj[:, :FF], grad_down, grad_mod,
    )


def solution(mesh):
    frames, rows = mesh.shape["frames"], mesh.shape["rows"]
    clips = 2
    split = Mesh(
        mesh.devices.reshape(frames, clips, rows // clips), ("frames", "half", "side")
    )
    tokens = P("frames", None, ("half", "side"), None, None)
    shared = P(("frames", "half", "side"), None)
    return jax.shard_map(
        shards,
        mesh=split,
        in_specs=(tokens, P(), P("frames", None), P(), P(), P(), P(), P(), P(), P(), tokens),
        out_specs=(tokens, tokens) + (shared,) * 7,
        check_vma=False,
    )
```
